32 devices in a mesh: dp: 8 (over y, x, core), mp: 4 (over z).
Axes of the slice: x: 2, y: 2, z: 4, core: 2. Of those that a mesh axis runs over, the one named last changes fastest.
Arguments:
- tokens: bfloat16 [8, 2048, 512], P('dp', 'mp'), may hold values from -6 to 6
- gain_mix: float32 [512], replicated, may hold values from 0.5 to 1.5
- w_mix: bfloat16 [512, 3, 1024], replicated, may hold values from -0.25 to 0.25
- bias_forget: float32 [1024], replicated, may hold values from 1 to 6
- bias_input: float32 [1024], replicated, may hold values from -7 to -1
- w_out: bfloat16 [1024, 512], replicated, may hold values from -0.5 to 0.5
- gain_mlp: float32 [512], replicated, may hold values from 0.5 to 1.5
- w_up: bfloat16 [512, 2048], P(None, 'mp'), may hold values from -0.25 to 0.25
- b_up: float32 [2048], P('mp'), may hold values from -1 to 1
- w_down: bfloat16 [2048, 512], P('mp'), may hold values from -0.125 to 0.125
- resets: int32 [8, 3], P('dp'), may hold values from 1 to 2047, as said below
- cotangent: bfloat16 [8, 2048, 512], P('dp', 'mp'), may hold values from -6 to 6
Outputs:
- mixed: bfloat16 [8, 2048, 512], P('dp', 'mp')
- grad_tokens: bfloat16 [8, 2048, 512], P('dp', 'mp')
- grad_gain_mix: float32 [512], P('mp')
- grad_w_mix: float32 [512, 3, 1024], P('mp')
- grad_bias_forget: float32 [1024], P('mp')
- grad_bias_input: float32 [1024], P('mp')
- grad_w_out: float32 [1024, 512], P('mp')
- grad_gain_mlp: float32 [512], P('mp')
- grad_w_up: float32 [512, 2048], P(None, 'mp')
- grad_b_up: float32 [2048], P('mp')
- grad_w_down: float32 [2048, 512], P('mp')
The draws below stay inside these ranges and needn't reach their ends.
Inputs may be any that keep to these rules, and one draw needn't show every extreme that they name: `resets`: in each packed row the first two positions are below 256 and the third is 1792 or later; equal positions may repeat.
All inputs are finite; a program needn't handle non-finite values.
Results may differ from the reference program's by a relative error of at most 0.007.
Values may be sent and summed in bfloat16 or wider, within the bound.
No kernel may reach another device: no remote copies, remote signals or barrier semaphores. Data moves between devices by JAX's collectives and lax.ppermute only.
A program may use at most 128 MiB of HBM per device.

```python
from functools import partial
import jax
import jax.numpy as jnp
from jax import lax

D = 512
H = 1024
FF = 2048
LEN = 2048
ROWS = 8


def draw_resets(key, part):
    key = jax.random.fold_in(key, 7)
    early_key, late_key = jax.random.split(key)
    early = jax.random.randint(early_key, (ROWS, 2), 1, LEN // 8)
    late = jax.random.randint(late_key, (ROWS, 1), LEN - LEN // 8, LEN)
    drawn = jnp.concatenate([early, late], axis=1)
    drawn = drawn.at[0, 0].set(1).at[0, 2].set(LEN - 1)
    return drawn.astype(jnp.int32)


def levels(own_key, shape, cuts, least, top_value):
    loudness, own = 1.0, jax.random.fold_in(own_key, 6)
    for position, blocks in cuts:
        heights = jnp.exp(jax.random.uniform(jax.random.fold_in(own, position), (blocks,), jnp.float32, least / len(cuts), top_value / len(cuts)))
        loudness = loudness * jnp.repeat(heights, shape[position] // blocks).reshape([-1 if axis == position else 1 for axis in range(len(shape))])
    return loudness


def scatter_about(stream_key, shape, deviation, limit, shards=(), kind=jnp.bfloat16):
    loudness = levels(stream_key, shape, shards, -0.22, 0.18) if shards else 1.0
    values = jax.random.normal(stream_key, shape, jnp.float32) * deviation * loudness
    return jnp.minimum(jnp.maximum(values, -limit), limit).astype(kind)


def setup_inputs(seed: int = 0) -> dict:
    key_list = jax.random.split(jax.random.key(seed), 13)
    return {
        "tokens": scatter_about(key_list[0], (ROWS, LEN, D), 1.0, 6.0, ((0, 8), (1, 4))),
        "gain_mix": jnp.clip(1.0 + 0.1 * jax.random.normal(key_list[1], (D,), jnp.float32), 0.5, 1.5),
        "w_mix": scatter_about(key_list[2], (D, 3, H), D ** -0.5, 0.25),
        "bias_forget": jnp.clip(jax.random.uniform(key_list[3], (H,), jnp.float32, 1.0, 6.0), 1.0, 6.0),
        "bias_input": jnp.clip(jax.random.uniform(key_list[4], (H,), jnp.float32, -7.0, -1.0), -7.0, -1.0),
        "w_out": scatter_about(key_list[5], (H, D), (H // 8) ** -0.5, 0.5),
        "gain_mlp": jnp.clip(1.0 + 0.1 * jax.random.normal(key_list[6], (D,), jnp.float32), 0.5, 1.5),
        "w_up": scatter_about(key_list[7], (D, FF), D ** -0.5, 0.25, ((1, 4),)),
        "b_up": jnp.clip(jax.random.uniform(key_list[8], (FF,), jnp.float32, -1.0, 1.0) * levels(key_list[8], (FF,), ((0, 4),), -0.4, 0.0), -1.0, 1.0),
        "w_down": scatter_about(key_list[9], (FF, D), FF ** -0.5, 0.125, ((0, 4),)),
        "resets": draw_resets(jax.random.fold_in(key_list[12], 71), 0),
        "cotangent": scatter_about(key_list[11], (ROWS, LEN, D), 1.0, 6.0, ((0, 8), (1, 4))),
    }


norm_eps = 1e-06
highest = lax.Precision.HIGHEST

@jax.custom_vjp
def low(v):
    return lax.optimization_barrier(v.astype(jnp.bfloat16)).astype(jnp.float32)

@jax.custom_vjp
def low_back(v):
    return v

def low_keep(v):
    return (low(v), None)

def low_pass(kept, grad):
    return (grad,)

def back_keep(v):
    return (v, None)

def back_low(kept, grad):
    return (low(grad),)
low.defvjp(low_keep, low_pass)
low_back.defvjp(back_keep, back_low)

def rms_norm(values, gain):
    return values * lax.rsqrt(lax.optimization_barrier(jnp.mean(values * values, axis=-1, keepdims=True)) + norm_eps) * gain

def combine(first, second):
    return (first[0] * second[0], second[0] * first[1] + second[1])

def gate_pair(projected, bias_forget, bias_input, reset_mask):
    forget = jax.nn.sigmoid(projected[:, :, 0] + bias_forget)
    admit = jax.nn.sigmoid(projected[:, :, 1] + bias_input)
    total = forget + admit
    decay = jnp.where(reset_mask[:, :, None], 0.0, forget / total)
    inject = admit / total * projected[:, :, 2]
    return (decay, inject)

def forward(reset_mask, inputs, gain_mix, w_mix, bias_forget, bias_input, w_out, gain_mlp, w_up, b_up, w_down):
    normed_mix = low(rms_norm(inputs, gain_mix))
    projected = low_back(jnp.einsum('rtd,dkh->rtkh', normed_mix, w_mix, precision=highest))
    decay, inject = gate_pair(projected, bias_forget, bias_input, reset_mask)
    unused, states = lax.associative_scan(combine, (decay, inject), axis=1)
    middle = inputs + low_back(jnp.einsum('rth,hd->rtd', low(states), w_out, precision=highest))
    normed_mlp = low(rms_norm(middle, gain_mlp))
    pre_act = low_back(jnp.einsum('rtd,df->rtf', normed_mlp, w_up, precision=highest)) + b_up
    hidden_act = low(jax.nn.gelu(pre_act))
    return middle + low_back(jnp.einsum('rtf,fd->rtd', hidden_act, w_down, precision=highest))

def reference(tokens, gain_mix, w_mix, bias_forget, bias_input, w_out, gain_mlp, w_up, b_up, w_down, resets, cotangent):
    positions = jnp.arange(LEN, dtype=jnp.int32)
    reset_mask = jnp.any(resets[:, :, None] == positions[None, None, :], axis=1)
    weights = [tokens, gain_mix, w_mix, bias_forget, bias_input, w_out, gain_mlp, w_up, b_up, w_down]
    weights = [item.astype(jnp.float32) for item in weights]
    output_f32, backward = jax.vjp(partial(forward, reset_mask), *weights)
    grads = backward(cotangent.astype(jnp.float32))
    return (output_f32.astype(jnp.bfloat16), grads[0].astype(jnp.bfloat16), grads[1], grads[2], grads[3], grads[4], grads[5], grads[6], grads[7], grads[8], grads[9])
```

```python
from functools import partial

import jax
import jax.numpy as jnp
from jax import lax
from jax.experimental import pallas as pl
from jax.experimental.pallas import tpu as pltpu
from jax.sharding import PartitionSpec as P

norm_eps = 1e-06
gelu_k = 0.7978845608028654
gelu_c = 0.044715
chunks = 8
f32 = jnp.float32
bf16 = jnp.bfloat16
VMEM = pl.BlockSpec(memory_space=pltpu.VMEM)
SMEM = pl.BlockSpec(memory_space=pltpu.SMEM)


def dot(a, b):
    return jnp.dot(a, b, preferred_element_type=f32)


def dot_nt(a, b):
    return lax.dot_general(a, b, (((1,), (1,)), ((), ())), preferred_element_type=f32)


def shape_of(dtype, *shape):
    return jax.ShapeDtypeStruct(shape, dtype)


def call(body, name, operands, outs, scratch=(), smem=1, flops=0, moved=0):
    return pl.pallas_call(
        body,
        out_shape=outs,
        in_specs=[SMEM] * smem + [VMEM] * (len(operands) - smem),
        out_specs=[VMEM] * len(outs),
        scratch_shapes=list(scratch),
        compiler_params=pltpu.CompilerParams(vmem_limit_bytes=48 << 20),
        cost_estimate=pl.CostEstimate(flops=flops, bytes_accessed=moved, transcendentals=0),
        name=name,
    )(*operands)


def to_chunked(src, split, put):
    length, width = src.shape
    steps = length // chunks
    for g in range(width // 128):
        cols = slice(g * 128, (g + 1) * 128)
        split[g] = src[:, cols].astype(f32)
        for s in range(steps):
            put(pl.ds(s * chunks, chunks), cols, split[g, pl.ds(s, chunks, stride=steps), :])


def from_chunked(values, split, out):
    length, width = out.shape
    steps = length // chunks
    for g in range(width // 128):
        cols = slice(g * 128, (g + 1) * 128)
        for s in range(steps):
            split[g, pl.ds(s, chunks, stride=steps), :] = values[s * chunks : (s + 1) * chunks, cols]
        out[:, cols] = split[g].astype(bf16)


def keep_mask(idx, resets, length):
    row = lax.broadcasted_iota(jnp.int32, (length, 1), 0)
    pos = idx[2] * length + (row % chunks) * (length // chunks) + row // chunks
    keep = jnp.ones((length, 1), f32)
    for i in range(3):
        keep = jnp.where(pos == resets[i], 0.0, keep)
    return keep


def mixer_in(idx, resets, tok, gain, w, bias_f, bias_i, b_up, decay, share, cand, du, dv, nmt, x, prods, ends, payload, split):
    length, width = tok.shape
    units = bias_f.shape[1]
    steps = length // chunks

    def put(rows, cols, values):
        x[rows, cols] = values

    to_chunked(tok, split, put)
    v = x[...]
    r = lax.rsqrt(jnp.mean(v * v, axis=-1, keepdims=True) + norm_eps)
    nm = (v * r * gain[...]).astype(bf16)
    nmt[...] = nm.T
    keep = keep_mask(idx, resets, length)
    block = 256
    for h in range(0, units, block):
        sl = pl.ds(h, block)
        a = jnp.exp(jnp.minimum(-(dot(nm, w[0, :, sl]) + bias_f[:, sl]), 88.0))
        b = jnp.exp(jnp.minimum(-(dot(nm, w[1, :, sl]) + bias_i[:, sl]), 88.0))
        t = 1.0 / (2.0 + a + b)
        p = (1.0 + b) * t
        q = (1.0 + a) * t
        decay[:, sl] = p * keep
        share[:, sl] = q
        cand[:, sl] = dot(nm, w[2, :, sl])
        du[:, sl] = p * (a * t)
        dv[:, sl] = q * (b * t)

    def step(s, carry):
        prod, end = carry
        rows = pl.ds(pl.multiple_of(s * chunks, chunks), chunks)
        d = decay[rows, :]
        return prod * d, end * d + share[rows, :] * cand[rows, :]

    prod, end = lax.fori_loop(
        0, steps, step, (jnp.ones((chunks, units), f32), jnp.zeros((chunks, units), f32)), unroll=8
    )
    prods[...] = prod
    ends[...] = end
    total, state = prod[0:1], end[0:1]
    for k in range(1, chunks):
        total = total * prod[k : k + 1]
        state = state * prod[k : k + 1] + end[k : k + 1]
    payload[...] = jnp.zeros_like(payload)
    payload[0:1, :] = total
    payload[1:2, :] = state
    payload[2:3, 0 : b_up.shape[1]] = b_up[...]


def feed_forward(nm, cot, wu, wd, bu):
    pre = dot(nm, wu) + bu
    grad_act = dot_nt(cot, wd)
    sq = pre * pre
    t = jnp.tanh(pre * (gelu_k + gelu_k * gelu_c * sq))
    half = 0.5 + 0.5 * t
    h = pre * half
    slope = half + h * (1.0 - t) * (gelu_k + 3.0 * gelu_k * gelu_c * sq)
    grad_pre = grad_act * slope
    return h.astype(bf16), grad_pre.astype(bf16), jnp.sum(grad_pre, axis=0, keepdims=True)


def store_pieces(ref, slot, base, rows, values):
    for p in range(4):
        ref[p, slot, base : base + rows, :] = values[p * rows : (p + 1) * rows].astype(bf16)


def ffn_block(slot, core, nm, nmt, cot, wu, wd, bu, mix, gn, keep, send, hT):
    h, g, bsum = feed_forward(nm, cot, wu, wd, bu)
    hT[...] = h.T
    half = nm.shape[1] // 2
    for ref, which in ((send, 1 - core), (keep, core)):
        rows = pl.ds(pl.multiple_of(which * half, half), half)
        store_pieces(ref, slot, 0, half // 4, dot(nmt[rows, :], g))
        store_pieces(ref, slot, half // 4, half // 4, dot(hT[rows, :], cot))
    mix[...] += dot(h, wd)
    gn[...] += dot_nt(g, wu)
    return bsum


def block_mid(idx, own, r1, r2, r3, prods, ends, decay, share, cand, x, cot, w_out, gain, wu, wd, bu,
              st, stT, middle, nm2, nm2t, cotp, mix, gn, bsum, keep, send, split, others, hT, carry8):
    length = x.shape[0]
    steps = length // chunks
    units = decay.shape[1]
    core, z = idx[0], idx[2]
    for j, ref in enumerate((own, r1, r2, r3)):
        others[j] = ref[...]
    state = jnp.zeros((1, units), f32)
    for k in range(4):
        part = others[k ^ z]
        state = jnp.where(k < z, state * part[0:1] + part[1:2], state)
    for k in range(chunks):
        carry8[k : k + 1, :] = state
        state = state * prods[k : k + 1, :] + ends[k : k + 1, :]
    st[0:chunks, :] = carry8[...]

    def step(s, state):
        rows = pl.ds(pl.multiple_of(s * chunks, chunks), chunks)
        state = state * decay[rows, :] + share[rows, :] * cand[rows, :]
        st[pl.ds(pl.multiple_of(s * chunks + chunks, chunks), chunks), :] = state
        return state

    lax.fori_loop(0, steps, step, carry8[...], unroll=8)
    low = st[chunks:, :].astype(bf16)
    stT[...] = low.T
    mid = x[...] + dot(low, w_out[...])
    middle[...] = mid
    r = lax.rsqrt(jnp.mean(mid * mid, axis=-1, keepdims=True) + norm_eps)
    nm = (mid * r * gain[...]).astype(bf16)
    nm2[...] = nm
    nm2t[...] = nm.T

    def put(rows, cols, values):
        gn[rows, cols] = values

    to_chunked(cot, split, put)
    cotp[...] = gn[...].astype(bf16)
    gn[...] = jnp.zeros_like(gn)
    mix[...] = mid
    bsum[...] = ffn_block(0, core, nm, nm2t, cotp[...], wu[...], wd[...], bu[...], mix, gn, keep, send, hT)


def block_mlp(idx, a0, a1, a2, a3, b0, b1, b2, b3, r1, r2, r3, mix0, gn0, bsum0, keep0, send0, nm2, nm2t, cotp, middle, gain,
              stT, w_out, decay,
              mixed, keep, send, grad_mid, grad_states, payload, small, mix, gn, hT, wu, wd, split):
    core, plane, z = idx[0], idx[1], idx[2]
    length, units = decay.shape
    steps = length // chunks
    mix[...] = mix0[...]
    gn[...] = gn0[...]
    small[...] = jnp.zeros_like(small)
    rows8 = wu.shape[0] // 8
    for p in range(4):
        keep[p, 0, 0 : 2 * rows8, :] = keep0[p, 0]
        send[p, 0, 0 : 2 * rows8, :] = send0[p, 0]
    small[pl.ds(6 + z, 1), :] = bsum0[...]
    for j, bias in ((1, r1), (2, r2), (3, r3)):
        for which, pieces in ((core, (a0, a1, a2, a3)), (1 - core, (b0, b1, b2, b3))):
            for k, piece in enumerate(pieces):
                at = pl.ds(pl.multiple_of((which * 4 + (plane ^ k)) * rows8, rows8), rows8)
                top = (j - 1) * 2 * rows8
                wu[at, :] = piece[top : top + rows8, :]
                wd[at, :] = piece[top + rows8 : top + 2 * rows8, :]
        bu = bias[2:3, 0 : wu.shape[1]]
        small[pl.ds(6 + (z ^ j), 1), :] = ffn_block(
            j, core, nm2[...], nm2t, cotp[...], wu[...], wd[...], bu, mix, gn, keep, send, hT
        )
    from_chunked(mix, split, mixed)
    mid = middle[...]
    r = lax.rsqrt(jnp.mean(mid * mid, axis=-1, keepdims=True) + norm_eps)
    scaled = mid * r
    g = gn[...]
    small[5:6, :] = jnp.sum(g * scaled, axis=0, keepdims=True)
    gg = g * gain[...]
    gm = cotp[...].astype(f32) + r * (gg - scaled * jnp.mean(gg * scaled, axis=-1, keepdims=True))
    grad_mid[...] = gm
    low = gm.astype(bf16)
    part = units // 8
    for k in range(4):
        for ref, which in ((send, 1 - core), (keep, core)):
            got = dot(stT[pl.ds(pl.multiple_of((2 * k + which) * part, part), part), :], low)
            for p in range(4):
                ref[p, k ^ z, 2 * rows8 :, :] = got[p * (part // 4) : (p + 1) * (part // 4)].astype(bf16)
    grad_states[...] = dot_nt(low, w_out[...])

    def step(i, carry):
        prod, flow = carry
        rows = pl.ds(pl.multiple_of((steps - 1 - i) * chunks, chunks), chunks)
        d = decay[rows, :]
        return prod * d, (flow + grad_states[rows, :]) * d

    prod, flow = lax.fori_loop(
        0, steps, step, (jnp.ones((chunks, units), f32), jnp.zeros((chunks, units), f32)), unroll=8
    )
    total, out = prod[chunks - 1 :], flow[chunks - 1 :]
    for k in range(chunks - 2, -1, -1):
        total = total * prod[k : k + 1]
        out = out * prod[k : k + 1] + flow[k : k + 1]
    payload[...] = jnp.zeros_like(payload)
    payload[0:1, :] = total
    payload[1:2, :] = out
    payload[8:16, :] = prod
    payload[16:24, :] = flow


def gate_grads(which, keep, carried, st, share, cand, du, dv, w, nmt, z, out, gnm, small):
    length, units = carried.shape
    half = units // 2
    cols = pl.ds(pl.multiple_of(which * half, half), half)
    cf = carried[:, cols]
    q = share[:, cols]
    s = cf * (st[0:length, cols] * keep - cand[:, cols])
    ga = s * du[:, cols]
    gb = -(s * dv[:, cols])
    small[pl.ds(which, 1), :] = jnp.sum(ga, axis=0, keepdims=True)
    small[pl.ds(2 + which, 1), :] = jnp.sum(gb, axis=0, keepdims=True)
    part = nmt.shape[0] // 4
    for k, g in enumerate((ga, gb, cf * q)):
        low = g.astype(bf16)
        got = dot(nmt[...], low)
        for zz in range(4):
            for p in range(4):
                top = zz * part + p * (part // 4)
                out[p, zz ^ z, k * (part // 4) : (k + 1) * (part // 4), :] = got[top : top + part // 4].astype(bf16)
        gnm[...] += dot_nt(low, w[k, :, cols])


def mixer_back(idx, resets, own, r1, r2, r3, decay, share, cand, du, dv, st, grad_states, nmt, w,
               carried, send, gnm, small, others, carry8):
    length, units = decay.shape
    steps = length // chunks
    core, z = idx[0], idx[2]
    for j, ref in enumerate((own, r1, r2, r3)):
        others[j] = ref[0:8, :]
    flow = jnp.zeros((1, units), f32)
    for k in range(3, -1, -1):
        part = others[k ^ z]
        flow = jnp.where(k > z, flow * part[0:1] + part[1:2], flow)
    for k in range(chunks - 1, -1, -1):
        carry8[k : k + 1, :] = flow
        flow = flow * own[8 + k : 9 + k, :] + own[16 + k : 17 + k, :]

    def step(i, flow):
        rows = pl.ds(pl.multiple_of((steps - 1 - i) * chunks, chunks), chunks)
        got = grad_states[rows, :] + flow
        carried[rows, :] = got
        return got * decay[rows, :]

    lax.fori_loop(0, steps, step, carry8[...], unroll=8)
    gnm[...] = jnp.zeros_like(gnm)
    small[...] = jnp.zeros_like(small)
    gate_grads(1 - core, keep_mask(idx, resets, length), carried, st, share, cand, du, dv, w, nmt, z, send, gnm, small)


def mixer_out(idx, resets, carried, share, cand, du, dv, st, nmt, w, gnm0, small0, small1, x, gain, grad_mid,
              keep, grad_tok, small, gnm, split):
    length, units = carried.shape
    core, z = idx[0], idx[2]
    gnm[...] = gnm0[...]
    small[...] = small0[...] + small1[...]
    gate_grads(core, keep_mask(idx, resets, length), carried, st, share, cand, du, dv, w, nmt, z, keep, gnm, small)
    v = x[...]
    r = lax.rsqrt(jnp.mean(v * v, axis=-1, keepdims=True) + norm_eps)
    scaled = v * r
    g = gnm[...]
    small[4:5, :] = jnp.sum(g * scaled, axis=0, keepdims=True)
    gg = g * gain[...]
    gnm[...] = grad_mid[...] + r * (gg - scaled * jnp.mean(gg * scaled, axis=-1, keepdims=True))
    from_chunked(gnm, split, grad_tok)


def pick_piece(idx, wu, wd, out):
    rows = wu.shape[0] // 8
    at = pl.ds(pl.multiple_of((idx[0] * 4 + idx[1]) * rows, rows), rows)
    out[0:rows, :] = wu[at, :]
    out[rows:, :] = wd[at, :]


def join3(a, b, c, out):
    n = a.shape[0]
    out[0:n, :] = a[...]
    out[n : 2 * n, :] = b[...]
    out[2 * n :, :] = c[...]


def two_terms(v):
    high = v.astype(bf16)
    return high, (v - high.astype(f32)).astype(bf16)


def add_plane(idx, keep, got, s1, s2, s3, own):
    plane = idx[1]
    for k, ref in ((1, s1), (2, s2), (3, s3)):
        at = plane ^ k
        ref[...] = (keep[at].astype(f32) + got[at].astype(f32)).astype(bf16)
    own[...] = keep[plane].astype(f32) + got[plane].astype(f32)


def add_depth(own, g1, g2, g3, s1, s2, s3, out):
    rows = out.shape[0]
    for k, ref in enumerate((out, s1, s2, s3)):
        at = pl.ds(k * rows, rows)
        total = (own[at, :] + g1[at, :].astype(f32)) + (g2[at, :].astype(f32) + g3[at, :].astype(f32))
        ref[...] = total.astype(ref.dtype)


def add_last(own, g1, g2, g3, out):
    total = (own[...] + g1[...].astype(f32)) + (g2[...].astype(f32) + g3[...].astype(f32))
    out[...] = total.astype(out.dtype)


def add_plane_small(idx, keep, got, small, small_got, s1, s2, s3, own, small_out):
    plane = idx[1]
    rows, n = own.shape[0], small.shape[0]
    high, low = two_terms(small[...] + small_got[...])
    small_out[0:n, :] = high
    small_out[n:, :] = low
    for k, ref in ((1, s1), (2, s2), (3, s3)):
        at = plane ^ k
        ref[0:rows, :] = (keep[at].astype(f32) + got[at].astype(f32)).astype(bf16)
        ref[rows : rows + n, :] = high
        ref[rows + n :, :] = low
    own[...] = keep[plane].astype(f32) + got[plane].astype(f32)


def add_depth_small(idx, own, small, g1, g2, g3, s1, s2, s3, out, small_out, parts):
    plane = idx[1]
    total_rows, n, rows = own.shape[0], small_out.shape[0], out.shape[0]
    parts[plane] = small[0:n, :].astype(f32) + small[n:, :].astype(f32)
    for k, ref in ((1, g1), (2, g2), (3, g3)):
        parts[plane ^ k] = ref[total_rows : total_rows + n, :].astype(f32) + ref[total_rows + n :, :].astype(f32)
    tiny = (parts[0] + parts[1]) + (parts[2] + parts[3])
    small_out[...] = tiny
    high, low = two_terms(tiny)
    for k, ref in enumerate((out, s1, s2, s3)):
        at = pl.ds(k * rows, rows)
        total = (own[at, :] + g1[at, :].astype(f32)) + (g2[at, :].astype(f32) + g3[at, :].astype(f32))
        ref[0:rows, :] = total.astype(ref.dtype)
        if k:
            ref[rows : rows + n, :] = high
            ref[rows + n :, :] = low


def add_last_small(own, small, g1, g2, g3, out, small_out):
    rows, n = own.shape[0], small.shape[0]
    total = own[...]
    tiny = small[...]
    for ref in (g1, g2, g3):
        total = total + ref[0:rows, :].astype(f32)
        tiny = tiny + (ref[rows : rows + n, :].astype(f32) + ref[rows + n :, :].astype(f32))
    out[...] = total.astype(out.dtype)
    small_out[...] = tiny


def spread_mlp(idx, a0, a1, a2, a3, b0, b1, b2, b3, up, down, w_out):
    core, plane = idx[0], idx[1]
    rows = up.shape[0] // 8
    rows_out = w_out.shape[0] // 8
    for which, pieces in ((core, (a0, a1, a2, a3)), (1 - core, (b0, b1, b2, b3))):
        for k, piece in enumerate(pieces):
            spot = which * 4 + (plane ^ k)
            at = pl.ds(pl.multiple_of(spot * rows, rows), rows)
            up[at, :] = piece[0:rows, :].astype(f32)
            down[at, :] = piece[rows : 2 * rows, :].astype(f32)
            w_out[pl.ds(pl.multiple_of(spot * rows_out, rows_out), rows_out), :] = piece[2 * rows :, :].astype(f32)


def spread_mix(idx, small, a0, a1, a2, a3, b0, b1, b2, b3, out, bias_f, bias_i, gain_mix, gain_mlp, b_up):
    core, plane, z = idx[0], idx[1], idx[2]
    rows, half = out.shape[1] // 4, out.shape[2] // 2
    for which, pieces in ((core, (a0, a1, a2, a3)), (1 - core, (b0, b1, b2, b3))):
        for k, piece in enumerate(pieces):
            at = pl.ds(pl.multiple_of((plane ^ k) * rows, rows), rows)
            cols = pl.ds(pl.multiple_of(which * half, half), half)
            for i in range(3):
                out[i, at, cols] = piece[i * rows : (i + 1) * rows, :].astype(f32)
    n = bias_f.shape[1]
    cols = pl.ds(pl.multiple_of((z % 2) * n, n), n)
    bias_f[...] = small[pl.ds(z // 2, 1), cols]
    bias_i[...] = small[pl.ds(2 + z // 2, 1), cols]
    n = gain_mix.shape[1]
    cols = pl.ds(pl.multiple_of(z * n, n), n)
    gain_mix[...] = small[4:5, cols]
    gain_mlp[...] = small[5:6, cols]
    b_up[...] = small[pl.ds(6 + z, 1), :]


def swap(value, axis, bit):
    size = lax.axis_size(axis)
    return lax.ppermute(value, axis, [(i, i ^ bit) for i in range(size)])


def on_device(tokens, gain_mix, w_mix, bias_forget, bias_input, w_out, gain_mlp, w_up, b_up, w_down, resets, cotangent):
    length, width = tokens.shape[1:]
    units = w_out.shape[0]
    ff = w_up.shape[1]
    dp, mp = lax.axis_size("dp"), lax.axis_size("mp")
    assert mp == 4 and dp % 8 == 0 and tokens.shape[0] == 1
    place = lax.axis_index("dp")
    idx = jnp.stack([place & 1, (place >> 1) & 3, lax.axis_index("mp")]).astype(jnp.int32)
    tok, cot, res = tokens[0], cotangent[0], resets[0]
    w3 = w_mix.transpose(1, 0, 2)
    row = lambda v: v.reshape(1, -1)
    lanes = width // 128

    (piece,) = call(pick_piece, "pick_piece", (idx, w_up, w_down), [shape_of(bf16, width // 4, ff)])
    depth = [swap(piece, "mp", j) for j in (1, 2, 3)]
    (cat,) = call(join3, "join3", depth, [shape_of(bf16, 3 * width // 4, ff)], smem=0)
    near = [cat] + [swap(cat, "dp", 2 * k) for k in (1, 2, 3)]
    far = [swap(v, "dp", 1) for v in near]

    wide = shape_of(f32, length, units)
    square = shape_of(f32, length, width)
    square16 = shape_of(bf16, length, width)
    edge = shape_of(f32, chunks, units)
    decay, share, cand, du, dv, nmt, x, prods, ends, payload = call(
        mixer_in, "mixer_in",
        (idx, res, tok, row(gain_mix), w3, row(bias_forget), row(bias_input), row(b_up)),
        [wide] * 5 + [shape_of(bf16, width, length), square, edge, edge, edge],
        [pltpu.VMEM((lanes, length, 128), f32)], smem=2, flops=6 * length * width * units, moved=16 << 20,
    )
    ahead = [swap(payload, "mp", j) for j in (1, 2, 3)]
    quarter = width // 8
    st, stT, middle, nm2, nm2t, cotp, mix, gn, bsum, keep0, send0 = call(
        block_mid, "block_mid",
        (idx, payload, *ahead, prods, ends, decay, share, cand, x, cot, w_out, row(gain_mlp), w_up, w_down, row(b_up)),
        [shape_of(f32, length + chunks, units), shape_of(bf16, units, length), square, square16, shape_of(bf16, width, length),
         square16, square, square, shape_of(f32, 1, ff)] + [shape_of(bf16, 4, 1, 2 * quarter, width)] * 2,
        [pltpu.VMEM((lanes, length, 128), f32), pltpu.VMEM((4, chunks, units), f32), pltpu.VMEM((ff, length), bf16),
         pltpu.VMEM((chunks, units), f32)],
        flops=16 * length * width * width, moved=16 << 20,
    )
    rows_f = 2 * quarter + units // 32
    mixed, keep, send, grad_mid, grad_states, payload, small = call(
        block_mlp, "block_mlp",
        (idx, *near, *far, *ahead, mix, gn, bsum, keep0, send0, nm2, nm2t, cotp, middle, row(gain_mlp), stT, w_out, decay),
        [square16] + [shape_of(bf16, 4, 4, rows_f, width)] * 2 + [square, wide, shape_of(f32, 24, units), shape_of(f32, 16, width)],
        [pltpu.VMEM((length, width), f32)] * 2 + [pltpu.VMEM((ff, length), bf16), pltpu.VMEM((width, ff), bf16),
         pltpu.VMEM((ff, width), bf16), pltpu.VMEM((lanes, length, 128), f32)],
        flops=44 * length * width * width, moved=24 << 20,
    )
    behind = [swap(payload, "mp", j) for j in (1, 2, 3)]

    flat = lambda v: v.reshape(4, -1, width)
    got = swap(send, "dp", 1)
    s1, s2, s3, own = call(add_plane, "add_plane", (idx, flat(keep), flat(got)),
                           [shape_of(bf16, 4 * rows_f, width)] * 3 + [shape_of(f32, 4 * rows_f, width)], moved=8 << 20)
    got = [swap(v, "dp", 2 * k) for k, v in ((1, s1), (2, s2), (3, s3))]
    s1, s2, s3, own = call(add_depth, "add_depth", (own, *got),
                           [shape_of(bf16, rows_f, width)] * 3 + [shape_of(f32, rows_f, width)], smem=0, moved=4 << 20)
    got = [swap(v, "mp", j) for j, v in ((1, s1), (2, s2), (3, s3))]
    across = [[g * 8 + i for g in range(dp // 8)] for i in range(8)]

    def last(fn, name, operands, outs):
        if dp == 8:
            return call(fn, name, operands, outs, smem=0, moved=1 << 20)
        done = call(fn, name, operands, [shape_of(f32, *o.shape) for o in outs], smem=0, moved=1 << 20)
        return [lax.psum(v, "dp", axis_index_groups=across).astype(o.dtype) for v, o in zip(done, outs)]

    (part,) = last(add_last, "add_last", (own, *got), [shape_of(bf16, rows_f, width)])
    near = [part] + [swap(part, "dp", 2 * k) for k in (1, 2, 3)]
    far = [swap(v, "dp", 1) for v in near]
    grad_up, grad_down, grad_out = call(
        spread_mlp, "spread_mlp", (idx, *near, *far),
        [shape_of(f32, width, ff), shape_of(f32, ff, width), shape_of(f32, units // 4, width)], moved=6 << 20,
    )

    rows_m = 3 * width // 16
    carried, send, gnm, small_a = call(
        mixer_back, "mixer_back",
        (idx, res, payload, *behind, decay, share, cand, du, dv, st, grad_states, nmt, w3),
        [wide, shape_of(bf16, 4, 4, rows_m, units // 2), square, shape_of(f32, 16, width)],
        [pltpu.VMEM((4, chunks, units), f32), pltpu.VMEM((chunks, units), f32)],
        smem=2, flops=6 * length * width * units, moved=16 << 20,
    )
    got = swap(send, "dp", 1)
    keep, grad_tok, small = call(
        mixer_out, "mixer_out",
        (idx, res, carried, share, cand, du, dv, st, nmt, w3, gnm, small_a, small, x, row(gain_mix), grad_mid),
        [shape_of(bf16, 4, 4, rows_m, units // 2), square16, shape_of(f32, 16, width)],
        [pltpu.VMEM((length, width), f32), pltpu.VMEM((lanes, length, 128), f32)],
        smem=2, flops=6 * length * width * units, moved=16 << 20,
    )
    small_got = swap(small, "dp", 1)
    s1, s2, s3, own, small = call(
        add_plane_small, "add_plane_small", (idx, flat(keep), flat(got), small, small_got),
        [shape_of(bf16, 4 * rows_m + 32, width)] * 3 + [shape_of(f32, 4 * rows_m, width), shape_of(bf16, 32, width)], moved=6 << 20,
    )
    got = [swap(v, "dp", 2 * k) for k, v in ((1, s1), (2, s2), (3, s3))]
    s1, s2, s3, own, small = call(
        add_depth_small, "add_depth_small", (idx, own, small, *got),
        [shape_of(bf16, rows_m + 32, width)] * 3 + [shape_of(f32, rows_m, width), shape_of(f32, 16, width)],
        [pltpu.VMEM((4, 16, width), f32)], moved=2 << 20,
    )
    got = [swap(v, "mp", j) for j, v in ((1, s1), (2, s2), (3, s3))]
    part, small = last(add_last_small, "add_last_small", (own, small, *got),
                       [shape_of(bf16, rows_m, width), shape_of(f32, 16, width)])
    near = [part] + [swap(part, "dp", 2 * k) for k in (1, 2, 3)]
    far = [swap(v, "dp", 1) for v in near]
    grad_mix, g_bf, g_bi, g_gain_mix, g_gain_mlp, g_bu = call(
        spread_mix, "spread_mix", (idx, small, *near, *far),
        [shape_of(f32, 3, width // 4, units), shape_of(f32, 1, units // 4), shape_of(f32, 1, units // 4),
         shape_of(f32, 1, width // 4), shape_of(f32, 1, width // 4), shape_of(f32, 1, ff)], moved=3 << 20,
    )
    return (
        mixed[None], grad_tok[None], g_gain_mix[0], grad_mix.transpose(1, 0, 2), g_bf[0], g_bi[0],
        grad_out, g_gain_mlp[0], grad_up, g_bu[0], grad_down,
    )


def solution(mesh):
    return jax.shard_map(
        on_device,
        mesh=mesh,
        in_specs=(P("dp", "mp", None), P(), P(), P(), P(), P(), P(), P(None, "mp"), P("mp"), P("mp", None), P("dp", None), P("dp", "mp", None)),
        out_specs=(P("dp", "mp", None), P("dp", "mp", None), P("mp"), P("mp", None, None), P("mp"), P("mp"), P("mp", None), P("mp"), P(None, "mp"), P("mp"), P("mp", None)),
        check_vma=False,
    )
```

```python
from functools import partial

import jax
import jax.numpy as jnp
from jax import lax
from jax.experimental import pallas as pl
from jax.experimental.pallas import tpu as pltpu
from jax.sharding import PartitionSpec as P

norm_eps = 1e-06
gelu_k = 0.7978845608028654
gelu_c = 0.044715
chunks = 8
f32 = jnp.float32
bf16 = jnp.bfloat16
VMEM = pl.BlockSpec(memory_space=pltpu.VMEM)
SMEM = pl.BlockSpec(memory_space=pltpu.SMEM)


def dot(a, b):
    return jnp.dot(a, b, preferred_element_type=f32)


def dot_nt(a, b):
    return lax.dot_general(a, b, (((1,), (1,)), ((), ())), preferred_element_type=f32)


def shape_of(dtype, *shape):
    return jax.ShapeDtypeStruct(shape, dtype)


def call(body, name, operands, outs, scratch=(), smem=1, flops=0, moved=0, limit=16, after=()):
    n, extra = len(operands), len(after)

    def run(*refs):
        body(*refs[:n], *refs[n + extra :])

    return pl.pallas_call(
        run,
        out_shape=outs,
        in_specs=[SMEM] * smem + [VMEM] * (n - smem) + [pl.BlockSpec(memory_space=pl.ANY)] * extra,
        out_specs=[VMEM] * len(outs),
        scratch_shapes=list(scratch),
        compiler_params=pltpu.CompilerParams(vmem_limit_bytes=limit << 20),
        cost_estimate=pl.CostEstimate(flops=flops, bytes_accessed=moved, transcendentals=0),
        name=name,
    )(*operands, *after)


def to_chunked(src, split, put):
    length, width = src.shape
    steps = length // chunks
    for g in range(width // 128):
        cols = slice(g * 128, (g + 1) * 128)
        split[g] = src[:, cols].astype(f32)
        for s in range(steps):
            put(pl.ds(s * chunks, chunks), cols, split[g, pl.ds(s, chunks, stride=steps), :])


def from_chunked(values, split, out):
    length, width = out.shape
    steps = length // chunks
    for g in range(width // 128):
        cols = slice(g * 128, (g + 1) * 128)
        for s in range(steps):
            split[g, pl.ds(s, chunks, stride=steps), :] = values[s * chunks : (s + 1) * chunks, cols]
        out[:, cols] = split[g].astype(bf16)


def keep_mask(idx, resets, length):
    row = lax.broadcasted_iota(jnp.int32, (length, 1), 0)
    pos = idx[2] * length + (row % chunks) * (length // chunks) + row // chunks
    keep = jnp.ones((length, 1), f32)
    for i in range(3):
        keep = jnp.where(pos == resets[i], 0.0, keep)
    return keep


def mixer_in(idx, resets, tok, gain, w, bias_f, bias_i, b_up, decay, share, cand, du, dv, nmt, x, prods, ends, payload, split):
    length, width = tok.shape
    units = bias_f.shape[1]
    steps = length // chunks

    def put(rows, cols, values):
        x[rows, cols] = values

    to_chunked(tok, split, put)
    v = x[...]
    r = lax.rsqrt(jnp.mean(v * v, axis=-1, keepdims=True) + norm_eps)
    nm = (v * r * gain[...]).astype(bf16)
    nmt[...] = nm.T
    keep = keep_mask(idx, resets, length)
    block = 256
    for h in range(0, units, block):
        sl = pl.ds(h, block)
        a = jnp.exp(jnp.minimum(-(dot(nm, w[0, :, sl]) + bias_f[:, sl]), 88.0))
        b = jnp.exp(jnp.minimum(-(dot(nm, w[1, :, sl]) + bias_i[:, sl]), 88.0))
        t = 1.0 / (2.0 + a + b)
        p = (1.0 + b) * t
        q = (1.0 + a) * t
        decay[:, sl] = p * keep
        share[:, sl] = q
        cand[:, sl] = dot(nm, w[2, :, sl])
        du[:, sl] = p * (a * t)
        dv[:, sl] = q * (b * t)

    def step(s, carry):
        prod, end = carry
        rows = pl.ds(pl.multiple_of(s * chunks, chunks), chunks)
        d = decay[rows, :]
        return prod * d, end * d + share[rows, :] * cand[rows, :]

    prod, end = lax.fori_loop(
        0, steps, step, (jnp.ones((chunks, units), f32), jnp.zeros((chunks, units), f32)), unroll=8
    )
    prods[...] = prod
    ends[...] = end
    total, state = prod[0:1], end[0:1]
    for k in range(1, chunks):
        total = total * prod[k : k + 1]
        state = state * prod[k : k + 1] + end[k : k + 1]
    payload[...] = jnp.zeros_like(payload)
    payload[0:1, :] = total
    payload[1:2, :] = state
    payload[2:3, 0 : b_up.shape[1]] = b_up[...]


def feed_forward(nm, cot, wu, wd, bu):
    pre = dot(nm, wu) + bu
    grad_act = dot_nt(cot, wd)
    sq = pre * pre
    t = jnp.tanh(pre * (gelu_k + gelu_k * gelu_c * sq))
    half = 0.5 + 0.5 * t
    h = pre * half
    slope = half + h * (1.0 - t) * (gelu_k + 3.0 * gelu_k * gelu_c * sq)
    grad_pre = grad_act * slope
    return h.astype(bf16), grad_pre.astype(bf16), jnp.sum(grad_pre, axis=0, keepdims=True)


def store_pieces(ref, slot, base, rows, values):
    for p in range(4):
        ref[p, slot, base : base + rows, :] = values[p * rows : (p + 1) * rows].astype(bf16)


def ffn_block(slot, core, nm, nmt, cot, wu, wd, bu, mix, gn, keep, send, hT):
    h, g, bsum = feed_forward(nm, cot, wu, wd, bu)
    hT[...] = h.T
    half = nm.shape[1] // 2
    for ref, which in ((send, 1 - core), (keep, core)):
        rows = pl.ds(pl.multiple_of(which * half, half), half)
        store_pieces(ref, slot, 0, half // 4, dot(nmt[rows, :], g))
        store_pieces(ref, slot, half // 4, half // 4, dot(hT[rows, :], cot))
    mix[...] += dot(h, wd)
    gn[...] += dot_nt(g, wu)
    return bsum


def block_mid(idx, own, r1, r2, r3, prods, ends, decay, share, cand, x, cot, w_out, gain, wu, wd, bu,
              st, stT, middle, nm2, nm2t, cotp, mix, gn, bsum, keep, send, split, others, hT, carry8):
    length = x.shape[0]
    steps = length // chunks
    units = decay.shape[1]
    core, z = idx[0], idx[2]
    for j, ref in enumerate((own, r1, r2, r3)):
        others[j] = ref[...]
    state = jnp.zeros((1, units), f32)
    for k in range(4):
        part = others[k ^ z]
        state = jnp.where(k < z, state * part[0:1] + part[1:2], state)
    for k in range(chunks):
        carry8[k : k + 1, :] = state
        state = state * prods[k : k + 1, :] + ends[k : k + 1, :]
    st[0:chunks, :] = carry8[...]

    def step(s, state):
        rows = pl.ds(pl.multiple_of(s * chunks, chunks), chunks)
        state = state * decay[rows, :] + share[rows, :] * cand[rows, :]
        st[pl.ds(pl.multiple_of(s * chunks + chunks, chunks), chunks), :] = state
        return state

    lax.fori_loop(0, steps, step, carry8[...], unroll=8)
    low = st[chunks:, :].astype(bf16)
    stT[...] = low.T
    mid = x[...] + dot(low, w_out[...])
    middle[...] = mid
    r = lax.rsqrt(jnp.mean(mid * mid, axis=-1, keepdims=True) + norm_eps)
    nm = (mid * r * gain[...]).astype(bf16)
    nm2[...] = nm
    nm2t[...] = nm.T

    def put(rows, cols, values):
        gn[rows, cols] = values

    to_chunked(cot, split, put)
    cotp[...] = gn[...].astype(bf16)
    gn[...] = jnp.zeros_like(gn)
    mix[...] = mid
    bsum[...] = ffn_block(0, core, nm, nm2t, cotp[...], wu[...], wd[...], bu[...], mix, gn, keep, send, hT)


def block_mlp(idx, a0, a1, a2, a3, b0, b1, b2, b3, r1, r2, r3, mix0, gn0, bsum0, keep0, send0, nm2, nm2t, cotp, middle, gain,
              stT, w_out, decay,
              mixed, keep, send, grad_mid, grad_states, payload, small, mix, gn, hT, wu, wd, split):
    core, plane, z = idx[0], idx[1], idx[2]
    length, units = decay.shape
    steps = length // chunks
    mix[...] = mix0[...]
    gn[...] = gn0[...]
    small[...] = jnp.zeros_like(small)
    rows8 = wu.shape[0] // 8
    for p in range(4):
        keep[p, 0, 0 : 2 * rows8, :] = keep0[p, 0]
        send[p, 0, 0 : 2 * rows8, :] = send0[p, 0]
    small[pl.ds(6 + z, 1), :] = bsum0[...]
    for j, bias in ((1, r1), (2, r2), (3, r3)):
        for which, pieces in ((core, (a0, a1, a2, a3)), (1 - core, (b0, b1, b2, b3))):
            for k, piece in enumerate(pieces):
                at = pl.ds(pl.multiple_of((which * 4 + (plane ^ k)) * rows8, rows8), rows8)
                top = (j - 1) * 2 * rows8
                wu[at, :] = piece[top : top + rows8, :]
                wd[at, :] = piece[top + rows8 : top + 2 * rows8, :]
        bu = bias[2:3, 0 : wu.shape[1]]
        small[pl.ds(6 + (z ^ j), 1), :] = ffn_block(
            j, core, nm2[...], nm2t, cotp[...], wu[...], wd[...], bu, mix, gn, keep, send, hT
        )
    from_chunked(mix, split, mixed)
    mid = middle[...]
    r = lax.rsqrt(jnp.mean(mid * mid, axis=-1, keepdims=True) + norm_eps)
    scaled = mid * r
    g = gn[...]
    small[5:6, :] = jnp.sum(g * scaled, axis=0, keepdims=True)
    gg = g * gain[...]
    gm = cotp[...].astype(f32) + r * (gg - scaled * jnp.mean(gg * scaled, axis=-1, keepdims=True))
    grad_mid[...] = gm
    low = gm.astype(bf16)
    part = units // 8
    for k in range(4):
        for ref, which in ((send, 1 - core), (keep, core)):
            got = dot(stT[pl.ds(pl.multiple_of((2 * k + which) * part, part), part), :], low)
            for p in range(4):
                ref[p, k ^ z, 2 * rows8 :, :] = got[p * (part // 4) : (p + 1) * (part // 4)].astype(bf16)
    grad_states[...] = dot_nt(low, w_out[...])

    def step(i, carry):
        prod, flow = carry
        rows = pl.ds(pl.multiple_of((steps - 1 - i) * chunks, chunks), chunks)
        d = decay[rows, :]
        return prod * d, (flow + grad_states[rows, :]) * d

    prod, flow = lax.fori_loop(
        0, steps, step, (jnp.ones((chunks, units), f32), jnp.zeros((chunks, units), f32)), unroll=8
    )
    total, out = prod[chunks - 1 :], flow[chunks - 1 :]
    for k in range(chunks - 2, -1, -1):
        total = total * prod[k : k + 1]
        out = out * prod[k : k + 1] + flow[k : k + 1]
    payload[...] = jnp.zeros_like(payload)
    payload[0:1, :] = total
    payload[1:2, :] = out
    payload[8:16, :] = prod
    payload[16:24, :] = flow


def gate_grads(which, keep, carried, st, share, cand, du, dv, w, nmt, z, out, gnm, small):
    length, units = carried.shape
    half = units // 2
    cols = pl.ds(pl.multiple_of(which * half, half), half)
    cf = carried[:, cols]
    q = share[:, cols]
    s = cf * (st[0:length, cols] * keep - cand[:, cols])
    ga = s * du[:, cols]
    gb = -(s * dv[:, cols])
    small[pl.ds(which, 1), :] = jnp.sum(ga, axis=0, keepdims=True)
    small[pl.ds(2 + which, 1), :] = jnp.sum(gb, axis=0, keepdims=True)
    part = nmt.shape[0] // 4
    for k, g in enumerate((ga, gb, cf * q)):
        low = g.astype(bf16)
        got = dot(nmt[...], low)
        for zz in range(4):
            for p in range(4):
                top = zz * part + p * (part // 4)
                out[p, zz ^ z, k * (part // 4) : (k + 1) * (part // 4), :] = got[top : top + part // 4].astype(bf16)
        gnm[...] += dot_nt(low, w[k, :, cols])


def mixer_back(idx, resets, own, r1, r2, r3, decay, share, cand, du, dv, st, grad_states, nmt, w,
               carried, send, gnm, small, others, carry8):
    length, units = decay.shape
    steps = length // chunks
    core, z = idx[0], idx[2]
    for j, ref in enumerate((own, r1, r2, r3)):
        others[j] = ref[0:8, :]
    flow = jnp.zeros((1, units), f32)
    for k in range(3, -1, -1):
        part = others[k ^ z]
        flow = jnp.where(k > z, flow * part[0:1] + part[1:2], flow)
    for k in range(chunks - 1, -1, -1):
        carry8[k : k + 1, :] = flow
        flow = flow * own[8 + k : 9 + k, :] + own[16 + k : 17 + k, :]

    def step(i, flow):
        rows = pl.ds(pl.multiple_of((steps - 1 - i) * chunks, chunks), chunks)
        got = grad_states[rows, :] + flow
        carried[rows, :] = got
        return got * decay[rows, :]

    lax.fori_loop(0, steps, step, carry8[...], unroll=8)
    gnm[...] = jnp.zeros_like(gnm)
    small[...] = jnp.zeros_like(small)
    gate_grads(1 - core, keep_mask(idx, resets, length), carried, st, share, cand, du, dv, w, nmt, z, send, gnm, small)


def mixer_out(idx, resets, carried, share, cand, du, dv, st, nmt, w, gnm0, small0, small1, x, gain, grad_mid,
              keep, grad_tok, small, gnm, split):
    length, units = carried.shape
    core, z = idx[0], idx[2]
    gnm[...] = gnm0[...]
    small[...] = small0[...] + small1[...]
    gate_grads(core, keep_mask(idx, resets, length), carried, st, share, cand, du, dv, w, nmt, z, keep, gnm, small)
    v = x[...]
    r = lax.rsqrt(jnp.mean(v * v, axis=-1, keepdims=True) + norm_eps)
    scaled = v * r
    g = gnm[...]
    small[4:5, :] = jnp.sum(g * scaled, axis=0, keepdims=True)
    gg = g * gain[...]
    gnm[...] = grad_mid[...] + r * (gg - scaled * jnp.mean(gg * scaled, axis=-1, keepdims=True))
    from_chunked(gnm, split, grad_tok)


def pick_piece(idx, wu, wd, out):
    rows = wu.shape[0]
    out[0:rows, :] = wu[...]
    out[rows:, :] = wd[...]


def own_piece(idx, w_up, w_down):
    rows, width = w_up.shape[0] // 8, w_up.shape[1]
    eighth = pl.BlockSpec((rows, width), lambda i, idx: (idx[0] * 4 + idx[1], 0))
    return pl.pallas_call(
        pick_piece,
        out_shape=shape_of(bf16, 2 * rows, width),
        grid_spec=pltpu.PrefetchScalarGridSpec(
            num_scalar_prefetch=1, grid=(1,), in_specs=[eighth, eighth],
            out_specs=pl.BlockSpec((2 * rows, width), lambda i, idx: (0, 0)),
        ),
        compiler_params=pltpu.CompilerParams(vmem_limit_bytes=2 << 20),
        name="pick_piece",
    )(idx, w_up, w_down)


def join3(a, b, c, out):
    n = a.shape[0]
    out[0:n, :] = a[...]
    out[n : 2 * n, :] = b[...]
    out[2 * n :, :] = c[...]


def two_terms(v):
    high = v.astype(bf16)
    return high, (v - high.astype(f32)).astype(bf16)


def add_plane(idx, keep, got, s1, s2, s3, own):
    plane = idx[1]
    for k, ref in ((1, s1), (2, s2), (3, s3)):
        at = plane ^ k
        ref[...] = (keep[at].astype(f32) + got[at].astype(f32)).astype(bf16)
    own[...] = keep[plane].astype(f32) + got[plane].astype(f32)


def add_depth(own, g1, g2, g3, s1, s2, s3, out):
    rows = out.shape[0]
    for k, ref in enumerate((out, s1, s2, s3)):
        at = pl.ds(k * rows, rows)
        total = (own[at, :] + g1[at, :].astype(f32)) + (g2[at, :].astype(f32) + g3[at, :].astype(f32))
        ref[...] = total.astype(ref.dtype)


def add_last(own, g1, g2, g3, out):
    total = (own[...] + g1[...].astype(f32)) + (g2[...].astype(f32) + g3[...].astype(f32))
    out[...] = total.astype(out.dtype)


def add_plane_small(idx, keep, got, small, small_got, s1, s2, s3, own, small_out):
    plane = idx[1]
    rows, n = own.shape[0], small.shape[0]
    high, low = two_terms(small[...] + small_got[...])
    small_out[0:n, :] = high
    small_out[n:, :] = low
    for k, ref in ((1, s1), (2, s2), (3, s3)):
        at = plane ^ k
        ref[0:rows, :] = (keep[at].astype(f32) + got[at].astype(f32)).astype(bf16)
        ref[rows : rows + n, :] = high
        ref[rows + n :, :] = low
    own[...] = keep[plane].astype(f32) + got[plane].astype(f32)


def add_depth_small(idx, own, small, g1, g2, g3, s1, s2, s3, out, small_out, parts):
    plane = idx[1]
    total_rows, n, rows = own.shape[0], small_out.shape[0], out.shape[0]
    parts[plane] = small[0:n, :].astype(f32) + small[n:, :].astype(f32)
    for k, ref in ((1, g1), (2, g2), (3, g3)):
        parts[plane ^ k] = ref[total_rows : total_rows + n, :].astype(f32) + ref[total_rows + n :, :].astype(f32)
    tiny = (parts[0] + parts[1]) + (parts[2] + parts[3])
    small_out[...] = tiny
    high, low = two_terms(tiny)
    for k, ref in enumerate((out, s1, s2, s3)):
        at = pl.ds(k * rows, rows)
        total = (own[at, :] + g1[at, :].astype(f32)) + (g2[at, :].astype(f32) + g3[at, :].astype(f32))
        ref[0:rows, :] = total.astype(ref.dtype)
        if k:
            ref[rows : rows + n, :] = high
            ref[rows + n :, :] = low


def add_last_small(own, small, g1, g2, g3, out, small_out):
    rows, n = own.shape[0], small.shape[0]
    total = own[...]
    tiny = small[...]
    for ref in (g1, g2, g3):
        total = total + ref[0:rows, :].astype(f32)
        tiny = tiny + (ref[rows : rows + n, :].astype(f32) + ref[rows + n :, :].astype(f32))
    out[...] = total.astype(out.dtype)
    small_out[...] = tiny


def spread_mlp(idx, a0, a1, a2, a3, b0, b1, b2, b3, up, down, w_out):
    core, plane = idx[0], idx[1]
    rows = up.shape[0] // 8
    rows_out = w_out.shape[0] // 8
    for which, pieces in ((core, (a0, a1, a2, a3)), (1 - core, (b0, b1, b2, b3))):
        for k, piece in enumerate(pieces):
            spot = which * 4 + (plane ^ k)
            at = pl.ds(pl.multiple_of(spot * rows, rows), rows)
            up[at, :] = piece[0:rows, :].astype(f32)
            down[at, :] = piece[rows : 2 * rows, :].astype(f32)
            w_out[pl.ds(pl.multiple_of(spot * rows_out, rows_out), rows_out), :] = piece[2 * rows :, :].astype(f32)


def spread_mix(idx, small, a0, a1, a2, a3, b0, b1, b2, b3, out, bias_f, bias_i, gain_mix, gain_mlp, b_up):
    core, plane, z = idx[0], idx[1], idx[2]
    rows, half = out.shape[1] // 4, out.shape[2] // 2
    for which, pieces in ((core, (a0, a1, a2, a3)), (1 - core, (b0, b1, b2, b3))):
        for k, piece in enumerate(pieces):
            at = pl.ds(pl.multiple_of((plane ^ k) * rows, rows), rows)
            cols = pl.ds(pl.multiple_of(which * half, half), half)
            for i in range(3):
                out[i, at, cols] = piece[i * rows : (i + 1) * rows, :].astype(f32)
    n = bias_f.shape[1]
    cols = pl.ds(pl.multiple_of((z % 2) * n, n), n)
    bias_f[...] = small[pl.ds(z // 2, 1), cols]
    bias_i[...] = small[pl.ds(2 + z // 2, 1), cols]
    n = gain_mix.shape[1]
    cols = pl.ds(pl.multiple_of(z * n, n), n)
    gain_mix[...] = small[4:5, cols]
    gain_mlp[...] = small[5:6, cols]
    b_up[...] = small[pl.ds(6 + z, 1), :]


def swap(value, axis, bit):
    size = lax.axis_size(axis)
    return lax.ppermute(value, axis, [(i, i ^ bit) for i in range(size)])


def on_device(tokens, gain_mix, w_mix, bias_forget, bias_input, w_out, gain_mlp, w_up, b_up, w_down, resets, cotangent):
    length, width = tokens.shape[1:]
    units = w_out.shape[0]
    ff = w_up.shape[1]
    dp, mp = lax.axis_size("dp"), lax.axis_size("mp")
    assert mp == 4 and dp % 8 == 0 and tokens.shape[0] == 1
    place = lax.axis_index("dp")
    idx = jnp.stack([place & 1, (place >> 1) & 3, lax.axis_index("mp")]).astype(jnp.int32)
    tok, cot, res = tokens[0], cotangent[0], resets[0]
    w3 = w_mix.transpose(1, 0, 2)
    row = lambda v: v.reshape(1, -1)
    lanes = width // 128

    piece = own_piece(idx, w_up, w_down)
    depth = [swap(piece, "mp", j) for j in (1, 2, 3)]

    wide = shape_of(f32, length, units)
    square = shape_of(f32, length, width)
    square16 = shape_of(bf16, length, width)
    edge = shape_of(f32, chunks, units)
    decay, share, cand, du, dv, nmt, x, prods, ends, payload = call(
        mixer_in, "mixer_in",
        (idx, res, tok, row(gain_mix), w3, row(bias_forget), row(bias_input), row(b_up)),
        [wide] * 5 + [shape_of(bf16, width, length), square, edge, edge, edge],
        [pltpu.VMEM((lanes, length, 128), f32)], smem=2, flops=6 * length * width * units, moved=16 << 20, after=(piece,),
    )
    ahead = [swap(payload, "mp", j) for j in (1, 2, 3)]
    (cat,) = call(join3, "join3", depth, [shape_of(bf16, 3 * width // 4, ff)], smem=0, after=(payload,))
    near = [cat] + [swap(cat, "dp", 2 * k) for k in (1, 2, 3)]
    far = [swap(v, "dp", 1) for v in near]
    quarter = width // 8
    st, stT, middle, nm2, nm2t, cotp, mix, gn, bsum, keep0, send0 = call(
        block_mid, "block_mid",
        (idx, payload, *ahead, prods, ends, decay, share, cand, x, cot, w_out, row(gain_mlp), w_up, w_down, row(b_up)),
        [shape_of(f32, length + chunks, units), shape_of(bf16, units, length), square, square16, shape_of(bf16, width, length),
         square16, square, square, shape_of(f32, 1, ff)] + [shape_of(bf16, 4, 1, 2 * quarter, width)] * 2,
        [pltpu.VMEM((lanes, length, 128), f32), pltpu.VMEM((4, chunks, units), f32), pltpu.VMEM((ff, length), bf16),
         pltpu.VMEM((chunks, units), f32)],
        flops=16 * length * width * width, moved=16 << 20,
    )
    rows_f = 2 * quarter + units // 32
    mixed, keep, send, grad_mid, grad_states, payload, small = call(
        block_mlp, "block_mlp",
        (idx, *near, *far, *ahead, mix, gn, bsum, keep0, send0, nm2, nm2t, cotp, middle, row(gain_mlp), stT, w_out, decay),
        [square16] + [shape_of(bf16, 4, 4, rows_f, width)] * 2 + [square, wide, shape_of(f32, 24, units), shape_of(f32, 16, width)],
        [pltpu.VMEM((length, width), f32)] * 2 + [pltpu.VMEM((ff, length), bf16), pltpu.VMEM((width, ff), bf16),
         pltpu.VMEM((ff, width), bf16), pltpu.VMEM((lanes, length, 128), f32)],
        flops=44 * length * width * width, moved=24 << 20,
    )
    behind = [swap(payload, "mp", j) for j in (1, 2, 3)]

    flat = lambda v: v.reshape(4, -1, width)
    got = swap(send, "dp", 1)
    s1, s2, s3, own_mlp = call(add_plane, "add_plane", (idx, flat(keep), flat(got)),
                           [shape_of(bf16, 4 * rows_f, width)] * 3 + [shape_of(f32, 4 * rows_f, width)], moved=8 << 20)
    got = [swap(v, "dp", 2 * k) for k, v in ((1, s1), (2, s2), (3, s3))]
    s1, s2, s3, own = call(add_depth, "add_depth", (own_mlp, *got),
                           [shape_of(bf16, rows_f, width)] * 3 + [shape_of(f32, rows_f, width)], smem=0, moved=4 << 20)
    got = [swap(v, "mp", j) for j, v in ((1, s1), (2, s2), (3, s3))]
    across = [[g * 8 + i for g in range(dp // 8)] for i in range(8)]

    def last(fn, name, operands, outs):
        if dp == 8:
            return call(fn, name, operands, outs, smem=0, moved=1 << 20)
        done = call(fn, name, operands, [shape_of(f32, *o.shape) for o in outs], smem=0, moved=1 << 20)
        return [lax.psum(v, "dp", axis_index_groups=across).astype(o.dtype) for v, o in zip(done, outs)]

    (part,) = last(add_last, "add_last", (own, *got), [shape_of(bf16, rows_f, width)])
    near = [part] + [swap(part, "dp", 2 * k) for k in (1, 2, 3)]
    far = [swap(v, "dp", 1) for v in near]
    grad_up, grad_down, grad_out = call(
        spread_mlp, "spread_mlp", (idx, *near, *far),
        [shape_of(f32, width, ff), shape_of(f32, ff, width), shape_of(f32, units // 4, width)], moved=6 << 20,
    )

    rows_m = 3 * width // 16
    carried, send, gnm, small_a = call(
        mixer_back, "mixer_back",
        (idx, res, payload, *behind, decay, share, cand, du, dv, st, grad_states, nmt, w3),
        [wide, shape_of(bf16, 4, 4, rows_m, units // 2), square, shape_of(f32, 16, width)],
        [pltpu.VMEM((4, chunks, units), f32), pltpu.VMEM((chunks, units), f32)],
        smem=2, flops=6 * length * width * units, moved=16 << 20, after=(own_mlp,),
    )
    got = swap(send, "dp", 1)
    keep, grad_tok, small = call(
        mixer_out, "mixer_out",
        (idx, res, carried, share, cand, du, dv, st, nmt, w3, gnm, small_a, small, x, row(gain_mix), grad_mid),
        [shape_of(bf16, 4, 4, rows_m, units // 2), square16, shape_of(f32, 16, width)],
        [pltpu.VMEM((length, width), f32), pltpu.VMEM((lanes, length, 128), f32)],
        smem=2, flops=6 * length * width * units, moved=16 << 20,
    )
    small_got = swap(small, "dp", 1)
    s1, s2, s3, own, small = call(
        add_plane_small, "add_plane_small", (idx, flat(keep), flat(got), small, small_got),
        [shape_of(bf16, 4 * rows_m + 32, width)] * 3 + [shape_of(f32, 4 * rows_m, width), shape_of(bf16, 32, width)], moved=6 << 20,
    )
    got = [swap(v, "dp", 2 * k) for k, v in ((1, s1), (2, s2), (3, s3))]
    s1, s2, s3, own, small = call(
        add_depth_small, "add_depth_small", (idx, own, small, *got),
        [shape_of(bf16, rows_m + 32, width)] * 3 + [shape_of(f32, rows_m, width), shape_of(f32, 16, width)],
        [pltpu.VMEM((4, 16, width), f32)], moved=2 << 20,
    )
    got = [swap(v, "mp", j) for j, v in ((1, s1), (2, s2), (3, s3))]
    part, small = last(add_last_small, "add_last_small", (own, small, *got),
                       [shape_of(bf16, rows_m, width), shape_of(f32, 16, width)])
    near = [part] + [swap(part, "dp", 2 * k) for k in (1, 2, 3)]
    far = [swap(v, "dp", 1) for v in near]
    grad_mix, g_bf, g_bi, g_gain_mix, g_gain_mlp, g_bu = call(
        spread_mix, "spread_mix", (idx, small, *near, *far),
        [shape_of(f32, 3, width // 4, units), shape_of(f32, 1, units // 4), shape_of(f32, 1, units // 4),
         shape_of(f32, 1, width // 4), shape_of(f32, 1, width // 4), shape_of(f32, 1, ff)], moved=3 << 20,
    )
    return (
        mixed[None], grad_tok[None], g_gain_mix[0], grad_mix.transpose(1, 0, 2), g_bf[0], g_bi[0],
        grad_out, g_gain_mlp[0], grad_up, g_bu[0], grad_down,
    )


def solution(mesh):
    return jax.shard_map(
        on_device,
        mesh=mesh,
        in_specs=(P("dp", "mp", None), P(), P(), P(), P(), P(), P(), P(None, "mp"), P("mp"), P("mp", None), P("dp", None), P("dp", "mp", None)),
        out_specs=(P("dp", "mp", None), P("dp", "mp", None), P("mp"), P("mp", None, None), P("mp"), P("mp"), P("mp", None), P("mp"), P(None, "mp"), P("mp"), P("mp", None)),
        check_vma=False,
    )
```

```python
from functools import partial

import jax
import jax.numpy as jnp
from jax import lax
from jax.experimental import pallas as pl
from jax.experimental.pallas import tpu as pltpu
from jax.sharding import PartitionSpec as P

norm_eps = 1e-06
gelu_k = 0.7978845608028654
gelu_c = 0.044715
chunks = 8
f32 = jnp.float32
bf16 = jnp.bfloat16
VMEM = pl.BlockSpec(memory_space=pltpu.VMEM)
SMEM = pl.BlockSpec(memory_space=pltpu.SMEM)
HBM = pl.BlockSpec(memory_space=pltpu.HBM)


weight = {
    "pick_piece": 16, "mixer_in": 32, "join_depth": 8, "block_mid": 16, "join_one": 32, "mlp_one": 8, "join_two": 1,
    "mlp_two": 16, "mid_back": 32, "add_core": 32, "mixer_back": 32, "mixer_out": 16, "add_core_small": 0, "add_cross": 0,
    "mixed_out": 1, "tokens_out": 2, "add_cross_small": 2, "add_depth": 16, "add_depth_small": 32, "add_far": 16,
    "add_far_small": 1, "add_last": 0, "add_last_small": 4, "join_mlp": 2, "join_mix": 32, "spread_mlp": 16, "spread_mix": 8,
}


def dot(a, b):
    return jnp.dot(a, b, preferred_element_type=f32)


def dot_nt(a, b):
    return lax.dot_general(a, b, (((1,), (1,)), ((), ())), preferred_element_type=f32)


def shape_of(dtype, *shape):
    return jax.ShapeDtypeStruct(shape, dtype)


def call(body, name, operands, outs, scratch=(), smem=1, limit=16, after=(), hbm=0):
    n, extra, cost = len(operands), len(after), weight[name]
    operands = [pltpu.with_memory_space_constraint(v, pltpu.HBM) if smem <= i < smem + hbm else v for i, v in enumerate(operands)]

    def run(*refs):
        body(*refs[:n], *refs[n + extra :])

    return pl.pallas_call(
        run,
        out_shape=outs,
        in_specs=[SMEM] * smem + [HBM] * hbm + [VMEM] * (n - smem - hbm) + [pl.BlockSpec(memory_space=pl.ANY)] * extra,
        out_specs=[VMEM] * len(outs),
        scratch_shapes=list(scratch),
        compiler_params=pltpu.CompilerParams(vmem_limit_bytes=limit << 20),
        cost_estimate=pl.CostEstimate(flops=cost << 30, bytes_accessed=cost << 22, transcendentals=0),
        name=name,
    )(*operands, *after)


def to_chunked(src, split, put):
    length, width = src.shape
    steps = length // chunks
    for g in range(width // 128):
        cols = slice(g * 128, (g + 1) * 128)
        split[g] = src[:, cols].astype(f32)
        for s in range(steps):
            put(pl.ds(s * chunks, chunks), cols, split[g, pl.ds(s, chunks, stride=steps), :])


def from_chunked(values, split, out):
    length, width = out.shape
    steps = length // chunks
    for g in range(width // 128):
        cols = slice(g * 128, (g + 1) * 128)
        for s in range(steps):
            split[g, pl.ds(s, chunks, stride=steps), :] = values[s * chunks : (s + 1) * chunks, cols]
        out[:, cols] = split[g].astype(bf16)


def keep_mask(idx, length):
    row = lax.broadcasted_iota(jnp.int32, (length, 1), 0)
    pos = idx[2] * length + (row % chunks) * (length // chunks) + row // chunks
    keep = jnp.ones((length, 1), f32)
    for i in range(3):
        keep = jnp.where(pos == idx[3 + i], 0.0, keep)
    return keep


def fetch(pairs, sems):
    copies = [pltpu.make_async_copy(src, dst, sems.at[i]) for i, (src, dst) in enumerate(pairs)]
    for copy in copies:
        copy.start()
    return copies


def mixer_in(idx, tok_hbm, gain_hbm, bias_f_hbm, bias_i_hbm, b_up_hbm, w_hbm, decay, share, cand, du, dv, nmt, x, prods, ends, payload,
             split, tok, gain, bias_f, bias_i, b_up, w, sems):
    length, width = tok.shape
    units = bias_f.shape[1]
    steps = length // chunks
    block = 256
    pairs = [(tok_hbm, tok), (gain_hbm, gain), (bias_f_hbm, bias_f), (bias_i_hbm, bias_i), (b_up_hbm, b_up)]
    for h in range(0, units, block):
        sl = pl.ds(h, block)
        pairs.append((w_hbm.at[:, :, sl], w.at[:, :, sl]))
    copies = fetch(pairs, sems)
    for copy in copies[:5]:
        copy.wait()

    def put(rows, cols, values):
        x[rows, cols] = values

    to_chunked(tok, split, put)
    v = x[...]
    r = lax.rsqrt(jnp.mean(v * v, axis=-1, keepdims=True) + norm_eps)
    nm = (v * r * gain[...]).astype(bf16)
    nmt[...] = nm.T
    keep = keep_mask(idx, length)
    for i, h in enumerate(range(0, units, block)):
        sl = pl.ds(h, block)
        copies[5 + i].wait()
        a = jnp.exp(jnp.minimum(-(dot(nm, w[0, :, sl]) + bias_f[:, sl]), 88.0))
        b = jnp.exp(jnp.minimum(-(dot(nm, w[1, :, sl]) + bias_i[:, sl]), 88.0))
        t = 1.0 / (2.0 + a + b)
        p = (1.0 + b) * t
        q = (1.0 + a) * t
        decay[:, sl] = p * keep
        share[:, sl] = q
        cand[:, sl] = dot(nm, w[2, :, sl])
        du[:, sl] = p * (a * t)
        dv[:, sl] = q * (b * t)

    def step(s, carry):
        prod, end = carry
        rows = pl.ds(pl.multiple_of(s * chunks, chunks), chunks)
        d = decay[rows, :]
        return prod * d, end * d + share[rows, :] * cand[rows, :]

    prod, end = lax.fori_loop(
        0, steps, step, (jnp.ones((chunks, units), f32), jnp.zeros((chunks, units), f32)), unroll=8
    )
    prods[...] = prod
    ends[...] = end
    total, state = prod[0:1], end[0:1]
    for k in range(1, chunks):
        total = total * prod[k : k + 1]
        state = state * prod[k : k + 1] + end[k : k + 1]
    payload[...] = jnp.zeros_like(payload)
    payload[0:1, :] = total
    payload[1:2, :] = state
    payload[2:3, 0 : b_up.shape[1]] = b_up[...]


def feed_forward(nm, cot, wu, wd, bu):
    pre = dot(nm, wu) + bu
    grad_act = dot_nt(cot, wd)
    sq = pre * pre
    t = jnp.tanh(pre * (gelu_k + gelu_k * gelu_c * sq))
    half = 0.5 + 0.5 * t
    h = pre * half
    slope = half + h * (1.0 - t) * (gelu_k + 3.0 * gelu_k * gelu_c * sq)
    grad_pre = grad_act * slope
    return h.astype(bf16), grad_pre.astype(bf16), jnp.sum(grad_pre, axis=0, keepdims=True)


def store_pieces(ref, base, rows, values):
    for p in range(4):
        ref[p, base : base + rows, :] = values[p * rows : (p + 1) * rows].astype(bf16)


def ffn_block(slot, core, nm, nmt, cot, wu, wd, bu, mix, gn, keep, send, hT):
    h, g, bsum = feed_forward(nm, cot, wu, wd, bu)
    hT[...] = h.T
    half = nm.shape[1] // 2
    for ref, which in ((send, 1 - core), (keep, core)):
        rows = pl.ds(pl.multiple_of(which * half, half), half)
        store_pieces(ref, slot * (half // 2), half // 4, dot(nmt[rows, :], g))
        store_pieces(ref, slot * (half // 2) + half // 4, half // 4, dot(hT[rows, :], cot))
    mix[...] += dot(h, wd)
    gn[...] += dot_nt(g, wu)
    return bsum


def block_mid(idx, own, r1, r2, r3, prods, ends, decay, share, cand, x, cot, w_out, gain, wu, wd, bu,
              st, stT, middle, nm2, nm2t, cotp, mix, gn, bsum, keep, send, split, others, hT, carry8):
    length = x.shape[0]
    steps = length // chunks
    units = decay.shape[1]
    core, z = idx[0], idx[2]
    for j, ref in enumerate((own, r1, r2, r3)):
        others[j] = ref[...]
    state = jnp.zeros((1, units), f32)
    for k in range(4):
        part = others[k ^ z]
        state = jnp.where(k < z, state * part[0:1] + part[1:2], state)
    for k in range(chunks):
        carry8[k : k + 1, :] = state
        state = state * prods[k : k + 1, :] + ends[k : k + 1, :]
    st[0:chunks, :] = carry8[...]

    def step(s, state):
        rows = pl.ds(pl.multiple_of(s * chunks, chunks), chunks)
        state = state * decay[rows, :] + share[rows, :] * cand[rows, :]
        st[pl.ds(pl.multiple_of(s * chunks + chunks, chunks), chunks), :] = state
        return state

    lax.fori_loop(0, steps, step, carry8[...], unroll=8)
    low = st[chunks:, :].astype(bf16)
    stT[...] = low.T
    mid = x[...] + dot(low, w_out[...])
    middle[...] = mid
    r = lax.rsqrt(jnp.mean(mid * mid, axis=-1, keepdims=True) + norm_eps)
    nm = (mid * r * gain[...]).astype(bf16)
    nm2[...] = nm
    nm2t[...] = nm.T

    def put(rows, cols, values):
        gn[rows, cols] = values

    to_chunked(cot, split, put)
    cotp[...] = gn[...].astype(bf16)
    gn[...] = jnp.zeros_like(gn)
    mix[...] = mid
    bsum[...] = ffn_block(0, core, nm, nm2t, cotp[...], wu[...], wd[...], bu[...], mix, gn, keep, send, hT)


def lay_out(idx, near, far, at, wu, wd):
    rows = wu.shape[0] // 8
    for which, pieces in ((idx[0], near), (1 - idx[0], far)):
        for k in range(4):
            spot = pl.ds(pl.multiple_of((which * 4 + (idx[1] ^ k)) * rows, rows), rows)
            wu[spot, :] = pieces[k, at : at + rows, :]
            wd[spot, :] = pieces[k, at + rows : at + 2 * rows, :]


def mlp_one(idx, near, far, bias, mix0, gn0, bsum0, nm2, nm2t, cotp, keep0, send0,
            mix, gn, keep, send, small, hT, wu, wd):
    z = idx[2]
    block = keep0.shape[1]
    mix[...] = mix0[...]
    gn[...] = gn0[...]
    keep[:, 0:block, :] = keep0[...]
    send[:, 0:block, :] = send0[...]
    small[...] = jnp.zeros_like(small)
    small[pl.ds(4 * z + 2, 1), :] = bsum0[...]
    lay_out(idx, near, far, 0, wu, wd)
    small[pl.ds(4 * (z ^ 1) + 2, 1), :] = ffn_block(
        1, idx[0], nm2[...], nm2t, cotp[...], wu[...], wd[...], bias[2:3, 0 : wu.shape[1]], mix, gn, keep, send, hT
    )


def mlp_two(idx, near, far, bias2, bias3, mix0, gn0, small0, nm2, nm2t, cotp, mix, gn, keep, send, small, hT, wu, wd):
    mix[...] = mix0[...]
    gn[...] = gn0[...]
    small[...] = small0[...]
    for slot, bias in enumerate((bias2, bias3)):
        lay_out(idx, near, far, slot * wu.shape[0] // 4, wu, wd)
        small[pl.ds(4 * (idx[2] ^ (2 + slot)) + 2, 1), :] = ffn_block(
            slot, idx[0], nm2[...], nm2t, cotp[...], wu[...], wd[...], bias[2:3, 0 : wu.shape[1]], mix, gn, keep, send, hT
        )


def mid_back(idx, gn, cotp, middle, gain, stT, w_out, decay,
             keep, send, grad_mid, grad_states, payload, prods, flows, gain_row):
    core, z = idx[0], idx[2]
    length, units = decay.shape
    steps = length // chunks
    mid = middle[...]
    r = lax.rsqrt(jnp.mean(mid * mid, axis=-1, keepdims=True) + norm_eps)
    scaled = mid * r
    g = gn[...]
    gain_row[...] = jnp.sum(g * scaled, axis=0, keepdims=True)
    gg = g * gain[...]
    gm = cotp[...].astype(f32) + r * (gg - scaled * jnp.mean(gg * scaled, axis=-1, keepdims=True))
    grad_mid[...] = gm
    low = gm.astype(bf16)
    grad_states[...] = dot_nt(low, w_out[...])
    part = units // 8
    for k in range(4):
        for ref, which in ((send, 1 - core), (keep, core)):
            got = dot(stT[pl.ds(pl.multiple_of((2 * k + which) * part, part), part), :], low)
            at = pl.ds(pl.multiple_of((k ^ z) * (part // 4), part // 4), part // 4)
            for p in range(4):
                ref[p, at, :] = got[p * (part // 4) : (p + 1) * (part // 4)].astype(bf16)

    def step(i, carry):
        prod, flow = carry
        rows = pl.ds(pl.multiple_of((steps - 1 - i) * chunks, chunks), chunks)
        d = decay[rows, :]
        return prod * d, (flow + grad_states[rows, :]) * d

    prod, flow = lax.fori_loop(
        0, steps, step, (jnp.ones((chunks, units), f32), jnp.zeros((chunks, units), f32)), unroll=8
    )
    total, out = prod[chunks - 1 :], flow[chunks - 1 :]
    for k in range(chunks - 2, -1, -1):
        total = total * prod[k : k + 1]
        out = out * prod[k : k + 1] + flow[k : k + 1]
    payload[0:1, :] = total
    payload[1:2, :] = out
    prods[...] = prod
    flows[...] = flow


def mixed_out(mix, mixed, done, split):
    from_chunked(mix, split, mixed)
    done[...] = jnp.zeros_like(done)


def gate_grads(which, keep, carried, st, share, cand, du, dv, w, nmt, z, out, gnm, small):
    length, units = carried.shape
    half = units // 2
    cols = pl.ds(pl.multiple_of(which * half, half), half)
    cf = carried[:, cols]
    q = share[:, cols]
    s = cf * (st[0:length, cols] * keep - cand[:, cols])
    ga = s * du[:, cols]
    gb = -(s * dv[:, cols])
    quarter = half // 2
    sum_a, sum_b = jnp.sum(ga, axis=0, keepdims=True), jnp.sum(gb, axis=0, keepdims=True)
    for i in range(2):
        at = pl.ds(4 * (2 * which + i), 1)
        small[at, 0:quarter] = sum_a[:, i * quarter : (i + 1) * quarter]
        small[at, quarter:] = sum_b[:, i * quarter : (i + 1) * quarter]
    part = nmt.shape[0] // 4
    for k, g in enumerate((ga, gb, cf * q)):
        low = g.astype(bf16)
        got = dot(nmt[...], low)
        for zz in range(4):
            for p in range(4):
                top = zz * part + p * (part // 4)
                out[p, zz ^ z, k * (part // 4) : (k + 1) * (part // 4), :] = got[top : top + part // 4].astype(bf16)
        gnm[...] += dot_nt(low, w[k, :, cols])


def mixer_back(idx, own, r1, r2, r3, prods, flows, decay, share, cand, du, dv, st, grad_states, nmt, w,
               carried, send, gnm, small, others, carry8):
    length, units = decay.shape
    steps = length // chunks
    core, z = idx[0], idx[2]
    for j, ref in enumerate((own, r1, r2, r3)):
        others[j] = ref[...]
    flow = jnp.zeros((1, units), f32)
    for k in range(3, -1, -1):
        part = others[k ^ z]
        flow = jnp.where(k > z, flow * part[0:1] + part[1:2], flow)
    for k in range(chunks - 1, -1, -1):
        carry8[k : k + 1, :] = flow
        flow = flow * prods[k : k + 1, :] + flows[k : k + 1, :]

    def step(i, flow):
        rows = pl.ds(pl.multiple_of((steps - 1 - i) * chunks, chunks), chunks)
        got = grad_states[rows, :] + flow
        carried[rows, :] = got
        return got * decay[rows, :]

    lax.fori_loop(0, steps, step, carry8[...], unroll=8)
    gnm[...] = jnp.zeros_like(gnm)
    small[...] = jnp.zeros_like(small)
    gate_grads(1 - core, keep_mask(idx, length), carried, st, share, cand, du, dv, w, nmt, z, send, gnm, small)


def mixer_out(idx, carried, share, cand, du, dv, st, nmt, w, gnm0, small0, small1, gain_row, x,
              keep, gnm, small):
    length, units = carried.shape
    core, z = idx[0], idx[2]
    gnm[...] = gnm0[...]
    small[...] = small0[...] + small1[...]
    gate_grads(core, keep_mask(idx, length), carried, st, share, cand, du, dv, w, nmt, z, keep, gnm, small)
    v = x[...]
    r = lax.rsqrt(jnp.mean(v * v, axis=-1, keepdims=True) + norm_eps)
    gains = jnp.sum(gnm[...] * (v * r), axis=0, keepdims=True)
    n = gains.shape[1] // 4
    for k in range(4):
        small[4 * k + 1 : 4 * k + 2, 0:n] = gains[:, k * n : (k + 1) * n]
        small[4 * k + 1 : 4 * k + 2, n : 2 * n] = gain_row[:, k * n : (k + 1) * n]


def tokens_out(gnm, x, gain, grad_mid, grad_tok, done, total, split):
    v = x[...]
    r = lax.rsqrt(jnp.mean(v * v, axis=-1, keepdims=True) + norm_eps)
    scaled = v * r
    gg = gnm[...] * gain[...]
    total[...] = grad_mid[...] + r * (gg - scaled * jnp.mean(gg * scaled, axis=-1, keepdims=True))
    from_chunked(total, split, grad_tok)
    done[...] = jnp.zeros_like(done)


def pick_piece(idx, wu, wd, out, sems):
    rows = wu.shape[0] // 8
    at = pl.ds(pl.multiple_of((idx[0] * 4 + idx[1]) * rows, rows), rows)
    for copy in fetch([(wu.at[at, :], out.at[pl.ds(0, rows), :]), (wd.at[at, :], out.at[pl.ds(rows, rows), :])], sems):
        copy.wait()


def gate(value, after):
    any_space = pl.BlockSpec(memory_space=pl.ANY)
    return pl.pallas_call(
        lambda *refs: None,
        out_shape=jax.ShapeDtypeStruct(value.shape, value.dtype),
        in_specs=[any_space, any_space],
        out_specs=any_space,
        input_output_aliases={0: 0},
        compiler_params=pltpu.CompilerParams(vmem_limit_bytes=1 << 20),
        name="gate",
    )(value, after)


def join(*refs):
    out, rows = refs[-1], refs[0].shape[0]
    for k, ref in enumerate(refs[:-1]):
        if len(out.shape) == 3:
            out[k] = ref[...]
        else:
            out[k * rows : (k + 1) * rows, :] = ref[...]


def two_terms(v):
    high = v.astype(bf16)
    return high, (v - high.astype(f32)).astype(bf16)


def add_core(idx, keep_a, got_a, keep_b, got_b, keep_c, got_c, send_x, send_y, own_x, own_y):
    x, y = idx[1] % 2, idx[1] // 2
    half = send_x.shape[1]

    def put(ref, k, p, first):
        top = 0
        for keep, got in ((keep_a, got_a), (keep_b, got_b), (keep_c, got_c)):
            low, high = max(first, top), min(first + half, top + keep.shape[1])
            if low < high:
                rows = slice(low - top, high - top)
                ref[k, low - first : high - first, :] = (
                    keep[p, rows, :].astype(f32) + got[p, rows, :].astype(f32)
                ).astype(ref.dtype)
            top += keep.shape[1]

    for k in range(2):
        put(send_x, k, 2 * k + 1 - x, 0)
        put(own_x, k, 2 * k + x, 0)
        put(send_y, k, 2 * (1 - y) + k, half)
        put(own_y, k, 2 * y + k, half)


def add_cross(idx, own_x, got_x, own_y, got_y, send_y, send_x, out_x, out_y):
    x, y = idx[1] % 2, idx[1] // 2
    send_y[...] = (own_x[1 - y] + got_x[1 - y].astype(f32)).astype(bf16)
    out_x[...] = own_x[y] + got_x[y].astype(f32)
    send_x[...] = (own_y[1 - x] + got_y[1 - x].astype(f32)).astype(bf16)
    out_y[...] = own_y[x] + got_y[x].astype(f32)


def add_depth(own_x, got_x, own_y, got_y, send, own, total):
    rows = send.shape[0] // 2
    part = rows // 5
    block = 4 * part
    half = own_x.shape[0]
    total[0:half, :] = own_x[...] + got_x[...].astype(f32)
    total[half:, :] = own_y[...] + got_y[...].astype(f32)
    for j, ref, base in ((1, send, 0), (2, own, rows), (3, send, rows), (0, own, 0)):
        at = j * block
        ref[base : base + block, :] = total[at : at + block, :].astype(ref.dtype)
        at = 4 * block + j * part
        ref[base + block : base + rows, :] = total[at : at + part, :].astype(ref.dtype)


def add_far(own, got, send, out):
    rows = out.shape[0]
    out[...] = own[0:rows, :] + got[0:rows, :].astype(f32)
    send[...] = (own[rows:, :] + got[rows:, :].astype(f32)).astype(bf16)


def add_last(own, got, out):
    out[...] = (own[...] + got[...].astype(f32)).astype(out.dtype)


def add_core_small(idx, keep, got, small, send_x, send_y, own_x, own_y, tiny):
    x, y = idx[1] % 2, idx[1] // 2
    half, n = own_x.shape[1], small.shape[0]
    high, low = two_terms(small[...])
    tiny[0:n, :] = high
    tiny[n:, :] = low
    send_x[2 * half : 2 * half + n, :] = high
    send_x[2 * half + n :, :] = low
    for k in range(2):
        at = slice(k * half, (k + 1) * half)
        p = 2 * k + 1 - x
        send_x[at, :] = (keep[p, 0:half, :].astype(f32) + got[p, 0:half, :].astype(f32)).astype(bf16)
        p = 2 * k + x
        own_x[k] = keep[p, 0:half, :].astype(f32) + got[p, 0:half, :].astype(f32)
        p = 2 * (1 - y) + k
        send_y[at, :] = (keep[p, half:, :].astype(f32) + got[p, half:, :].astype(f32)).astype(bf16)
        p = 2 * y + k
        own_y[k] = keep[p, half:, :].astype(f32) + got[p, half:, :].astype(f32)


def add_tiny(tiny, got, at):
    n = tiny.shape[0] // 2
    return (tiny[0:n, :].astype(f32) + tiny[n:, :].astype(f32)) + (
        got[at : at + n, :].astype(f32) + got[at + n : at + 2 * n, :].astype(f32)
    )


def add_cross_small(idx, own_x, got_x, own_y, got_y, tiny, send_y, send_x, out_x, out_y, tiny_out):
    x, y = idx[1] % 2, idx[1] // 2
    half, n = out_x.shape[0], tiny.shape[0] // 2
    high, low = two_terms(add_tiny(tiny, got_x, 2 * half))
    tiny_out[0:n, :] = high
    tiny_out[n:, :] = low
    send_y[half : half + n, :] = high
    send_y[half + n :, :] = low
    side = pl.ds(pl.multiple_of((1 - y) * half, half), half)
    send_y[0:half, :] = (own_x[1 - y] + got_x[side, :].astype(f32)).astype(bf16)
    side = pl.ds(pl.multiple_of(y * half, half), half)
    out_x[...] = own_x[y] + got_x[side, :].astype(f32)
    side = pl.ds(pl.multiple_of((1 - x) * half, half), half)
    send_x[...] = (own_y[1 - x] + got_y[side, :].astype(f32)).astype(bf16)
    side = pl.ds(pl.multiple_of(x * half, half), half)
    out_y[...] = own_y[x] + got_y[side, :].astype(f32)


def add_depth_small(idx, own_x, got_x, own_y, got_y, tiny, send, own, small):
    half, z = own_x.shape[0], idx[2]
    rows = half // 2
    total = add_tiny(tiny, got_x, half)
    n = total.shape[0] // 4
    small[...] = jnp.zeros_like(small)
    for k in range(4):
        small[k, 0:n, :] = total[k * n : (k + 1) * n]
    for j in range(4):
        own_ref, got = ((own_x, got_x), (own_y, got_y))[j // 2]
        at = slice((j % 2) * rows, (j % 2 + 1) * rows)
        value = own_ref[at, :] + got[at, :].astype(f32)
        base = (j // 2) * (rows + 16)
        if j % 2:
            send[base : base + rows, :] = value.astype(bf16)
            high, low = two_terms(small[z ^ j])
            send[base + rows : base + rows + 16, :] = jnp.concatenate([high, low], axis=0)
        else:
            own[(j // 2) * rows : (j // 2 + 1) * rows, :] = value


def add_far_small(idx, own, got, small, send, out, tiny_out):
    z = idx[2]
    rows, n = out.shape[0], tiny_out.shape[0]
    tiny = []
    for k in range(2):
        base = k * (rows + 16)
        mine = small[z ^ (2 * k)]
        other = got[base + rows : base + rows + 16, :].astype(f32)
        tiny.append(mine + (other[0:n] + other[n : 2 * n]))
    out[...] = own[0:rows, :] + got[0:rows, :].astype(f32)
    tiny_out[...] = tiny[0]
    send[0:rows, :] = (own[rows:, :] + got[rows + 16 : 2 * rows + 16, :].astype(f32)).astype(bf16)
    high, low = two_terms(tiny[1])
    send[rows:, :] = jnp.concatenate([high, low], axis=0)


def add_last_small(own, tiny, got, out, tiny_out):
    rows, n = own.shape[0], tiny.shape[0]
    out[...] = (own[...] + got[0:rows, :].astype(f32)).astype(out.dtype)
    other = got[rows:, :].astype(f32)
    tiny_out[...] = tiny[...] + (other[0:n] + other[n : 2 * n])


def spread_mlp(idx, near, far, up, down, w_out, done):
    rows = up.shape[0] // 8
    rows_out = w_out.shape[0] // 8
    for which, pieces in ((idx[0], near), (1 - idx[0], far)):
        for k in range(4):
            spot = which * 4 + (idx[1] ^ k)
            at = pl.ds(pl.multiple_of(spot * rows, rows), rows)
            up[at, :] = pieces[k, 0:rows, :].astype(f32)
            down[at, :] = pieces[k, rows : 2 * rows, :].astype(f32)
            w_out[pl.ds(pl.multiple_of(spot * rows_out, rows_out), rows_out), :] = pieces[k, 2 * rows :, :].astype(f32)
    done[...] = jnp.zeros_like(done)


def spread_mix(idx, tiny, tiny_far, near, far, out, bias_f, bias_i, gain_mix, gain_mlp, b_up):
    rows, half = out.shape[1] // 4, out.shape[2] // 2
    for which, pieces in ((idx[0], near), (1 - idx[0], far)):
        cols = pl.ds(pl.multiple_of(which * half, half), half)
        for k in range(4):
            at = pl.ds(pl.multiple_of((idx[1] ^ k) * rows, rows), rows)
            for i in range(3):
                out[i, at, cols] = pieces[k, i * rows : (i + 1) * rows, :].astype(f32)
    small = tiny[...] + tiny_far[...]
    n = bias_f.shape[1]
    bias_f[...] = small[0:1, 0:n]
    bias_i[...] = small[0:1, n:]
    n = gain_mix.shape[1]
    gain_mix[...] = small[1:2, 0:n]
    gain_mlp[...] = small[1:2, n : 2 * n]
    b_up[...] = small[2:3, :]


def swap(value, axis, bit):
    size = lax.axis_size(axis)
    return lax.ppermute(value, axis, [(i, i ^ bit) for i in range(size)])


def on_device(tokens, gain_mix, w_mix, bias_forget, bias_input, w_out, gain_mlp, w_up, b_up, w_down, resets, cotangent):
    length, width = tokens.shape[1:]
    units = w_out.shape[0]
    ff = w_up.shape[1]
    dp, mp = lax.axis_size("dp"), lax.axis_size("mp")
    assert mp == 4 and dp % 8 == 0 and tokens.shape[0] == 1
    place = lax.axis_index("dp")
    here = jnp.stack([place & 1, (place >> 1) & 3, lax.axis_index("mp")]).astype(jnp.int32)
    idx = jnp.concatenate([here, resets[0]])
    tok, cot = tokens[0], cotangent[0]
    w3 = w_mix.transpose(1, 0, 2)
    row = lambda v: v.reshape(1, -1)
    lanes = width // 128

    (piece,) = call(pick_piece, "pick_piece", (idx, w_up, w_down), [shape_of(bf16, width // 4, ff)],
                    [pltpu.SemaphoreType.DMA((2,))], hbm=2, limit=2)
    depth = [swap(piece, "mp", j) for j in (1, 2, 3)]

    wide = shape_of(f32, length, units)
    square = shape_of(f32, length, width)
    square16 = shape_of(bf16, length, width)
    edge = shape_of(f32, chunks, units)
    decay, share, cand, du, dv, nmt, x, prods, ends, payload = call(
        mixer_in, "mixer_in",
        (idx, tok, row(gain_mix), row(bias_forget), row(bias_input), row(b_up), w3),
        [wide] * 5 + [shape_of(bf16, width, length), square, edge, edge, shape_of(f32, 4, units)],
        [pltpu.VMEM((lanes, length, 128), f32), pltpu.VMEM((length, width), bf16), pltpu.VMEM((1, width), f32)]
        + [pltpu.VMEM((1, units), f32)] * 2 + [pltpu.VMEM((1, ff), f32), pltpu.VMEM((3, width, units), bf16),
                                              pltpu.SemaphoreType.DMA((5 + units // 256,))],
        hbm=6, after=(piece,),
    )
    ahead = [swap(payload, "mp", j) for j in (1, 2, 3)]
    around = lambda v: [v] + [swap(v, "dp", 2 * k) for k in (1, 2, 3)]
    near_one = around(gate(depth[0], payload))
    (pair,) = call(join, "join_depth", depth[1:], [shape_of(bf16, width // 2, ff)], smem=0, after=(payload,))
    near_two = around(pair)
    (near_one,) = call(join, "join_one", near_one, [shape_of(bf16, 4, width // 4, ff)], smem=0)
    far_one = swap(near_one, "dp", 1)
    quarter = width // 8
    st, stT, middle, nm2, nm2t, cotp, mix, gn, bsum, keep0, send0 = call(
        block_mid, "block_mid",
        (idx, payload, *ahead, prods, ends, decay, share, cand, x, cot, w_out, row(gain_mlp), w_up, w_down, row(b_up)),
        [shape_of(f32, length + chunks, units), shape_of(bf16, units, length), square, square16, shape_of(bf16, width, length),
         square16, square, square, shape_of(f32, 1, ff)] + [shape_of(bf16, 4, 2 * quarter, width)] * 2,
        [pltpu.VMEM((lanes, length, 128), f32), pltpu.VMEM((4, 4, units), f32), pltpu.VMEM((ff, length), bf16),
         pltpu.VMEM((chunks, units), f32)], after=(pair,),
    )
    block = 2 * quarter
    pair = lambda dtype, rows: shape_of(dtype, 2, rows, width)
    weights = [pltpu.VMEM((ff, length), bf16), pltpu.VMEM((width, ff), bf16), pltpu.VMEM((ff, width), bf16)]
    mix, gn, keep_a, send_a, small_mlp = call(
        mlp_one, "mlp_one",
        (idx, near_one, far_one, ahead[0], mix, gn, bsum, nm2, nm2t, cotp, keep0, send0),
        [square] * 2 + [shape_of(bf16, 4, 2 * block, width)] * 2 + [shape_of(f32, 16, width)], weights,
    )
    (near_two,) = call(join, "join_two", near_two, [shape_of(bf16, 4, width // 2, ff)], smem=0, after=(gn,))
    mix, gn, keep, send, small_mlp = call(
        mlp_two, "mlp_two",
        (idx, near_two, swap(near_two, "dp", 1), ahead[1], ahead[2], mix, gn, small_mlp, nm2, nm2t, cotp),
        [square] * 2 + [shape_of(bf16, 4, 2 * block, width)] * 2 + [shape_of(f32, 16, width)], weights,
    )
    got_a, got = swap(send_a, "dp", 1), swap(send, "dp", 1)
    out_rows = units // 8
    keep_out, send_out, grad_mid, grad_states, payload, prods, flows, gain_row = call(
        mid_back, "mid_back",
        (idx, gn, cotp, middle, row(gain_mlp), stT, w_out, decay),
        [shape_of(bf16, 4, out_rows, width)] * 2 + [square, wide, shape_of(f32, 2, units), edge, edge, shape_of(f32, 1, width)],
    )
    behind = [swap(payload, "mp", j) for j in (1, 2, 3)]

    half = (4 * block + out_rows) // 2
    send_x, send_y, own_x, own_y = call(add_core, "add_core", (idx, keep_a, got_a, keep, got, keep_out, swap(send_out, "dp", 1)),
                                        [pair(bf16, half)] * 2 + [pair(f32, half)] * 2)
    got_x, got_y = swap(send_x, "dp", 2), swap(send_y, "dp", 4)

    rows_m = 3 * width // 16
    carried, send, gnm, small = call(
        mixer_back, "mixer_back",
        (idx, payload, *behind, prods, flows, decay, share, cand, du, dv, st, grad_states, nmt, w3),
        [wide, shape_of(bf16, 4, 4, rows_m, units // 2), square, shape_of(f32, 16, width)],
        [pltpu.VMEM((4, 2, units), f32), pltpu.VMEM((chunks, units), f32)], after=(own_x,),
    )
    flat = lambda v: v.reshape(4, -1, width)
    got = swap(send, "dp", 1)
    keep, gnm, small = call(
        mixer_out, "mixer_out",
        (idx, carried, share, cand, du, dv, st, nmt, w3, gnm, small, small_mlp, gain_row, x),
        [shape_of(bf16, 4, 4, rows_m, units // 2), square, shape_of(f32, 16, width)],
    )
    half_m = 2 * rows_m
    one = lambda dtype, rows: shape_of(dtype, rows, width)
    send_mx, send_my, own_mx, own_my, tiny = call(
        add_core_small, "add_core_small", (idx, flat(keep), flat(got), small),
        [one(bf16, 2 * half_m + 32), one(bf16, 2 * half_m), pair(f32, half_m), pair(f32, half_m), one(bf16, 32)],
    )
    got_mx, got_my = swap(send_mx, "dp", 2), swap(send_my, "dp", 4)
    mark = shape_of(f32, 8, 128)
    grad_tok, done_tok = call(tokens_out, "tokens_out", (gnm, x, row(gain_mix), grad_mid), [square16, mark],
                       [pltpu.VMEM((length, width), f32), pltpu.VMEM((lanes, length, 128), f32)], smem=0, after=(own_mx,))
    mixed, done_mix = call(mixed_out, "mixed_out", (mix,), [square16, mark], [pltpu.VMEM((lanes, length, 128), f32)], smem=0, after=(own_mx,))

    send_y, send_x, own_x, own_y = call(add_cross, "add_cross", (idx, own_x, got_x, own_y, got_y),
                                        [one(bf16, half)] * 2 + [one(f32, half)] * 2, after=(own_mx,))
    got_x, got_y = swap(send_y, "dp", 4), swap(send_x, "dp", 2)
    send_my, send_mx, own_mx, own_my, tiny = call(
        add_cross_small, "add_cross_small", (idx, own_mx, got_mx, own_my, got_my, tiny),
        [one(bf16, half_m + 32), one(bf16, half_m), one(f32, half_m), one(f32, half_m), one(bf16, 32)],
        after=(own_x, done_mix, done_tok),
    )
    got_mx, got_my = swap(send_my, "dp", 4), swap(send_mx, "dp", 2)
    rows_f = block + units // 32
    send, own = call(add_depth, "add_depth", (own_x, got_x, own_y, got_y), [one(bf16, 2 * rows_f), one(f32, 2 * rows_f)],
                     [pltpu.VMEM((2 * half, width), f32)], smem=0, after=(own_mx,))
    got = swap(send, "mp", 1)
    send_m, own_m, small = call(
        add_depth_small, "add_depth_small", (idx, own_mx, got_mx, own_my, got_my, tiny),
        [one(bf16, 2 * rows_m + 32), one(f32, 2 * rows_m), shape_of(f32, 4, 8, width)], after=(own,),
    )
    got_m = swap(send_m, "mp", 1)
    send, own = call(add_far, "add_far", (own, got), [one(bf16, rows_f), one(f32, rows_f)], smem=0, after=(small,))
    got = swap(send, "mp", 2)
    send_m, own_m, tiny = call(
        add_far_small, "add_far_small", (idx, own_m, got_m, small),
        [one(bf16, rows_m + 16), one(f32, rows_m), one(f32, 8)], after=(own,),
    )
    got_m = swap(send_m, "mp", 2)
    across = [[g * 8 + i for g in range(dp // 8)] for i in range(8)]

    def last(fn, name, operands, outs, after):
        if dp == 8:
            return call(fn, name, operands, outs, smem=0, after=after)
        done = call(fn, name, operands, [shape_of(f32, *o.shape) for o in outs], smem=0, after=after)
        return [lax.psum(v, "dp", axis_index_groups=across).astype(o.dtype) for v, o in zip(done, outs)]

    (part,) = last(add_last, "add_last", (own, got), [one(bf16, rows_f)], (tiny,))
    near_f = around(part)
    part, tiny = last(add_last_small, "add_last_small", (own_m, tiny, got_m), [one(bf16, rows_m), one(f32, 8)], (part,))
    near_m = around(part)
    (near,) = call(join, "join_mlp", near_f, [shape_of(bf16, 4, rows_f, width)], smem=0, after=(part,))
    grad_up, grad_down, grad_out, done = call(
        spread_mlp, "spread_mlp", (idx, near, swap(near, "dp", 1)),
        [shape_of(f32, width, ff), shape_of(f32, ff, width), shape_of(f32, units // 4, width), mark],
    )
    (near,) = call(join, "join_mix", near_m, [shape_of(bf16, 4, rows_m, width)], smem=0)
    grad_mix, g_bf, g_bi, g_gain_mix, g_gain_mlp, g_bu = call(
        spread_mix, "spread_mix", (idx, tiny, swap(tiny, "dp", 1), near, swap(near, "dp", 1)),
        [shape_of(f32, 3, width // 4, units), shape_of(f32, 1, units // 4), shape_of(f32, 1, units // 4),
         shape_of(f32, 1, width // 4), shape_of(f32, 1, width // 4), shape_of(f32, 1, ff)],
        after=(done,),
    )
    return (
        mixed[None], grad_tok[None], g_gain_mix[0], grad_mix.transpose(1, 0, 2), g_bf[0], g_bi[0],
        grad_out, g_gain_mlp[0], grad_up, g_bu[0], grad_down,
    )


def solution(mesh):
    return jax.shard_map(
        on_device,
        mesh=mesh,
        in_specs=(P("dp", "mp", None), P(), P(), P(), P(), P(), P(), P(None, "mp"), P("mp"), P("mp", None), P("dp", None), P("dp", "mp", None)),
        out_specs=(P("dp", "mp", None), P("dp", "mp", None), P("mp"), P("mp", None, None), P("mp"), P("mp"), P("mp", None), P("mp"), P(None, "mp"), P("mp"), P("mp", None)),
        check_vma=False,
    )
```

```python
from functools import partial

import jax
import jax.numpy as jnp
from jax import lax
from jax.experimental import pallas as pl
from jax.experimental.pallas import tpu as pltpu
from jax.sharding import PartitionSpec as P

norm_eps = 1e-06
gelu_k = 0.7978845608028654
gelu_c = 0.044715
chunks = 8
f32 = jnp.float32
bf16 = jnp.bfloat16
VMEM = pl.BlockSpec(memory_space=pltpu.VMEM)
SMEM = pl.BlockSpec(memory_space=pltpu.SMEM)
HBM = pl.BlockSpec(memory_space=pltpu.HBM)


weight = {
    "pick_piece": 4, "mixer_in": 0, "join_depth": 16, "join_one": 0, "mlp_one": 0, "join_two": 0, "mlp_two": 32, "mid_back": 32,
    "add_core": 32, "mixer_back": 0, "mixer_out": 16, "add_core_small": 4, "add_cross": 0, "mixed_out": 0, "tokens_out": 2,
    "add_cross_small": 0, "add_depth": 0, "add_depth_small": 8, "add_far": 2, "add_far_small": 16, "add_last": 4,
    "add_last_small": 4, "join_mlp": 2, "join_mix": 16, "spread_mlp": 8, "spread_mix": 8, "add_pair": 2, "mid_in": 0,
    "mlp_own": 16,
}


def dot(a, b):
    return jnp.dot(a, b, preferred_element_type=f32)


def dot_nt(a, b):
    return lax.dot_general(a, b, (((1,), (1,)), ((), ())), preferred_element_type=f32)


def shape_of(dtype, *shape):
    return jax.ShapeDtypeStruct(shape, dtype)


def call(body, name, operands, outs, scratch=(), smem=1, limit=16, after=(), hbm=0):
    n, extra, cost = len(operands), len(after), weight[name]
    operands = [pltpu.with_memory_space_constraint(v, pltpu.HBM) if smem <= i < smem + hbm else v for i, v in enumerate(operands)]

    def run(*refs):
        body(*refs[:n], *refs[n + extra :])

    return pl.pallas_call(
        run,
        out_shape=outs,
        in_specs=[SMEM] * smem + [HBM] * hbm + [VMEM] * (n - smem - hbm) + [pl.BlockSpec(memory_space=pl.ANY)] * extra,
        out_specs=[VMEM] * len(outs),
        scratch_shapes=list(scratch),
        compiler_params=pltpu.CompilerParams(vmem_limit_bytes=limit << 20),
        cost_estimate=pl.CostEstimate(flops=cost << 30, bytes_accessed=cost << 22, transcendentals=0),
        name=name,
    )(*operands, *after)


def to_chunked(src, split, put):
    length, width = src.shape
    steps = length // chunks
    for g in range(width // 128):
        cols = slice(g * 128, (g + 1) * 128)
        split[g] = src[:, cols].astype(f32)
        for s in range(steps):
            put(pl.ds(s * chunks, chunks), cols, split[g, pl.ds(s, chunks, stride=steps), :])


def from_chunked(values, split, out):
    length, width = out.shape
    steps = length // chunks
    for g in range(width // 128):
        cols = slice(g * 128, (g + 1) * 128)
        for s in range(steps):
            split[g, pl.ds(s, chunks, stride=steps), :] = values[s * chunks : (s + 1) * chunks, cols]
        out[:, cols] = split[g].astype(bf16)


def keep_mask(idx, length):
    row = lax.broadcasted_iota(jnp.int32, (length, 1), 0)
    pos = idx[2] * length + (row % chunks) * (length // chunks) + row // chunks
    keep = jnp.ones((length, 1), f32)
    for i in range(3):
        keep = jnp.where(pos == idx[3 + i], 0.0, keep)
    return keep


def fetch(pairs, sems):
    copies = [pltpu.make_async_copy(src, dst, sems.at[i]) for i, (src, dst) in enumerate(pairs)]
    for copy in copies:
        copy.start()
    return copies


def mixer_in(idx, tok_hbm, gain_hbm, bias_f_hbm, bias_i_hbm, b_up_hbm, w_hbm, decay, share, cand, du, dv, nmt, x, prods, ends, payload,
             split, tok, gain, bias_f, bias_i, b_up, w, sems):
    length, width = tok.shape
    units = bias_f.shape[1]
    steps = length // chunks
    block = 256
    pairs = [(tok_hbm, tok), (gain_hbm, gain), (bias_f_hbm, bias_f), (bias_i_hbm, bias_i), (b_up_hbm, b_up)]
    for h in range(0, units, block):
        sl = pl.ds(h, block)
        pairs.append((w_hbm.at[:, :, sl], w.at[:, :, sl]))
    copies = fetch(pairs, sems)
    for copy in copies[:5]:
        copy.wait()

    def put(rows, cols, values):
        x[rows, cols] = values

    to_chunked(tok, split, put)
    v = x[...]
    r = lax.rsqrt(jnp.mean(v * v, axis=-1, keepdims=True) + norm_eps)
    nm = (v * r * gain[...]).astype(bf16)
    nmt[...] = nm.T
    keep = keep_mask(idx, length)
    for i, h in enumerate(range(0, units, block)):
        sl = pl.ds(h, block)
        copies[5 + i].wait()
        a = jnp.exp(jnp.minimum(-(dot(nm, w[0, :, sl]) + bias_f[:, sl]), 88.0))
        b = jnp.exp(jnp.minimum(-(dot(nm, w[1, :, sl]) + bias_i[:, sl]), 88.0))
        t = 1.0 / (2.0 + a + b)
        p = (1.0 + b) * t
        q = (1.0 + a) * t
        decay[:, sl] = p * keep
        share[:, sl] = q
        cand[:, sl] = dot(nm, w[2, :, sl])
        du[:, sl] = p * (a * t)
        dv[:, sl] = q * (b * t)

    def step(s, carry):
        prod, end = carry
        rows = pl.ds(pl.multiple_of(s * chunks, chunks), chunks)
        d = decay[rows, :]
        return prod * d, end * d + share[rows, :] * cand[rows, :]

    prod, end = lax.fori_loop(
        0, steps, step, (jnp.ones((chunks, units), f32), jnp.zeros((chunks, units), f32)), unroll=8
    )
    prods[...] = prod
    ends[...] = end
    total, state = prod[0:1], end[0:1]
    for k in range(1, chunks):
        total = total * prod[k : k + 1]
        state = state * prod[k : k + 1] + end[k : k + 1]
    payload[...] = jnp.zeros_like(payload)
    payload[0:1, :] = total
    payload[1:2, :] = state
    payload[2:3, 0 : b_up.shape[1]] = b_up[...]


def feed_forward(nm, cot, wu, wd, bu):
    pre = dot(nm, wu) + bu
    grad_act = dot_nt(cot, wd)
    sq = pre * pre
    t = jnp.tanh(pre * (gelu_k + gelu_k * gelu_c * sq))
    half = 0.5 + 0.5 * t
    h = pre * half
    slope = half + h * (1.0 - t) * (gelu_k + 3.0 * gelu_k * gelu_c * sq)
    grad_pre = grad_act * slope
    return h.astype(bf16), grad_pre.astype(bf16), jnp.sum(grad_pre, axis=0, keepdims=True)


def store_pieces(ref, base, rows, values):
    for p in range(4):
        ref[p, base : base + rows, :] = values[p * rows : (p + 1) * rows].astype(bf16)


def ffn_block(slot, core, nm, nmt, cot, wu, wd, bu, mix, gn, keep, send, hT):
    h, g, bsum = feed_forward(nm, cot, wu, wd, bu)
    hT[...] = h.T
    half = nm.shape[1] // 2
    for ref, which in ((send, 1 - core), (keep, core)):
        rows = pl.ds(pl.multiple_of(which * half, half), half)
        store_pieces(ref, slot * (half // 2), half // 4, dot(nmt[rows, :], g))
        store_pieces(ref, slot * (half // 2) + half // 4, half // 4, dot(hT[rows, :], cot))
    mix[...] += dot(h, wd)
    gn[...] += dot_nt(g, wu)
    return bsum


def mid_in(idx, own, r1, r2, r3, prods, ends, decay, share, cand, x, cot, w_out, gain,
           st, stT, middle, nm2, nm2t, cotp, split, others, carry8, square):
    length = x.shape[0]
    steps = length // chunks
    units = decay.shape[1]
    z = idx[2]
    for j, ref in enumerate((own, r1, r2, r3)):
        others[j] = ref[...]
    state = jnp.zeros((1, units), f32)
    for k in range(4):
        part = others[k ^ z]
        state = jnp.where(k < z, state * part[0:1] + part[1:2], state)
    for k in range(chunks):
        carry8[k : k + 1, :] = state
        state = state * prods[k : k + 1, :] + ends[k : k + 1, :]
    st[0:chunks, :] = carry8[...]

    def step(s, state):
        rows = pl.ds(pl.multiple_of(s * chunks, chunks), chunks)
        state = state * decay[rows, :] + share[rows, :] * cand[rows, :]
        st[pl.ds(pl.multiple_of(s * chunks + chunks, chunks), chunks), :] = state
        return state

    lax.fori_loop(0, steps, step, carry8[...], unroll=8)
    low = st[chunks:, :].astype(bf16)
    stT[...] = low.T
    mid = x[...] + dot(low, w_out[...])
    middle[...] = mid
    r = lax.rsqrt(jnp.mean(mid * mid, axis=-1, keepdims=True) + norm_eps)
    nm = (mid * r * gain[...]).astype(bf16)
    nm2[...] = nm
    nm2t[...] = nm.T

    def put(rows, cols, values):
        square[rows, cols] = values

    to_chunked(cot, split, put)
    cotp[...] = square[...].astype(bf16)


def pieces_of(idx, near, near_far, far, far_far):
    for which, arrays in ((idx[0], (near, near_far)), (1 - idx[0], (far, far_far))):
        for k in range(2):
            for i in range(2):
                yield which, idx[1] ^ (i * (1 + which) + k * (2 - which)), arrays[k].at[i]


def lay_out(idx, arrays, at, wu, wd):
    rows = wu.shape[0] // 8
    for which, place, piece in pieces_of(idx, *arrays):
        spot = pl.ds(pl.multiple_of((which * 4 + place) * rows, rows), rows)
        wu[spot, :] = piece[at : at + rows, :]
        wd[spot, :] = piece[at + rows : at + 2 * rows, :]


def mlp_own(idx, wu, wd, bu, middle, nm2, nm2t, cotp, mix, gn, keep, send, small, hT):
    mix[...] = middle[...]
    gn[...] = jnp.zeros_like(gn)
    small[...] = jnp.zeros_like(small)
    small[pl.ds(4 * idx[2] + 2, 1), :] = ffn_block(
        0, idx[0], nm2[...], nm2t, cotp[...], wu[...], wd[...], bu[...], mix, gn, keep, send, hT
    )


def mlp_one(idx, n1, n2, f1, f2, bias, mix0, gn0, small0, nm2, nm2t, cotp, mix, gn, keep, send, small, hT, wu, wd):
    mix[...] = mix0[...]
    gn[...] = gn0[...]
    small[...] = small0[...]
    lay_out(idx, (n1, n2, f1, f2), 0, wu, wd)
    small[pl.ds(4 * (idx[2] ^ 1) + 2, 1), :] = ffn_block(
        0, idx[0], nm2[...], nm2t, cotp[...], wu[...], wd[...], bias[2:3, 0 : wu.shape[1]], mix, gn, keep, send, hT
    )


def mlp_two(idx, n1, n2, f1, f2, bias2, bias3, mix0, gn0, small0, nm2, nm2t, cotp, mix, gn, keep, send, small, hT, wu, wd):
    mix[...] = mix0[...]
    gn[...] = gn0[...]
    small[...] = small0[...]
    for slot, bias in enumerate((bias2, bias3)):
        lay_out(idx, (n1, n2, f1, f2), slot * wu.shape[0] // 4, wu, wd)
        small[pl.ds(4 * (idx[2] ^ (2 + slot)) + 2, 1), :] = ffn_block(
            slot, idx[0], nm2[...], nm2t, cotp[...], wu[...], wd[...], bias[2:3, 0 : wu.shape[1]], mix, gn, keep, send, hT
        )


def mid_back(idx, gn, cotp, middle, gain, stT, w_out, decay,
             keep, send, grad_mid, grad_states, payload, prods, flows, gain_row):
    core, z = idx[0], idx[2]
    length, units = decay.shape
    steps = length // chunks
    mid = middle[...]
    r = lax.rsqrt(jnp.mean(mid * mid, axis=-1, keepdims=True) + norm_eps)
    scaled = mid * r
    g = gn[...]
    gain_row[...] = jnp.sum(g * scaled, axis=0, keepdims=True)
    gg = g * gain[...]
    gm = cotp[...].astype(f32) + r * (gg - scaled * jnp.mean(gg * scaled, axis=-1, keepdims=True))
    grad_mid[...] = gm
    low = gm.astype(bf16)
    grad_states[...] = dot_nt(low, w_out[...])
    part = units // 8
    for k in range(4):
        for ref, which in ((send, 1 - core), (keep, core)):
            got = dot(stT[pl.ds(pl.multiple_of((2 * k + which) * part, part), part), :], low)
            at = pl.ds(pl.multiple_of((k ^ z) * (part // 4), part // 4), part // 4)
            for p in range(4):
                ref[p, at, :] = got[p * (part // 4) : (p + 1) * (part // 4)].astype(bf16)

    def step(i, carry):
        prod, flow = carry
        rows = pl.ds(pl.multiple_of((steps - 1 - i) * chunks, chunks), chunks)
        d = decay[rows, :]
        return prod * d, (flow + grad_states[rows, :]) * d

    prod, flow = lax.fori_loop(
        0, steps, step, (jnp.ones((chunks, units), f32), jnp.zeros((chunks, units), f32)), unroll=8
    )
    total, out = prod[chunks - 1 :], flow[chunks - 1 :]
    for k in range(chunks - 2, -1, -1):
        total = total * prod[k : k + 1]
        out = out * prod[k : k + 1] + flow[k : k + 1]
    payload[0:1, :] = total
    payload[1:2, :] = out
    prods[...] = prod
    flows[...] = flow


def mixed_out(mix, mixed, done, split):
    from_chunked(mix, split, mixed)
    done[...] = jnp.zeros_like(done)


def gate_grads(which, keep, carried, st, share, cand, du, dv, w, nmt, z, out, gnm, small):
    length, units = carried.shape
    half = units // 2
    cols = pl.ds(pl.multiple_of(which * half, half), half)
    cf = carried[:, cols]
    q = share[:, cols]
    s = cf * (st[0:length, cols] * keep - cand[:, cols])
    ga = s * du[:, cols]
    gb = -(s * dv[:, cols])
    quarter = half // 2
    sum_a, sum_b = jnp.sum(ga, axis=0, keepdims=True), jnp.sum(gb, axis=0, keepdims=True)
    for i in range(2):
        at = pl.ds(4 * (2 * which + i), 1)
        small[at, 0:quarter] = sum_a[:, i * quarter : (i + 1) * quarter]
        small[at, quarter:] = sum_b[:, i * quarter : (i + 1) * quarter]
    part = nmt.shape[0] // 4
    for k, g in enumerate((ga, gb, cf * q)):
        low = g.astype(bf16)
        got = dot(nmt[...], low)
        for zz in range(4):
            for p in range(4):
                top = zz * part + p * (part // 4)
                out[p, zz ^ z, k * (part // 4) : (k + 1) * (part // 4), :] = got[top : top + part // 4].astype(bf16)
        gnm[...] += dot_nt(low, w[k, :, cols])


def mixer_back(idx, own, r1, r2, r3, prods, flows, decay, share, cand, du, dv, st, grad_states, nmt, w,
               carried, send, gnm, small, others, carry8):
    length, units = decay.shape
    steps = length // chunks
    core, z = idx[0], idx[2]
    for j, ref in enumerate((own, r1, r2, r3)):
        others[j] = ref[...]
    flow = jnp.zeros((1, units), f32)
    for k in range(3, -1, -1):
        part = others[k ^ z]
        flow = jnp.where(k > z, flow * part[0:1] + part[1:2], flow)
    for k in range(chunks - 1, -1, -1):
        carry8[k : k + 1, :] = flow
        flow = flow * prods[k : k + 1, :] + flows[k : k + 1, :]

    def step(i, flow):
        rows = pl.ds(pl.multiple_of((steps - 1 - i) * chunks, chunks), chunks)
        got = grad_states[rows, :] + flow
        carried[rows, :] = got
        return got * decay[rows, :]

    lax.fori_loop(0, steps, step, carry8[...], unroll=8)
    gnm[...] = jnp.zeros_like(gnm)
    small[...] = jnp.zeros_like(small)
    gate_grads(1 - core, keep_mask(idx, length), carried, st, share, cand, du, dv, w, nmt, z, send, gnm, small)


def mixer_out(idx, carried, share, cand, du, dv, st, nmt, w, gnm0, small0, small1, gain_row, x,
              keep, gnm, small):
    length, units = carried.shape
    core, z = idx[0], idx[2]
    gnm[...] = gnm0[...]
    small[...] = small0[...] + small1[...]
    gate_grads(core, keep_mask(idx, length), carried, st, share, cand, du, dv, w, nmt, z, keep, gnm, small)
    v = x[...]
    r = lax.rsqrt(jnp.mean(v * v, axis=-1, keepdims=True) + norm_eps)
    gains = jnp.sum(gnm[...] * (v * r), axis=0, keepdims=True)
    n = gains.shape[1] // 4
    for k in range(4):
        small[4 * k + 1 : 4 * k + 2, 0:n] = gains[:, k * n : (k + 1) * n]
        small[4 * k + 1 : 4 * k + 2, n : 2 * n] = gain_row[:, k * n : (k + 1) * n]


def tokens_out(gnm, x, gain, grad_mid, grad_tok, done, total, split):
    v = x[...]
    r = lax.rsqrt(jnp.mean(v * v, axis=-1, keepdims=True) + norm_eps)
    scaled = v * r
    gg = gnm[...] * gain[...]
    total[...] = grad_mid[...] + r * (gg - scaled * jnp.mean(gg * scaled, axis=-1, keepdims=True))
    from_chunked(total, split, grad_tok)
    done[...] = jnp.zeros_like(done)


def pick_piece(idx, wu, wd, out, sems):
    rows = wu.shape[0] // 8
    at = pl.ds(pl.multiple_of((idx[0] * 4 + idx[1]) * rows, rows), rows)
    for copy in fetch([(wu.at[at, :], out.at[pl.ds(0, rows), :]), (wd.at[at, :], out.at[pl.ds(rows, rows), :])], sems):
        copy.wait()


def gate(value, after):
    any_space = pl.BlockSpec(memory_space=pl.ANY)
    return pl.pallas_call(
        lambda *refs: None,
        out_shape=jax.ShapeDtypeStruct(value.shape, value.dtype),
        in_specs=[any_space, any_space],
        out_specs=any_space,
        input_output_aliases={0: 0},
        compiler_params=pltpu.CompilerParams(vmem_limit_bytes=1 << 20),
        name="gate",
    )(value, after)


def join(*refs):
    out, rows = refs[-1], refs[0].shape[0]
    for k, ref in enumerate(refs[:-1]):
        if len(out.shape) == 3:
            out[k] = ref[...]
        else:
            out[k * rows : (k + 1) * rows, :] = ref[...]


def two_terms(v):
    high = v.astype(bf16)
    return high, (v - high.astype(f32)).astype(bf16)


def add_pair(keep, got, out):
    out[...] = (keep[...].astype(f32) + got[...].astype(f32)).astype(bf16)


def add_core(idx, keep_a, got_a, more_a, keep_b, got_b, keep_c, got_c, send_x, send_y, own_x, own_y):
    x, y = idx[1] % 2, idx[1] // 2
    half = send_x.shape[1]

    def put(ref, k, p, first):
        top = 0
        for arrays in ((keep_a, got_a, more_a), (keep_b, got_b), (keep_c, got_c)):
            n = arrays[0].shape[1]
            low, high = max(first, top), min(first + half, top + n)
            if low < high:
                rows = slice(low - top, high - top)
                total = arrays[0][p, rows, :].astype(f32)
                for more in arrays[1:]:
                    total = total + more[p, rows, :].astype(f32)
                ref[k, low - first : high - first, :] = total.astype(ref.dtype)
            top += n

    for k in range(2):
        put(send_x, k, 2 * k + 1 - x, 0)
        put(own_x, k, 2 * k + x, 0)
        put(send_y, k, 2 * (1 - y) + k, half)
        put(own_y, k, 2 * y + k, half)


def add_cross(idx, own_x, got_x, own_y, got_y, send_y, send_x, out_x, out_y):
    x, y = idx[1] % 2, idx[1] // 2
    send_y[...] = (own_x[1 - y] + got_x[1 - y].astype(f32)).astype(bf16)
    out_x[...] = own_x[y] + got_x[y].astype(f32)
    send_x[...] = (own_y[1 - x] + got_y[1 - x].astype(f32)).astype(bf16)
    out_y[...] = own_y[x] + got_y[x].astype(f32)


def add_depth(own_x, got_x, own_y, got_y, send, own, total):
    half = own_x.shape[0]
    part = send.shape[0] // 6
    block = 4 * part
    total[0:half, :] = own_x[...] + got_x[...].astype(f32)
    total[half:, :] = own_y[...] + got_y[...].astype(f32)
    out = 3 * block
    for ref, to, at, n in ((send, 0, 2 * block, block), (send, block, out + part, part), (send, block + part, out + 3 * part, part),
                           (own, 0, 0, block), (own, block, out, part), (own, block + part, block, block), (own, 2 * block + part, out + 2 * part, part)):
        ref[to : to + n, :] = total[at : at + n, :].astype(ref.dtype)


def add_far(own, got, send, out):
    rows = out.shape[0]
    part = rows // 5
    block = 4 * part
    out[0:block, :] = own[0:block, :]
    out[block:, :] = own[block:rows, :] + got[block:rows, :].astype(f32)
    send[0:block, :] = (own[rows : rows + block, :] + got[0:block, :].astype(f32)).astype(bf16)
    send[block:, :] = (own[rows + block :, :] + got[rows:, :].astype(f32)).astype(bf16)


def add_last(own, got, out):
    out[...] = (own[...] + got[...].astype(f32)).astype(out.dtype)


def add_core_small(idx, keep, got, small, send_x, send_y, own_x, own_y, tiny):
    x, y = idx[1] % 2, idx[1] // 2
    half, n = own_x.shape[1], small.shape[0]
    high, low = two_terms(small[...])
    tiny[0:n, :] = high
    tiny[n:, :] = low
    send_x[2 * half : 2 * half + n, :] = high
    send_x[2 * half + n :, :] = low
    for k in range(2):
        at = slice(k * half, (k + 1) * half)
        p = 2 * k + 1 - x
        send_x[at, :] = (keep[p, 0:half, :].astype(f32) + got[p, 0:half, :].astype(f32)).astype(bf16)
        p = 2 * k + x
        own_x[k] = keep[p, 0:half, :].astype(f32) + got[p, 0:half, :].astype(f32)
        p = 2 * (1 - y) + k
        send_y[at, :] = (keep[p, half:, :].astype(f32) + got[p, half:, :].astype(f32)).astype(bf16)
        p = 2 * y + k
        own_y[k] = keep[p, half:, :].astype(f32) + got[p, half:, :].astype(f32)


def add_tiny(tiny, got, at):
    n = tiny.shape[0] // 2
    return (tiny[0:n, :].astype(f32) + tiny[n:, :].astype(f32)) + (
        got[at : at + n, :].astype(f32) + got[at + n : at + 2 * n, :].astype(f32)
    )


def add_cross_small(idx, own_x, got_x, own_y, got_y, tiny, send_y, send_x, out_x, out_y, tiny_out):
    x, y = idx[1] % 2, idx[1] // 2
    half, n = out_x.shape[0], tiny.shape[0] // 2
    high, low = two_terms(add_tiny(tiny, got_x, 2 * half))
    tiny_out[0:n, :] = high
    tiny_out[n:, :] = low
    send_y[half : half + n, :] = high
    send_y[half + n :, :] = low
    side = pl.ds(pl.multiple_of((1 - y) * half, half), half)
    send_y[0:half, :] = (own_x[1 - y] + got_x[side, :].astype(f32)).astype(bf16)
    side = pl.ds(pl.multiple_of(y * half, half), half)
    out_x[...] = own_x[y] + got_x[side, :].astype(f32)
    side = pl.ds(pl.multiple_of((1 - x) * half, half), half)
    send_x[...] = (own_y[1 - x] + got_y[side, :].astype(f32)).astype(bf16)
    side = pl.ds(pl.multiple_of(x * half, half), half)
    out_y[...] = own_y[x] + got_y[side, :].astype(f32)


def add_depth_small(idx, own_x, got_x, own_y, got_y, tiny, send, own, small):
    half, z = own_x.shape[0], idx[2]
    rows = half // 2
    total = add_tiny(tiny, got_x, half)
    n = total.shape[0] // 4
    small[...] = jnp.zeros_like(small)
    for k in range(4):
        small[k, 0:n, :] = total[k * n : (k + 1) * n]
    for j in range(4):
        own_ref, got = ((own_x, got_x), (own_y, got_y))[j // 2]
        at = slice((j % 2) * rows, (j % 2 + 1) * rows)
        value = own_ref[at, :] + got[at, :].astype(f32)
        base = (j // 2) * (rows + 16)
        if j % 2:
            send[base : base + rows, :] = value.astype(bf16)
            high, low = two_terms(small[z ^ j])
            send[base + rows : base + rows + 16, :] = jnp.concatenate([high, low], axis=0)
        else:
            own[(j // 2) * rows : (j // 2 + 1) * rows, :] = value


def add_far_small(idx, own, got, small, send, out, tiny_out):
    z = idx[2]
    rows, n = out.shape[0], tiny_out.shape[0]
    tiny = []
    for k in range(2):
        base = k * (rows + 16)
        mine = small[z ^ (2 * k)]
        other = got[base + rows : base + rows + 16, :].astype(f32)
        tiny.append(mine + (other[0:n] + other[n : 2 * n]))
    out[...] = own[0:rows, :] + got[0:rows, :].astype(f32)
    tiny_out[...] = tiny[0]
    send[0:rows, :] = (own[rows:, :] + got[rows + 16 : 2 * rows + 16, :].astype(f32)).astype(bf16)
    high, low = two_terms(tiny[1])
    send[rows:, :] = jnp.concatenate([high, low], axis=0)


def add_last_small(own, tiny, got, out, tiny_out):
    rows, n = own.shape[0], tiny.shape[0]
    out[...] = (own[...] + got[0:rows, :].astype(f32)).astype(out.dtype)
    other = got[rows:, :].astype(f32)
    tiny_out[...] = tiny[...] + (other[0:n] + other[n : 2 * n])


def spread_mlp(idx, near, far, up, down, w_out, done):
    rows = up.shape[0] // 8
    rows_out = w_out.shape[0] // 8
    for which, pieces in ((idx[0], near), (1 - idx[0], far)):
        for k in range(4):
            spot = which * 4 + (idx[1] ^ k)
            at = pl.ds(pl.multiple_of(spot * rows, rows), rows)
            up[at, :] = pieces[k, 0:rows, :].astype(f32)
            down[at, :] = pieces[k, rows : 2 * rows, :].astype(f32)
            w_out[pl.ds(pl.multiple_of(spot * rows_out, rows_out), rows_out), :] = pieces[k, 2 * rows :, :].astype(f32)
    done[...] = jnp.zeros_like(done)


def spread_mix(idx, tiny, tiny_far, near, far, out, bias_f, bias_i, gain_mix, gain_mlp, b_up):
    rows, half = out.shape[1] // 4, out.shape[2] // 2
    for which, pieces in ((idx[0], near), (1 - idx[0], far)):
        cols = pl.ds(pl.multiple_of(which * half, half), half)
        for k in range(4):
            at = pl.ds(pl.multiple_of((idx[1] ^ k) * rows, rows), rows)
            for i in range(3):
                out[i, at, cols] = pieces[k, i * rows : (i + 1) * rows, :].astype(f32)
    small = tiny[...] + tiny_far[...]
    n = bias_f.shape[1]
    bias_f[...] = small[0:1, 0:n]
    bias_i[...] = small[0:1, n:]
    n = gain_mix.shape[1]
    gain_mix[...] = small[1:2, 0:n]
    gain_mlp[...] = small[1:2, n : 2 * n]
    b_up[...] = small[2:3, :]


def swap(value, axis, bit):
    size = lax.axis_size(axis)
    return lax.ppermute(value, axis, [(i, i ^ bit) for i in range(size)])


def across(value, turn):
    size = lax.axis_size("dp")
    return lax.ppermute(value, "dp", [(i, i ^ (2 << ((i & 1) ^ turn))) for i in range(size)])


def on_device(tokens, gain_mix, w_mix, bias_forget, bias_input, w_out, gain_mlp, w_up, b_up, w_down, resets, cotangent):
    length, width = tokens.shape[1:]
    units = w_out.shape[0]
    ff = w_up.shape[1]
    dp, mp = lax.axis_size("dp"), lax.axis_size("mp")
    assert mp == 4 and dp % 8 == 0 and tokens.shape[0] == 1
    place = lax.axis_index("dp")
    here = jnp.stack([place & 1, (place >> 1) & 3, lax.axis_index("mp")]).astype(jnp.int32)
    idx = jnp.concatenate([here, resets[0]])
    tok, cot = tokens[0], cotangent[0]
    w3 = w_mix.transpose(1, 0, 2)
    row = lambda v: v.reshape(1, -1)
    lanes = width // 128

    (piece,) = call(pick_piece, "pick_piece", (idx, w_up, w_down), [shape_of(bf16, width // 4, ff)],
                    [pltpu.SemaphoreType.DMA((2,))], hbm=2, limit=2)
    depth = [swap(piece, "mp", j) for j in (1, 2, 3)]

    wide = shape_of(f32, length, units)
    square = shape_of(f32, length, width)
    square16 = shape_of(bf16, length, width)
    edge = shape_of(f32, chunks, units)
    decay, share, cand, du, dv, nmt, x, prods, ends, payload = call(
        mixer_in, "mixer_in",
        (idx, tok, row(gain_mix), row(bias_forget), row(bias_input), row(b_up), w3),
        [wide] * 5 + [shape_of(bf16, width, length), square, edge, edge, shape_of(f32, 4, units)],
        [pltpu.VMEM((lanes, length, 128), f32), pltpu.VMEM((length, width), bf16), pltpu.VMEM((1, width), f32)]
        + [pltpu.VMEM((1, units), f32)] * 2 + [pltpu.VMEM((1, ff), f32), pltpu.VMEM((3, width, units), bf16),
                                              pltpu.SemaphoreType.DMA((5 + units // 256,))],
        hbm=6, after=(piece,),
    )
    ahead = [swap(payload, "mp", j) for j in (1, 2, 3)]
    around = lambda v: [v] + [swap(v, "dp", 2 * k) for k in (1, 2, 3)]
    mine = gate(depth[0], payload)
    (two,) = call(join, "join_depth", depth[1:], [shape_of(bf16, width // 2, ff)], smem=0, after=(payload,))
    (one_a,) = call(join, "join_one", (mine, across(mine, 0)), [shape_of(bf16, 2, width // 4, ff)], smem=0, after=(two,))
    (two_a,) = call(join, "join_two", (two, across(two, 0)), [shape_of(bf16, 2, width // 2, ff)], smem=0)
    two_b = across(two_a, 1)
    quarter = width // 8
    st, stT, middle, nm2, nm2t, cotp = call(
        mid_in, "mid_in",
        (idx, payload, *ahead, prods, ends, decay, share, cand, x, cot, w_out, row(gain_mlp)),
        [shape_of(f32, length + chunks, units), shape_of(bf16, units, length), square, square16, shape_of(bf16, width, length), square16],
        [pltpu.VMEM((lanes, length, 128), f32), pltpu.VMEM((4, 4, units), f32), pltpu.VMEM((chunks, units), f32), pltpu.VMEM((length, width), f32)],
        after=(two_a,),
    )
    block = 2 * quarter
    pair = lambda dtype, rows: shape_of(dtype, 2, rows, width)
    weights = [pltpu.VMEM((ff, length), bf16), pltpu.VMEM((width, ff), bf16), pltpu.VMEM((ff, width), bf16)]
    grads = lambda rows: [square] * 2 + [shape_of(bf16, 4, rows, width)] * 2 + [shape_of(f32, 16, width)]
    one_b = gate(across(one_a, 1), nm2)
    mix, gn, keep0, send0, small_mlp = call(
        mlp_own, "mlp_own", (idx, w_up, w_down, row(b_up), middle, nm2, nm2t, cotp), grads(block), weights[:1],
    )
    mix, gn, keep_a, send_a, small_mlp = call(
        mlp_one, "mlp_one",
        (idx, one_a, one_b, swap(one_a, "dp", 1), swap(one_b, "dp", 1), ahead[0], mix, gn, small_mlp, nm2, nm2t, cotp), grads(block), weights,
    )
    (pair_a,) = call(add_pair, "add_pair", (keep_a, swap(send_a, "dp", 1)), [shape_of(bf16, 4, block, width)], smem=0)
    more_a = swap(pair_a, "mp", 1)
    mix, gn, keep, send, small_mlp = call(
        mlp_two, "mlp_two",
        (idx, two_a, two_b, swap(two_a, "dp", 1), swap(two_b, "dp", 1), ahead[1], ahead[2], mix, gn, small_mlp, nm2, nm2t, cotp),
        grads(2 * block), weights, after=(pair_a,),
    )
    got, got0 = swap(send, "dp", 1), swap(send0, "dp", 1)
    out_rows = units // 8
    keep_out, send_out, grad_mid, grad_states, payload, prods, flows, gain_row = call(
        mid_back, "mid_back",
        (idx, gn, cotp, middle, row(gain_mlp), stT, w_out, decay),
        [shape_of(bf16, 4, out_rows, width)] * 2 + [square, wide, shape_of(f32, 2, units), edge, edge, shape_of(f32, 1, width)],
    )
    payload = gate(payload, got)
    behind = [swap(payload, "mp", j) for j in (1, 2, 3)]

    half = (3 * block + out_rows) // 2
    send_x, send_y, own_x, own_y = call(add_core, "add_core", (idx, keep0, got0, more_a, keep, got, keep_out, swap(send_out, "dp", 1)),
                                        [pair(bf16, half)] * 2 + [pair(f32, half)] * 2)
    got_x, got_y = swap(send_x, "dp", 2), swap(send_y, "dp", 4)

    rows_m = 3 * width // 16
    carried, send, gnm, small = call(
        mixer_back, "mixer_back",
        (idx, payload, *behind, prods, flows, decay, share, cand, du, dv, st, grad_states, nmt, w3),
        [wide, shape_of(bf16, 4, 4, rows_m, units // 2), square, shape_of(f32, 16, width)],
        [pltpu.VMEM((4, 2, units), f32), pltpu.VMEM((chunks, units), f32)], after=(own_x,),
    )
    flat = lambda v: v.reshape(4, -1, width)
    got = swap(send, "dp", 1)
    keep, gnm, small = call(
        mixer_out, "mixer_out",
        (idx, carried, share, cand, du, dv, st, nmt, w3, gnm, small, small_mlp, gain_row, x),
        [shape_of(bf16, 4, 4, rows_m, units // 2), square, shape_of(f32, 16, width)],
    )
    half_m = 2 * rows_m
    one = lambda dtype, rows: shape_of(dtype, rows, width)
    send_mx, send_my, own_mx, own_my, tiny = call(
        add_core_small, "add_core_small", (idx, flat(keep), flat(got), small),
        [one(bf16, 2 * half_m + 32), one(bf16, 2 * half_m), pair(f32, half_m), pair(f32, half_m), one(bf16, 32)],
    )
    got_mx, got_my = swap(send_mx, "dp", 2), swap(send_my, "dp", 4)
    mark = shape_of(f32, 8, 128)
    grad_tok, done_tok = call(tokens_out, "tokens_out", (gnm, x, row(gain_mix), grad_mid), [square16, mark],
                       [pltpu.VMEM((length, width), f32), pltpu.VMEM((lanes, length, 128), f32)], smem=0, after=(own_mx,))
    mixed, done_mix = call(mixed_out, "mixed_out", (mix,), [square16, mark], [pltpu.VMEM((lanes, length, 128), f32)], smem=0, after=(own_mx,))

    send_y, send_x, own_x, own_y = call(add_cross, "add_cross", (idx, own_x, got_x, own_y, got_y),
                                        [one(bf16, half)] * 2 + [one(f32, half)] * 2, after=(own_mx,))
    got_x, got_y = swap(send_y, "dp", 4), swap(send_x, "dp", 2)
    send_my, send_mx, own_mx, own_my, tiny = call(
        add_cross_small, "add_cross_small", (idx, own_mx, got_mx, own_my, got_my, tiny),
        [one(bf16, half_m + 32), one(bf16, half_m), one(f32, half_m), one(f32, half_m), one(bf16, 32)],
        after=(own_x, done_mix, done_tok),
    )
    got_mx, got_my = swap(send_my, "dp", 4), swap(send_mx, "dp", 2)
    rows_f = block + units // 32
    send, own = call(add_depth, "add_depth", (own_x, got_x, own_y, got_y), [one(bf16, block + units // 16), one(f32, 2 * rows_f)],
                     [pltpu.VMEM((2 * half, width), f32)], smem=0, after=(own_mx,))
    got = swap(send, "mp", 1)
    send_m, own_m, small = call(
        add_depth_small, "add_depth_small", (idx, own_mx, got_mx, own_my, got_my, tiny),
        [one(bf16, 2 * rows_m + 32), one(f32, 2 * rows_m), shape_of(f32, 4, 8, width)], after=(own,),
    )
    got_m = swap(send_m, "mp", 1)
    send, own = call(add_far, "add_far", (own, got), [one(bf16, rows_f), one(f32, rows_f)], smem=0, after=(small,))
    got = swap(send, "mp", 2)
    send_m, own_m, tiny = call(
        add_far_small, "add_far_small", (idx, own_m, got_m, small),
        [one(bf16, rows_m + 16), one(f32, rows_m), one(f32, 8)], after=(own,),
    )
    got_m = swap(send_m, "mp", 2)
    groups = [[g * 8 + i for g in range(dp // 8)] for i in range(8)]

    def last(fn, name, operands, outs, after):
        if dp == 8:
            return call(fn, name, operands, outs, smem=0, after=after)
        done = call(fn, name, operands, [shape_of(f32, *o.shape) for o in outs], smem=0, after=after)
        return [lax.psum(v, "dp", axis_index_groups=groups).astype(o.dtype) for v, o in zip(done, outs)]

    (part,) = last(add_last, "add_last", (own, got), [one(bf16, rows_f)], (tiny,))
    near_f = around(part)
    part, tiny = last(add_last_small, "add_last_small", (own_m, tiny, got_m), [one(bf16, rows_m), one(f32, 8)], (part,))
    near_m = around(part)
    (near,) = call(join, "join_mlp", near_f, [shape_of(bf16, 4, rows_f, width)], smem=0, after=(part,))
    grad_up, grad_down, grad_out, done = call(
        spread_mlp, "spread_mlp", (idx, near, swap(near, "dp", 1)),
        [shape_of(f32, width, ff), shape_of(f32, ff, width), shape_of(f32, units // 4, width), mark],
    )
    (near,) = call(join, "join_mix", near_m, [shape_of(bf16, 4, rows_m, width)], smem=0)
    grad_mix, g_bf, g_bi, g_gain_mix, g_gain_mlp, g_bu = call(
        spread_mix, "spread_mix", (idx, tiny, swap(tiny, "dp", 1), near, swap(near, "dp", 1)),
        [shape_of(f32, 3, width // 4, units), shape_of(f32, 1, units // 4), shape_of(f32, 1, units // 4),
         shape_of(f32, 1, width // 4), shape_of(f32, 1, width // 4), shape_of(f32, 1, ff)],
        after=(done,),
    )
    return (
        mixed[None], grad_tok[None], g_gain_mix[0], grad_mix.transpose(1, 0, 2), g_bf[0], g_bi[0],
        grad_out, g_gain_mlp[0], grad_up, g_bu[0], grad_down,
    )


def solution(mesh):
    return jax.shard_map(
        on_device,
        mesh=mesh,
        in_specs=(P("dp", "mp", None), P(), P(), P(), P(), P(), P(), P(None, "mp"), P("mp"), P("mp", None), P("dp", None), P("dp", "mp", None)),
        out_specs=(P("dp", "mp", None), P("dp", "mp", None), P("mp"), P("mp", None, None), P("mp"), P("mp"), P("mp", None), P("mp"), P(None, "mp"), P("mp"), P("mp", None)),
        check_vma=False,
    )
```

```python
from functools import partial

import jax
import jax.numpy as jnp
from jax import lax
from jax.experimental import pallas as pl
from jax.experimental.pallas import tpu as pltpu
from jax.sharding import PartitionSpec as P

norm_eps = 1e-06
gelu_k = 0.7978845608028654
gelu_c = 0.044715
chunks = 8
f32 = jnp.float32
bf16 = jnp.bfloat16
VMEM = pl.BlockSpec(memory_space=pltpu.VMEM)
SMEM = pl.BlockSpec(memory_space=pltpu.SMEM)
HBM = pl.BlockSpec(memory_space=pltpu.HBM)


weight = {
    "pick_piece": 4, "mixer_in": 0, "join_depth": 16, "join_one": 0, "mlp_one": 0, "join_two": 0, "mlp_two": 32, "mid_back": 32,
    "add_core": 32, "mixer_back": 0, "mixer_out": 16, "add_core_small": 4, "add_cross": 0, "mixed_out": 0, "tokens_out": 2,
    "add_cross_small": 0, "add_depth": 0, "add_depth_small": 8, "add_far": 2, "add_far_small": 16, "add_last": 4,
    "add_last_small": 4, "join_mlp": 2, "join_mix": 16, "spread_mlp": 8, "spread_mix": 8, "add_pair": 2, "mid_in": 0,
    "mlp_own": 16,
}


def dot(a, b):
    return jnp.dot(a, b, preferred_element_type=f32)


def dot_nt(a, b):
    return lax.dot_general(a, b, (((1,), (1,)), ((), ())), preferred_element_type=f32)


def shape_of(dtype, *shape):
    return jax.ShapeDtypeStruct(shape, dtype)


def call(body, name, operands, outs, scratch=(), smem=1, limit=16, after=(), hbm=0):
    n, extra, cost = len(operands), len(after), weight[name]
    operands = [pltpu.with_memory_space_constraint(v, pltpu.HBM) if smem <= i < smem + hbm else v for i, v in enumerate(operands)]

    def run(*refs):
        body(*refs[:n], *refs[n + extra :])

    return pl.pallas_call(
        run,
        out_shape=outs,
        in_specs=[SMEM] * smem + [HBM] * hbm + [VMEM] * (n - smem - hbm) + [pl.BlockSpec(memory_space=pl.ANY)] * extra,
        out_specs=[VMEM] * len(outs),
        scratch_shapes=list(scratch),
        compiler_params=pltpu.CompilerParams(vmem_limit_bytes=limit << 20),
        cost_estimate=pl.CostEstimate(flops=cost << 30, bytes_accessed=cost << 22, transcendentals=0),
        name=name,
    )(*operands, *after)


def to_chunked(src, split, put):
    length, width = src.shape
    steps = length // chunks
    for g in range(width // 128):
        cols = slice(g * 128, (g + 1) * 128)
        split[g] = src[:, cols].astype(f32)
        for s in range(steps):
            put(pl.ds(s * chunks, chunks), cols, split[g, pl.ds(s, chunks, stride=steps), :])


def from_chunked(values, split, out):
    length, width = out.shape
    steps = length // chunks
    for g in range(width // 128):
        cols = slice(g * 128, (g + 1) * 128)
        for s in range(steps):
            split[g, pl.ds(s, chunks, stride=steps), :] = values[s * chunks : (s + 1) * chunks, cols]
        out[:, cols] = split[g].astype(bf16)


def keep_mask(idx, resets, length):
    row = lax.broadcasted_iota(jnp.int32, (length, 1), 0)
    pos = idx[2] * length + (row % chunks) * (length // chunks) + row // chunks
    keep = jnp.ones((length, 1), f32)
    for i in range(3):
        keep = jnp.where(pos == resets[0, i], 0.0, keep)
    return keep


def fetch(pairs, sems):
    copies = [pltpu.make_async_copy(src, dst, sems.at[i]) for i, (src, dst) in enumerate(pairs)]
    for copy in copies:
        copy.start()
    return copies


def mixer_in(idx, res_hbm, tok_hbm, gain_hbm, bias_f_hbm, bias_i_hbm, b_up_hbm, w_hbm, decay, share, cand, du, dv, nmt, x, prods, ends, payload, mask,
             resets, split, tok, gain, bias_f, bias_i, b_up, w, sems):
    length, width = tok.shape
    units = bias_f.shape[1]
    steps = length // chunks
    block = 256
    pairs = [(tok_hbm, tok), (gain_hbm, gain), (bias_f_hbm, bias_f), (bias_i_hbm, bias_i), (b_up_hbm, b_up), (res_hbm, resets)]
    for h in range(0, units, block):
        sl = pl.ds(h, block)
        pairs.append((w_hbm.at[:, :, sl], w.at[:, :, sl]))
    copies = fetch(pairs, sems)
    for copy in copies[:6]:
        copy.wait()

    def put(rows, cols, values):
        x[rows, cols] = values

    to_chunked(tok, split, put)
    v = x[...]
    r = lax.rsqrt(jnp.mean(v * v, axis=-1, keepdims=True) + norm_eps)
    nm = (v * r * gain[...]).astype(bf16)
    nmt[...] = nm.T
    keep = keep_mask(idx, resets, length)
    mask[...] = keep
    for i, h in enumerate(range(0, units, block)):
        sl = pl.ds(h, block)
        copies[6 + i].wait()
        a = jnp.exp(jnp.minimum(-(dot(nm, w[0, :, sl]) + bias_f[:, sl]), 88.0))
        b = jnp.exp(jnp.minimum(-(dot(nm, w[1, :, sl]) + bias_i[:, sl]), 88.0))
        t = 1.0 / (2.0 + a + b)
        p = (1.0 + b) * t
        q = (1.0 + a) * t
        decay[:, sl] = p * keep
        share[:, sl] = q
        cand[:, sl] = dot(nm, w[2, :, sl])
        du[:, sl] = p * (a * t)
        dv[:, sl] = q * (b * t)

    def step(s, carry):
        prod, end = carry
        rows = pl.ds(pl.multiple_of(s * chunks, chunks), chunks)
        d = decay[rows, :]
        return prod * d, end * d + share[rows, :] * cand[rows, :]

    prod, end = lax.fori_loop(
        0, steps, step, (jnp.ones((chunks, units), f32), jnp.zeros((chunks, units), f32)), unroll=8
    )
    prods[...] = prod
    ends[...] = end
    total, state = prod[0:1], end[0:1]
    for k in range(1, chunks):
        total = total * prod[k : k + 1]
        state = state * prod[k : k + 1] + end[k : k + 1]
    payload[...] = jnp.zeros_like(payload)
    payload[0:1, :] = total
    payload[1:2, :] = state
    payload[2:3, 0 : b_up.shape[1]] = b_up[...]


def feed_forward(nm, cot, wu, wd, bu):
    pre = dot(nm, wu) + bu
    grad_act = dot_nt(cot, wd)
    sq = pre * pre
    t = jnp.tanh(pre * (gelu_k + gelu_k * gelu_c * sq))
    half = 0.5 + 0.5 * t
    h = pre * half
    slope = half + h * (1.0 - t) * (gelu_k + 3.0 * gelu_k * gelu_c * sq)
    grad_pre = grad_act * slope
    return h.astype(bf16), grad_pre.astype(bf16), jnp.sum(grad_pre, axis=0, keepdims=True)


def store_pieces(ref, base, rows, values):
    for p in range(4):
        ref[p, base : base + rows, :] = values[p * rows : (p + 1) * rows].astype(bf16)


def ffn_block(slot, core, nm, nmt, cot, wu, wd, bu, mix, gn, keep, send, hT):
    h, g, bsum = feed_forward(nm, cot, wu, wd, bu)
    hT[...] = h.T
    half = nm.shape[1] // 2
    for ref, which in ((send, 1 - core), (keep, core)):
        rows = pl.ds(pl.multiple_of(which * half, half), half)
        store_pieces(ref, slot * (half // 2), half // 4, dot(nmt[rows, :], g))
        store_pieces(ref, slot * (half // 2) + half // 4, half // 4, dot(hT[rows, :], cot))
    mix[...] += dot(h, wd)
    gn[...] += dot_nt(g, wu)
    return bsum


def mid_in(idx, own, r1, r2, r3, prods, ends, decay, share, cand, x, cot, w_out, gain,
           st, stT, middle, nm2, nm2t, cotp, split, others, carry8, square):
    length = x.shape[0]
    steps = length // chunks
    units = decay.shape[1]
    z = idx[2]
    for j, ref in enumerate((own, r1, r2, r3)):
        others[j] = ref[...]
    state = jnp.zeros((1, units), f32)
    for k in range(4):
        part = others[k ^ z]
        state = jnp.where(k < z, state * part[0:1] + part[1:2], state)
    for k in range(chunks):
        carry8[k : k + 1, :] = state
        state = state * prods[k : k + 1, :] + ends[k : k + 1, :]
    st[0:chunks, :] = carry8[...]

    def step(s, state):
        rows = pl.ds(pl.multiple_of(s * chunks, chunks), chunks)
        state = state * decay[rows, :] + share[rows, :] * cand[rows, :]
        st[pl.ds(pl.multiple_of(s * chunks + chunks, chunks), chunks), :] = state
        return state

    lax.fori_loop(0, steps, step, carry8[...], unroll=8)
    low = st[chunks:, :].astype(bf16)
    stT[...] = low.T
    mid = x[...] + dot(low, w_out[...])
    middle[...] = mid
    r = lax.rsqrt(jnp.mean(mid * mid, axis=-1, keepdims=True) + norm_eps)
    nm = (mid * r * gain[...]).astype(bf16)
    nm2[...] = nm
    nm2t[...] = nm.T

    def put(rows, cols, values):
        square[rows, cols] = values

    to_chunked(cot, split, put)
    cotp[...] = square[...].astype(bf16)


def pieces_of(idx, near, near_far, far, far_far):
    for which, arrays in ((idx[0], (near, near_far)), (1 - idx[0], (far, far_far))):
        for k in range(2):
            for i in range(2):
                yield which, idx[1] ^ (i * (1 + which) + k * (2 - which)), arrays[k].at[i]


def lay_out(idx, arrays, at, wu, wd):
    rows = wu.shape[0] // 8
    for which, place, piece in pieces_of(idx, *arrays):
        spot = pl.ds(pl.multiple_of((which * 4 + place) * rows, rows), rows)
        wu[spot, :] = piece[at : at + rows, :]
        wd[spot, :] = piece[at + rows : at + 2 * rows, :]


def mlp_own(idx, wu, wd, bu, middle, nm2, nm2t, cotp, mix, gn, keep, send, small, hT):
    mix[...] = middle[...]
    gn[...] = jnp.zeros_like(gn)
    small[...] = jnp.zeros_like(small)
    small[pl.ds(4 * idx[2] + 2, 1), :] = ffn_block(
        0, idx[0], nm2[...], nm2t, cotp[...], wu[...], wd[...], bu[...], mix, gn, keep, send, hT
    )


def mlp_one(idx, n1, n2, f1, f2, bias, mix0, gn0, small0, nm2, nm2t, cotp, mix, gn, keep, send, small, hT, wu, wd):
    mix[...] = mix0[...]
    gn[...] = gn0[...]
    small[...] = small0[...]
    lay_out(idx, (n1, n2, f1, f2), 0, wu, wd)
    small[pl.ds(4 * (idx[2] ^ 1) + 2, 1), :] = ffn_block(
        0, idx[0], nm2[...], nm2t, cotp[...], wu[...], wd[...], bias[2:3, 0 : wu.shape[1]], mix, gn, keep, send, hT
    )


def mlp_two(idx, n1, n2, f1, f2, bias2, bias3, mix0, gn0, small0, nm2, nm2t, cotp, mix, gn, keep, send, small, hT, wu, wd):
    mix[...] = mix0[...]
    gn[...] = gn0[...]
    small[...] = small0[...]
    for slot, bias in enumerate((bias2, bias3)):
        lay_out(idx, (n1, n2, f1, f2), slot * wu.shape[0] // 4, wu, wd)
        small[pl.ds(4 * (idx[2] ^ (2 + slot)) + 2, 1), :] = ffn_block(
            slot, idx[0], nm2[...], nm2t, cotp[...], wu[...], wd[...], bias[2:3, 0 : wu.shape[1]], mix, gn, keep, send, hT
        )


def mid_back(idx, gn, cotp, middle, gain, stT, w_out, decay,
             keep, send, grad_mid, grad_states, payload, prods, flows, gain_row):
    core, z = idx[0], idx[2]
    length, units = decay.shape
    steps = length // chunks
    mid = middle[...]
    r = lax.rsqrt(jnp.mean(mid * mid, axis=-1, keepdims=True) + norm_eps)
    scaled = mid * r
    g = gn[...]
    gain_row[...] = jnp.sum(g * scaled, axis=0, keepdims=True)
    gg = g * gain[...]
    gm = cotp[...].astype(f32) + r * (gg - scaled * jnp.mean(gg * scaled, axis=-1, keepdims=True))
    grad_mid[...] = gm
    low = gm.astype(bf16)
    grad_states[...] = dot_nt(low, w_out[...])
    part = units // 8
    for k in range(4):
        for ref, which in ((send, 1 - core), (keep, core)):
            got = dot(stT[pl.ds(pl.multiple_of((2 * k + which) * part, part), part), :], low)
            at = pl.ds(pl.multiple_of((k ^ z) * (part // 4), part // 4), part // 4)
            for p in range(4):
                ref[p, at, :] = got[p * (part // 4) : (p + 1) * (part // 4)].astype(bf16)

    def step(i, carry):
        prod, flow = carry
        rows = pl.ds(pl.multiple_of((steps - 1 - i) * chunks, chunks), chunks)
        d = decay[rows, :]
        return prod * d, (flow + grad_states[rows, :]) * d

    prod, flow = lax.fori_loop(
        0, steps, step, (jnp.ones((chunks, units), f32), jnp.zeros((chunks, units), f32)), unroll=8
    )
    total, out = prod[chunks - 1 :], flow[chunks - 1 :]
    for k in range(chunks - 2, -1, -1):
        total = total * prod[k : k + 1]
        out = out * prod[k : k + 1] + flow[k : k + 1]
    payload[0:1, :] = total
    payload[1:2, :] = out
    prods[...] = prod
    flows[...] = flow


def mixed_out(mix, mixed, done, split):
    from_chunked(mix, split, mixed)
    done[...] = jnp.zeros_like(done)


def gate_grads(which, keep, carried, st, share, cand, du, dv, w, nmt, z, out, gnm, small):
    length, units = carried.shape
    half = units // 2
    cols = pl.ds(pl.multiple_of(which * half, half), half)
    cf = carried[:, cols]
    q = share[:, cols]
    s = cf * (st[0:length, cols] * keep - cand[:, cols])
    ga = s * du[:, cols]
    gb = -(s * dv[:, cols])
    quarter = half // 2
    sum_a, sum_b = jnp.sum(ga, axis=0, keepdims=True), jnp.sum(gb, axis=0, keepdims=True)
    for i in range(2):
        at = pl.ds(4 * (2 * which + i), 1)
        small[at, 0:quarter] = sum_a[:, i * quarter : (i + 1) * quarter]
        small[at, quarter:] = sum_b[:, i * quarter : (i + 1) * quarter]
    part = nmt.shape[0] // 4
    for k, g in enumerate((ga, gb, cf * q)):
        low = g.astype(bf16)
        got = dot(nmt[...], low)
        for zz in range(4):
            for p in range(4):
                top = zz * part + p * (part // 4)
                out[p, zz ^ z, k * (part // 4) : (k + 1) * (part // 4), :] = got[top : top + part // 4].astype(bf16)
        gnm[...] += dot_nt(low, w[k, :, cols])


def mixer_back(idx, own, r1, r2, r3, prods, flows, decay, share, cand, du, dv, st, grad_states, nmt, w, mask,
               carried, send, gnm, small, others, carry8):
    length, units = decay.shape
    steps = length // chunks
    core, z = idx[0], idx[2]
    for j, ref in enumerate((own, r1, r2, r3)):
        others[j] = ref[...]
    flow = jnp.zeros((1, units), f32)
    for k in range(3, -1, -1):
        part = others[k ^ z]
        flow = jnp.where(k > z, flow * part[0:1] + part[1:2], flow)
    for k in range(chunks - 1, -1, -1):
        carry8[k : k + 1, :] = flow
        flow = flow * prods[k : k + 1, :] + flows[k : k + 1, :]

    def step(i, flow):
        rows = pl.ds(pl.multiple_of((steps - 1 - i) * chunks, chunks), chunks)
        got = grad_states[rows, :] + flow
        carried[rows, :] = got
        return got * decay[rows, :]

    lax.fori_loop(0, steps, step, carry8[...], unroll=8)
    gnm[...] = jnp.zeros_like(gnm)
    small[...] = jnp.zeros_like(small)
    gate_grads(1 - core, mask[...], carried, st, share, cand, du, dv, w, nmt, z, send, gnm, small)


def mixer_out(idx, carried, share, cand, du, dv, st, nmt, w, gnm0, small0, small1, gain_row, x, mask,
              keep, gnm, small):
    length, units = carried.shape
    core, z = idx[0], idx[2]
    gnm[...] = gnm0[...]
    small[...] = small0[...] + small1[...]
    gate_grads(core, mask[...], carried, st, share, cand, du, dv, w, nmt, z, keep, gnm, small)
    v = x[...]
    r = lax.rsqrt(jnp.mean(v * v, axis=-1, keepdims=True) + norm_eps)
    gains = jnp.sum(gnm[...] * (v * r), axis=0, keepdims=True)
    n = gains.shape[1] // 4
    for k in range(4):
        small[4 * k + 1 : 4 * k + 2, 0:n] = gains[:, k * n : (k + 1) * n]
        small[4 * k + 1 : 4 * k + 2, n : 2 * n] = gain_row[:, k * n : (k + 1) * n]


def tokens_out(gnm, x, gain, grad_mid, grad_tok, done, total, split):
    v = x[...]
    r = lax.rsqrt(jnp.mean(v * v, axis=-1, keepdims=True) + norm_eps)
    scaled = v * r
    gg = gnm[...] * gain[...]
    total[...] = grad_mid[...] + r * (gg - scaled * jnp.mean(gg * scaled, axis=-1, keepdims=True))
    from_chunked(total, split, grad_tok)
    done[...] = jnp.zeros_like(done)


def pick_piece(idx, wu, wd, out, sems):
    rows = wu.shape[0] // 8
    at = pl.ds(pl.multiple_of((idx[0] * 4 + idx[1]) * rows, rows), rows)
    for copy in fetch([(wu.at[at, :], out.at[pl.ds(0, rows), :]), (wd.at[at, :], out.at[pl.ds(rows, rows), :])], sems):
        copy.wait()


def gate(value, after):
    any_space = pl.BlockSpec(memory_space=pl.ANY)
    return pl.pallas_call(
        lambda *refs: None,
        out_shape=jax.ShapeDtypeStruct(value.shape, value.dtype),
        in_specs=[any_space, any_space],
        out_specs=any_space,
        input_output_aliases={0: 0},
        compiler_params=pltpu.CompilerParams(vmem_limit_bytes=1 << 20),
        name="gate",
    )(value, after)


def join(*refs):
    out, rows = refs[-1], refs[0].shape[0]
    for k, ref in enumerate(refs[:-1]):
        if len(out.shape) == 3:
            out[k] = ref[...]
        else:
            out[k * rows : (k + 1) * rows, :] = ref[...]


def two_terms(v):
    high = v.astype(bf16)
    return high, (v - high.astype(f32)).astype(bf16)


def add_pair(keep, got, out):
    out[...] = (keep[...].astype(f32) + got[...].astype(f32)).astype(bf16)


def add_core(idx, keep_a, got_a, more_a, keep_b, got_b, keep_c, got_c, send_x, send_y, own_x, own_y):
    x, y = idx[1] % 2, idx[1] // 2
    half = send_x.shape[1]

    def put(ref, k, p, first):
        top = 0
        for arrays in ((keep_a, got_a, more_a), (keep_b, got_b), (keep_c, got_c)):
            n = arrays[0].shape[1]
            low, high = max(first, top), min(first + half, top + n)
            if low < high:
                rows = slice(low - top, high - top)
                total = arrays[0][p, rows, :].astype(f32)
                for more in arrays[1:]:
                    total = total + more[p, rows, :].astype(f32)
                ref[k, low - first : high - first, :] = total.astype(ref.dtype)
            top += n

    for k in range(2):
        put(send_x, k, 2 * k + 1 - x, 0)
        put(own_x, k, 2 * k + x, 0)
        put(send_y, k, 2 * (1 - y) + k, half)
        put(own_y, k, 2 * y + k, half)


def add_cross(idx, own_x, got_x, own_y, got_y, send_y, send_x, out_x, out_y):
    x, y = idx[1] % 2, idx[1] // 2
    send_y[...] = (own_x[1 - y] + got_x[1 - y].astype(f32)).astype(bf16)
    out_x[...] = own_x[y] + got_x[y].astype(f32)
    send_x[...] = (own_y[1 - x] + got_y[1 - x].astype(f32)).astype(bf16)
    out_y[...] = own_y[x] + got_y[x].astype(f32)


def add_depth(own_x, got_x, own_y, got_y, send, own, total):
    half = own_x.shape[0]
    part = send.shape[0] // 6
    block = 4 * part
    total[0:half, :] = own_x[...] + got_x[...].astype(f32)
    total[half:, :] = own_y[...] + got_y[...].astype(f32)
    out = 3 * block
    for ref, to, at, n in ((send, 0, 2 * block, block), (send, block, out + part, part), (send, block + part, out + 3 * part, part),
                           (own, 0, 0, block), (own, block, out, part), (own, block + part, block, block), (own, 2 * block + part, out + 2 * part, part)):
        ref[to : to + n, :] = total[at : at + n, :].astype(ref.dtype)


def add_far(own, got, send, out):
    rows = out.shape[0]
    part = rows // 5
    block = 4 * part
    out[0:block, :] = own[0:block, :]
    out[block:, :] = own[block:rows, :] + got[block:rows, :].astype(f32)
    send[0:block, :] = (own[rows : rows + block, :] + got[0:block, :].astype(f32)).astype(bf16)
    send[block:, :] = (own[rows + block :, :] + got[rows:, :].astype(f32)).astype(bf16)


def add_last(own, got, out):
    out[...] = (own[...] + got[...].astype(f32)).astype(out.dtype)


def add_core_small(idx, keep, got, small, send_x, send_y, own_x, own_y, tiny):
    x, y = idx[1] % 2, idx[1] // 2
    half, n = own_x.shape[1], small.shape[0]
    high, low = two_terms(small[...])
    tiny[0:n, :] = high
    tiny[n:, :] = low
    send_x[2 * half : 2 * half + n, :] = high
    send_x[2 * half + n :, :] = low
    for k in range(2):
        at = slice(k * half, (k + 1) * half)
        p = 2 * k + 1 - x
        send_x[at, :] = (keep[p, 0:half, :].astype(f32) + got[p, 0:half, :].astype(f32)).astype(bf16)
        p = 2 * k + x
        own_x[k] = keep[p, 0:half, :].astype(f32) + got[p, 0:half, :].astype(f32)
        p = 2 * (1 - y) + k
        send_y[at, :] = (keep[p, half:, :].astype(f32) + got[p, half:, :].astype(f32)).astype(bf16)
        p = 2 * y + k
        own_y[k] = keep[p, half:, :].astype(f32) + got[p, half:, :].astype(f32)


def add_tiny(tiny, got, at):
    n = tiny.shape[0] // 2
    return (tiny[0:n, :].astype(f32) + tiny[n:, :].astype(f32)) + (
        got[at : at + n, :].astype(f32) + got[at + n : at + 2 * n, :].astype(f32)
    )


def add_cross_small(idx, own_x, got_x, own_y, got_y, tiny, send_y, send_x, out_x, out_y, tiny_out):
    x, y = idx[1] % 2, idx[1] // 2
    half, n = out_x.shape[0], tiny.shape[0] // 2
    high, low = two_terms(add_tiny(tiny, got_x, 2 * half))
    tiny_out[0:n, :] = high
    tiny_out[n:, :] = low
    send_y[half : half + n, :] = high
    send_y[half + n :, :] = low
    side = pl.ds(pl.multiple_of((1 - y) * half, half), half)
    send_y[0:half, :] = (own_x[1 - y] + got_x[side, :].astype(f32)).astype(bf16)
    side = pl.ds(pl.multiple_of(y * half, half), half)
    out_x[...] = own_x[y] + got_x[side, :].astype(f32)
    side = pl.ds(pl.multiple_of((1 - x) * half, half), half)
    send_x[...] = (own_y[1 - x] + got_y[side, :].astype(f32)).astype(bf16)
    side = pl.ds(pl.multiple_of(x * half, half), half)
    out_y[...] = own_y[x] + got_y[side, :].astype(f32)


def add_depth_small(idx, own_x, got_x, own_y, got_y, tiny, send, own, small):
    half, z = own_x.shape[0], idx[2]
    rows = half // 2
    total = add_tiny(tiny, got_x, half)
    n = total.shape[0] // 4
    small[...] = jnp.zeros_like(small)
    for k in range(4):
        small[k, 0:n, :] = total[k * n : (k + 1) * n]
    for j in range(4):
        own_ref, got = ((own_x, got_x), (own_y, got_y))[j // 2]
        at = slice((j % 2) * rows, (j % 2 + 1) * rows)
        value = own_ref[at, :] + got[at, :].astype(f32)
        base = (j // 2) * (rows + 16)
        if j % 2:
            send[base : base + rows, :] = value.astype(bf16)
            high, low = two_terms(small[z ^ j])
            send[base + rows : base + rows + 16, :] = jnp.concatenate([high, low], axis=0)
        else:
            own[(j // 2) * rows : (j // 2 + 1) * rows, :] = value


def add_far_small(idx, own, got, small, send, out, tiny_out):
    z = idx[2]
    rows, n = out.shape[0], tiny_out.shape[0]
    tiny = []
    for k in range(2):
        base = k * (rows + 16)
        mine = small[z ^ (2 * k)]
        other = got[base + rows : base + rows + 16, :].astype(f32)
        tiny.append(mine + (other[0:n] + other[n : 2 * n]))
    out[...] = own[0:rows, :] + got[0:rows, :].astype(f32)
    tiny_out[...] = tiny[0]
    send[0:rows, :] = (own[rows:, :] + got[rows + 16 : 2 * rows + 16, :].astype(f32)).astype(bf16)
    high, low = two_terms(tiny[1])
    send[rows:, :] = jnp.concatenate([high, low], axis=0)


def add_last_small(own, tiny, got, out, tiny_out):
    rows, n = own.shape[0], tiny.shape[0]
    out[...] = (own[...] + got[0:rows, :].astype(f32)).astype(out.dtype)
    other = got[rows:, :].astype(f32)
    tiny_out[...] = tiny[...] + (other[0:n] + other[n : 2 * n])


def spread_mlp(idx, near, far, up, down, w_out, done):
    rows = up.shape[0] // 8
    rows_out = w_out.shape[0] // 8
    for which, pieces in ((idx[0], near), (1 - idx[0], far)):
        for k in range(4):
            spot = which * 4 + (idx[1] ^ k)
            at = pl.ds(pl.multiple_of(spot * rows, rows), rows)
            up[at, :] = pieces[k, 0:rows, :].astype(f32)
            down[at, :] = pieces[k, rows : 2 * rows, :].astype(f32)
            w_out[pl.ds(pl.multiple_of(spot * rows_out, rows_out), rows_out), :] = pieces[k, 2 * rows :, :].astype(f32)
    done[...] = jnp.zeros_like(done)


def spread_mix(idx, tiny, tiny_far, near, far, out, bias_f, bias_i, gain_mix, gain_mlp, b_up):
    rows, half = out.shape[1] // 4, out.shape[2] // 2
    for which, pieces in ((idx[0], near), (1 - idx[0], far)):
        cols = pl.ds(pl.multiple_of(which * half, half), half)
        for k in range(4):
            at = pl.ds(pl.multiple_of((idx[1] ^ k) * rows, rows), rows)
            for i in range(3):
                out[i, at, cols] = pieces[k, i * rows : (i + 1) * rows, :].astype(f32)
    small = tiny[...] + tiny_far[...]
    n = bias_f.shape[1]
    bias_f[...] = small[0:1, 0:n]
    bias_i[...] = small[0:1, n:]
    n = gain_mix.shape[1]
    gain_mix[...] = small[1:2, 0:n]
    gain_mlp[...] = small[1:2, n : 2 * n]
    b_up[...] = small[2:3, :]


def swap(value, axis, bit):
    size = lax.axis_size(axis)
    return lax.ppermute(value, axis, [(i, i ^ bit) for i in range(size)])


def across(value, turn):
    size = lax.axis_size("dp")
    return lax.ppermute(value, "dp", [(i, i ^ (2 << ((i & 1) ^ turn))) for i in range(size)])


def on_device(tokens, gain_mix, w_mix, bias_forget, bias_input, w_out, gain_mlp, w_up, b_up, w_down, resets, cotangent):
    length, width = tokens.shape[1:]
    units = w_out.shape[0]
    ff = w_up.shape[1]
    dp, mp = lax.axis_size("dp"), lax.axis_size("mp")
    assert mp == 4 and dp % 8 == 0 and tokens.shape[0] == 1
    place = lax.axis_index("dp")
    idx = jnp.stack([place & 1, (place >> 1) & 3, lax.axis_index("mp")]).astype(jnp.int32)
    tok, cot = tokens[0], cotangent[0]
    w3 = w_mix.transpose(1, 0, 2)
    row = lambda v: v.reshape(1, -1)
    lanes = width // 128

    (piece,) = call(pick_piece, "pick_piece", (idx, w_up, w_down), [shape_of(bf16, width // 4, ff)],
                    [pltpu.SemaphoreType.DMA((2,))], hbm=2, limit=2)
    depth = [swap(piece, "mp", j) for j in (1, 2, 3)]

    wide = shape_of(f32, length, units)
    square = shape_of(f32, length, width)
    square16 = shape_of(bf16, length, width)
    edge = shape_of(f32, chunks, units)
    decay, share, cand, du, dv, nmt, x, prods, ends, payload, mask = call(
        mixer_in, "mixer_in",
        (idx, resets, tok, row(gain_mix), row(bias_forget), row(bias_input), row(b_up), w3),
        [wide] * 5 + [shape_of(bf16, width, length), square, edge, edge, shape_of(f32, 4, units), shape_of(f32, length, 1)],
        [pltpu.SMEM(resets.shape, jnp.int32), pltpu.VMEM((lanes, length, 128), f32), pltpu.VMEM((length, width), bf16), pltpu.VMEM((1, width), f32)]
        + [pltpu.VMEM((1, units), f32)] * 2 + [pltpu.VMEM((1, ff), f32), pltpu.VMEM((3, width, units), bf16),
                                              pltpu.SemaphoreType.DMA((6 + units // 256,))],
        hbm=7, after=(piece,),
    )
    ahead = [swap(payload, "mp", j) for j in (1, 2, 3)]
    around = lambda v: [v] + [swap(v, "dp", 2 * k) for k in (1, 2, 3)]
    mine = gate(depth[0], payload)
    (two,) = call(join, "join_depth", depth[1:], [shape_of(bf16, width // 2, ff)], smem=0, after=(payload,))
    (one_a,) = call(join, "join_one", (mine, across(mine, 0)), [shape_of(bf16, 2, width // 4, ff)], smem=0, after=(two, *ahead))
    far_two = across(two, 0)
    quarter = width // 8
    st, stT, middle, nm2, nm2t, cotp = call(
        mid_in, "mid_in",
        (idx, payload, *ahead, prods, ends, decay, share, cand, x, cot, w_out, row(gain_mlp)),
        [shape_of(f32, length + chunks, units), shape_of(bf16, units, length), square, square16, shape_of(bf16, width, length), square16],
        [pltpu.VMEM((lanes, length, 128), f32), pltpu.VMEM((4, 4, units), f32), pltpu.VMEM((chunks, units), f32), pltpu.VMEM((length, width), f32)],
    )
    (two_a,) = call(join, "join_two", (two, far_two), [shape_of(bf16, 2, width // 2, ff)], smem=0, after=(nm2,))
    two_b = across(two_a, 1)
    block = 2 * quarter
    pair = lambda dtype, rows: shape_of(dtype, 2, rows, width)
    weights = [pltpu.VMEM((ff, length), bf16), pltpu.VMEM((width, ff), bf16), pltpu.VMEM((ff, width), bf16)]
    grads = lambda rows: [square] * 2 + [shape_of(bf16, 4, rows, width)] * 2 + [shape_of(f32, 16, width)]
    one_b = gate(across(one_a, 1), nm2)
    mix, gn, keep0, send0, small_mlp = call(
        mlp_own, "mlp_own", (idx, w_up, w_down, row(b_up), middle, nm2, nm2t, cotp), grads(block), weights[:1], after=(two_a,),
    )
    mix, gn, keep_a, send_a, small_mlp = call(
        mlp_one, "mlp_one",
        (idx, one_a, one_b, swap(one_a, "dp", 1), swap(one_b, "dp", 1), ahead[0], mix, gn, small_mlp, nm2, nm2t, cotp), grads(block), weights,
    )
    (pair_a,) = call(add_pair, "add_pair", (keep_a, swap(send_a, "dp", 1)), [shape_of(bf16, 4, block, width)], smem=0)
    more_a = swap(pair_a, "mp", 1)
    mix, gn, keep, send, small_mlp = call(
        mlp_two, "mlp_two",
        (idx, two_a, two_b, swap(two_a, "dp", 1), swap(two_b, "dp", 1), ahead[1], ahead[2], mix, gn, small_mlp, nm2, nm2t, cotp),
        grads(2 * block), weights, after=(pair_a,),
    )
    got, got0 = swap(send, "dp", 1), swap(send0, "dp", 1)
    out_rows = units // 8
    keep_out, send_out, grad_mid, grad_states, payload, prods, flows, gain_row = call(
        mid_back, "mid_back",
        (idx, gn, cotp, middle, row(gain_mlp), stT, w_out, decay),
        [shape_of(bf16, 4, out_rows, width)] * 2 + [square, wide, shape_of(f32, 2, units), edge, edge, shape_of(f32, 1, width)],
    )
    payload = gate(payload, got)
    behind = [swap(payload, "mp", j) for j in (1, 2, 3)]

    half = (3 * block + out_rows) // 2
    send_x, send_y, own_x, own_y = call(add_core, "add_core", (idx, keep0, got0, more_a, keep, got, keep_out, swap(send_out, "dp", 1)),
                                        [pair(bf16, half)] * 2 + [pair(f32, half)] * 2)
    got_x, got_y = swap(send_x, "dp", 2), swap(send_y, "dp", 4)

    rows_m = 3 * width // 16
    carried, send, gnm, small = call(
        mixer_back, "mixer_back",
        (idx, payload, *behind, prods, flows, decay, share, cand, du, dv, st, grad_states, nmt, w3, mask),
        [wide, shape_of(bf16, 4, 4, rows_m, units // 2), square, shape_of(f32, 16, width)],
        [pltpu.VMEM((4, 2, units), f32), pltpu.VMEM((chunks, units), f32)], after=(own_x,),
    )
    flat = lambda v: v.reshape(4, -1, width)
    got = swap(send, "dp", 1)
    keep, gnm, small = call(
        mixer_out, "mixer_out",
        (idx, carried, share, cand, du, dv, st, nmt, w3, gnm, small, small_mlp, gain_row, x, mask),
        [shape_of(bf16, 4, 4, rows_m, units // 2), square, shape_of(f32, 16, width)],
    )
    half_m = 2 * rows_m
    one = lambda dtype, rows: shape_of(dtype, rows, width)
    send_mx, send_my, own_mx, own_my, tiny = call(
        add_core_small, "add_core_small", (idx, flat(keep), flat(got), small),
        [one(bf16, 2 * half_m + 32), one(bf16, 2 * half_m), pair(f32, half_m), pair(f32, half_m), one(bf16, 32)],
    )
    got_mx, got_my = swap(send_mx, "dp", 2), swap(send_my, "dp", 4)
    mark = shape_of(f32, 8, 128)
    grad_tok, done_tok = call(tokens_out, "tokens_out", (gnm, x, row(gain_mix), grad_mid), [square16, mark],
                       [pltpu.VMEM((length, width), f32), pltpu.VMEM((lanes, length, 128), f32)], smem=0, after=(own_mx,))
    mixed, done_mix = call(mixed_out, "mixed_out", (mix,), [square16, mark], [pltpu.VMEM((lanes, length, 128), f32)], smem=0, after=(own_mx,))

    send_y, send_x, own_x, own_y = call(add_cross, "add_cross", (idx, own_x, got_x, own_y, got_y),
                                        [one(bf16, half)] * 2 + [one(f32, half)] * 2, after=(own_mx,))
    got_x, got_y = swap(send_y, "dp", 4), swap(send_x, "dp", 2)
    send_my, send_mx, own_mx, own_my, tiny = call(
        add_cross_small, "add_cross_small", (idx, own_mx, got_mx, own_my, got_my, tiny),
        [one(bf16, half_m + 32), one(bf16, half_m), one(f32, half_m), one(f32, half_m), one(bf16, 32)],
        after=(own_x, done_mix, done_tok),
    )
    got_mx, got_my = swap(send_my, "dp", 4), swap(send_mx, "dp", 2)
    rows_f = block + units // 32
    send, own = call(add_depth, "add_depth", (own_x, got_x, own_y, got_y), [one(bf16, block + units // 16), one(f32, 2 * rows_f)],
                     [pltpu.VMEM((2 * half, width), f32)], smem=0, after=(own_mx,))
    got = swap(send, "mp", 1)
    send_m, own_m, small = call(
        add_depth_small, "add_depth_small", (idx, own_mx, got_mx, own_my, got_my, tiny),
        [one(bf16, 2 * rows_m + 32), one(f32, 2 * rows_m), shape_of(f32, 4, 8, width)], after=(own,),
    )
    got_m = swap(send_m, "mp", 1)
    send, own = call(add_far, "add_far", (own, got), [one(bf16, rows_f), one(f32, rows_f)], smem=0, after=(small,))
    got = swap(send, "mp", 2)
    send_m, own_m, tiny = call(
        add_far_small, "add_far_small", (idx, own_m, got_m, small),
        [one(bf16, rows_m + 16), one(f32, rows_m), one(f32, 8)], after=(own,),
    )
    got_m = swap(send_m, "mp", 2)
    groups = [[g * 8 + i for g in range(dp // 8)] for i in range(8)]

    def last(fn, name, operands, outs, after):
        if dp == 8:
            return call(fn, name, operands, outs, smem=0, after=after)
        done = call(fn, name, operands, [shape_of(f32, *o.shape) for o in outs], smem=0, after=after)
        return [lax.psum(v, "dp", axis_index_groups=groups).astype(o.dtype) for v, o in zip(done, outs)]

    (part,) = last(add_last, "add_last", (own, got), [one(bf16, rows_f)], (tiny,))
    near_f = around(part)
    part, tiny = last(add_last_small, "add_last_small", (own_m, tiny, got_m), [one(bf16, rows_m), one(f32, 8)], (part,))
    near_m = around(part)
    (near,) = call(join, "join_mlp", near_f, [shape_of(bf16, 4, rows_f, width)], smem=0, after=(part,))
    grad_up, grad_down, grad_out, done = call(
        spread_mlp, "spread_mlp", (idx, near, swap(near, "dp", 1)),
        [shape_of(f32, width, ff), shape_of(f32, ff, width), shape_of(f32, units // 4, width), mark],
    )
    (near,) = call(join, "join_mix", near_m, [shape_of(bf16, 4, rows_m, width)], smem=0)
    grad_mix, g_bf, g_bi, g_gain_mix, g_gain_mlp, g_bu = call(
        spread_mix, "spread_mix", (idx, tiny, swap(tiny, "dp", 1), near, swap(near, "dp", 1)),
        [shape_of(f32, 3, width // 4, units), shape_of(f32, 1, units // 4), shape_of(f32, 1, units // 4),
         shape_of(f32, 1, width // 4), shape_of(f32, 1, width // 4), shape_of(f32, 1, ff)],
        after=(done,),
    )
    return (
        mixed[None], grad_tok[None], g_gain_mix[0], grad_mix.transpose(1, 0, 2), g_bf[0], g_bi[0],
        grad_out, g_gain_mlp[0], grad_up, g_bu[0], grad_down,
    )


def solution(mesh):
    return jax.shard_map(
        on_device,
        mesh=mesh,
        in_specs=(P("dp", "mp", None), P(), P(), P(), P(), P(), P(), P(None, "mp"), P("mp"), P("mp", None), P("dp", None), P("dp", "mp", None)),
        out_specs=(P("dp", "mp", None), P("dp", "mp", None), P("mp"), P("mp", None, None), P("mp"), P("mp"), P("mp", None), P("mp"), P(None, "mp"), P("mp"), P("mp", None)),
        check_vma=False,
    )
```

```python
from functools import partial

import jax
import jax.numpy as jnp
from jax import lax
from jax.experimental import pallas as pl
from jax.experimental.pallas import tpu as pltpu
from jax.sharding import PartitionSpec as P

norm_eps = 1e-06
gelu_k = 0.7978845608028654
gelu_c = 0.044715
chunks = 8
f32 = jnp.float32
bf16 = jnp.bfloat16
VMEM = pl.BlockSpec(memory_space=pltpu.VMEM)
HBM = pl.BlockSpec(memory_space=pltpu.HBM)


weight = {
    "pick_piece": 4, "mixer_in": 32, "join_depth": 32, "join_one": 4, "mlp_one": 0, "join_two": 0, "mlp_two": 8, "mid_back": 8,
    "add_core": 32, "mixer_back": 0, "mixer_out": 0, "add_core_small": 0, "add_cross": 16, "mixed_out": 0, "tokens_out": 2,
    "add_cross_small": 16, "add_depth": 0, "add_near_small": 8, "add_far": 16, "add_far_small": 0, "add_last": 4,
    "add_last_small": 4, "join_mlp": 2, "join_mix": 16, "spread_mlp": 8, "spread_mix": 0, "add_pair": 8, "mid_in": 8,
    "mlp_own": 4,
}


def dot(a, b):
    return jnp.dot(a, b, preferred_element_type=f32)


def dot_nt(a, b):
    return lax.dot_general(a, b, (((1,), (1,)), ((), ())), preferred_element_type=f32)


def shape_of(dtype, *shape):
    return jax.ShapeDtypeStruct(shape, dtype)


def place():
    row = lax.axis_index("dp")
    return row & 1, (row >> 1) & 3, lax.axis_index("mp")


def call(body, name, operands, outs, scratch=(), limit=16, after=(), hbm=0):
    placed = operands[0] is None
    operands = operands[placed:]
    n, extra, cost = len(operands), len(after), weight[name]
    operands = [pltpu.with_memory_space_constraint(v, pltpu.HBM) if i < hbm else v for i, v in enumerate(operands)]

    def run(*refs):
        body(*((place(),) if placed else ()), *refs[:n], *refs[n + extra :])

    return pl.pallas_call(
        run,
        out_shape=outs,
        in_specs=[HBM] * hbm + [VMEM] * (n - hbm) + [pl.BlockSpec(memory_space=pl.ANY)] * extra,
        out_specs=[VMEM] * len(outs),
        scratch_shapes=list(scratch),
        compiler_params=pltpu.CompilerParams(vmem_limit_bytes=limit << 20),
        cost_estimate=pl.CostEstimate(flops=cost << 30, bytes_accessed=cost << 22, transcendentals=0),
        name=name,
    )(*operands, *after)


def to_chunked(src, split, put):
    length, width = src.shape
    steps = length // chunks
    for g in range(width // 128):
        cols = slice(g * 128, (g + 1) * 128)
        split[g] = src[:, cols].astype(f32)
        for s in range(steps):
            put(pl.ds(s * chunks, chunks), cols, split[g, pl.ds(s, chunks, stride=steps), :])


def from_chunked(values, split, out):
    length, width = out.shape
    steps = length // chunks
    for g in range(width // 128):
        cols = slice(g * 128, (g + 1) * 128)
        for s in range(steps):
            split[g, pl.ds(s, chunks, stride=steps), :] = values[s * chunks : (s + 1) * chunks, cols]
        out[:, cols] = split[g].astype(bf16)


def keep_mask(idx, resets, length):
    row = lax.broadcasted_iota(jnp.int32, (length, 1), 0)
    pos = idx[2] * length + (row % chunks) * (length // chunks) + row // chunks
    keep = jnp.ones((length, 1), f32)
    for i in range(3):
        keep = jnp.where(pos == resets[0, i], 0.0, keep)
    return keep


def fetch(pairs, sems):
    copies = [pltpu.make_async_copy(src, dst, sems.at[i]) for i, (src, dst) in enumerate(pairs)]
    for copy in copies:
        copy.start()
    return copies


def mixer_in(idx, res_hbm, tok_hbm, gain_hbm, bias_f_hbm, bias_i_hbm, b_up_hbm, w_hbm, decay, share, cand, du, dv, nmt, x, prods, ends, payload, mask,
             resets, split, tok, gain, bias_f, bias_i, b_up, w, sems):
    length, width = tok.shape
    units = bias_f.shape[1]
    steps = length // chunks
    block = 256
    pairs = [(tok_hbm, tok), (gain_hbm, gain), (bias_f_hbm, bias_f), (bias_i_hbm, bias_i), (b_up_hbm, b_up), (res_hbm, resets)]
    for h in range(0, units, block):
        sl = pl.ds(h, block)
        pairs.append((w_hbm.at[:, :, sl], w.at[:, :, sl]))
    copies = fetch(pairs, sems)
    for copy in copies[:6]:
        copy.wait()

    def put(rows, cols, values):
        x[rows, cols] = values

    to_chunked(tok, split, put)
    v = x[...]
    r = lax.rsqrt(jnp.mean(v * v, axis=-1, keepdims=True) + norm_eps)
    nm = (v * r * gain[...]).astype(bf16)
    nmt[...] = nm.T
    keep = keep_mask(idx, resets, length)
    mask[...] = keep
    for i, h in enumerate(range(0, units, block)):
        sl = pl.ds(h, block)
        copies[6 + i].wait()
        a = jnp.exp(jnp.minimum(-(dot(nm, w[0, :, sl]) + bias_f[:, sl]), 88.0))
        b = jnp.exp(jnp.minimum(-(dot(nm, w[1, :, sl]) + bias_i[:, sl]), 88.0))
        t = 1.0 / (2.0 + a + b)
        p = (1.0 + b) * t
        q = (1.0 + a) * t
        decay[:, sl] = p * keep
        share[:, sl] = q
        cand[:, sl] = dot(nm, w[2, :, sl])
        du[:, sl] = p * (a * t)
        dv[:, sl] = q * (b * t)

    def step(s, carry):
        prod, end = carry
        rows = pl.ds(pl.multiple_of(s * chunks, chunks), chunks)
        d = decay[rows, :]
        return prod * d, end * d + share[rows, :] * cand[rows, :]

    prod, end = lax.fori_loop(
        0, steps, step, (jnp.ones((chunks, units), f32), jnp.zeros((chunks, units), f32)), unroll=8
    )
    prods[...] = prod
    ends[...] = end
    total, state = prod[0:1], end[0:1]
    for k in range(1, chunks):
        total = total * prod[k : k + 1]
        state = state * prod[k : k + 1] + end[k : k + 1]
    payload[...] = jnp.zeros_like(payload)
    payload[0:1, :] = total
    payload[1:2, :] = state
    payload[2:3, 0 : b_up.shape[1]] = b_up[...]


def store_pieces(ref, base, rows, values):
    for p in range(4):
        ref[p, base : base + rows, :] = values[p * rows : (p + 1) * rows].astype(bf16)


def send_first(ref, core, values):
    n = values.shape[0] // 2
    ref[pl.ds(pl.multiple_of((1 - core) * n, n), n), :] = values[0:n]
    ref[pl.ds(pl.multiple_of(core * n, n), n), :] = values[n:]


def ffn_block(slot, core, nm, nmt, cot, wu, wd, bu, mix, gn, keep, send, hT):
    pre = dot(nm, wu[...]) + bu
    grad_act = dot_nt(cot, wd[...])
    sq = pre * pre
    t = jnp.tanh(pre * (gelu_k + gelu_k * gelu_c * sq))
    half = 0.5 + 0.5 * t
    h = pre * half
    slope = half + h * (1.0 - t) * (gelu_k + 3.0 * gelu_k * gelu_c * sq)
    grad_pre = grad_act * slope
    total = jnp.sum(grad_pre, axis=0, keepdims=True)
    h, g = h.astype(bf16), grad_pre.astype(bf16)
    send_first(hT, core, h.T)
    mix[...] += dot(h, wd[...])
    gn[...] += dot_nt(g, wu[...])
    n = nm.shape[1] // 2
    for base, got in ((0, dot(nmt[...], g)), (n // 4, dot(hT[...], cot))):
        store_pieces(send, slot * (n // 2) + base, n // 4, got[0:n])
        store_pieces(keep, slot * (n // 2) + base, n // 4, got[n:])
    return total


def mid_in(idx, own, r1, r2, r3, prods, ends, decay, share, cand, x, cot, w_out, gain,
           st, stT, middle, nm2, nm2t, cotp, split, others, carry8, square):
    length = x.shape[0]
    steps = length // chunks
    units = decay.shape[1]
    z = idx[2]
    for j, ref in enumerate((own, r1, r2, r3)):
        others[j] = ref[...]
    state = jnp.zeros((1, units), f32)
    for k in range(4):
        part = others[k ^ z]
        state = jnp.where(k < z, state * part[0:1] + part[1:2], state)
    for k in range(chunks):
        carry8[k : k + 1, :] = state
        state = state * prods[k : k + 1, :] + ends[k : k + 1, :]
    st[0:chunks, :] = carry8[...]

    def step(s, state):
        rows = pl.ds(pl.multiple_of(s * chunks, chunks), chunks)
        state = state * decay[rows, :] + share[rows, :] * cand[rows, :]
        st[pl.ds(pl.multiple_of(s * chunks + chunks, chunks), chunks), :] = state
        return state

    lax.fori_loop(0, steps, step, carry8[...], unroll=8)
    low = st[chunks:, :].astype(bf16)
    stT[...] = low.T
    mid = x[...] + dot(low, w_out[...])
    middle[...] = mid
    r = lax.rsqrt(jnp.mean(mid * mid, axis=-1, keepdims=True) + norm_eps)
    nm = (mid * r * gain[...]).astype(bf16)
    nm2[...] = nm
    send_first(nm2t, idx[0], nm.T)

    def put(rows, cols, values):
        square[rows, cols] = values

    to_chunked(cot, split, put)
    cotp[...] = square[...].astype(bf16)


def pieces_of(idx, near, near_far, far, far_far):
    for which, arrays in ((idx[0], (near, near_far)), (1 - idx[0], (far, far_far))):
        for k in range(2):
            for i in range(2):
                yield which, idx[1] ^ (i * (1 + which) + k * (2 - which)), arrays[k].at[i]


def lay_out(idx, arrays, at, wu, wd):
    rows = wu.shape[0] // 8
    for which, place, piece in pieces_of(idx, *arrays):
        spot = pl.ds(pl.multiple_of((which * 4 + place) * rows, rows), rows)
        wu[spot, :] = piece[at : at + rows, :]
        wd[spot, :] = piece[at + rows : at + 2 * rows, :]


def mlp_own(idx, wu, wd, bu, middle, nm2, nm2t, cotp, mix, gn, keep, send, small, hT):
    mix[...] = middle[...]
    gn[...] = jnp.zeros_like(gn)
    small[...] = jnp.zeros_like(small)
    small[pl.ds(4 * idx[2] + 2, 1), :] = ffn_block(
        0, idx[0], nm2[...], nm2t, cotp[...], wu, wd, bu[...], mix, gn, keep, send, hT
    )


def mlp_one(idx, n1, n2, f1, f2, bias, mix0, gn0, small0, nm2, nm2t, cotp, mix, gn, keep, send, small, hT, wu, wd):
    mix[...] = mix0[...]
    gn[...] = gn0[...]
    small[...] = small0[...]
    lay_out(idx, (n1, n2, f1, f2), 0, wu, wd)
    small[pl.ds(4 * (idx[2] ^ 1) + 2, 1), :] = ffn_block(
        0, idx[0], nm2[...], nm2t, cotp[...], wu, wd, bias[2:3, 0 : wu.shape[1]], mix, gn, keep, send, hT
    )


def mlp_two(idx, n1, n2, f1, f2, bias2, bias3, mix0, gn0, small0, nm2, nm2t, cotp, mix, gn, keep, send, small, hT, wu, wd):
    mix[...] = mix0[...]
    gn[...] = gn0[...]
    small[...] = small0[...]
    for slot, bias in enumerate((bias2, bias3)):
        lay_out(idx, (n1, n2, f1, f2), slot * wu.shape[0] // 4, wu, wd)
        small[pl.ds(4 * (idx[2] ^ (2 + slot)) + 2, 1), :] = ffn_block(
            slot, idx[0], nm2[...], nm2t, cotp[...], wu, wd, bias[2:3, 0 : wu.shape[1]], mix, gn, keep, send, hT
        )


def mid_back(idx, gn, cotp, middle, gain, stT, w_out, decay,
             keep, send, grad_mid, grad_states, payload, prods, flows, gain_row):
    core, z = idx[0], idx[2]
    length, units = decay.shape
    steps = length // chunks
    mid = middle[...]
    r = lax.rsqrt(jnp.mean(mid * mid, axis=-1, keepdims=True) + norm_eps)
    scaled = mid * r
    g = gn[...]
    gain_row[...] = jnp.sum(g * scaled, axis=0, keepdims=True)
    gg = g * gain[...]
    gm = cotp[...].astype(f32) + r * (gg - scaled * jnp.mean(gg * scaled, axis=-1, keepdims=True))
    grad_mid[...] = gm
    low = gm.astype(bf16)
    grad_states[...] = dot_nt(low, w_out[...])
    part = units // 8
    for k in range(4):
        for ref, which in ((send, 1 - core), (keep, core)):
            got = dot(stT[pl.ds(pl.multiple_of((2 * k + which) * part, part), part), :], low)
            at = pl.ds(pl.multiple_of((k ^ z) * (part // 4), part // 4), part // 4)
            for p in range(4):
                ref[p, at, :] = got[p * (part // 4) : (p + 1) * (part // 4)].astype(bf16)

    def step(i, carry):
        prod, flow = carry
        rows = pl.ds(pl.multiple_of((steps - 1 - i) * chunks, chunks), chunks)
        d = decay[rows, :]
        return prod * d, (flow + grad_states[rows, :]) * d

    prod, flow = lax.fori_loop(
        0, steps, step, (jnp.ones((chunks, units), f32), jnp.zeros((chunks, units), f32)), unroll=8
    )
    total, out = prod[chunks - 1 :], flow[chunks - 1 :]
    for k in range(chunks - 2, -1, -1):
        total = total * prod[k : k + 1]
        out = out * prod[k : k + 1] + flow[k : k + 1]
    payload[0:1, :] = total
    payload[1:2, :] = out
    prods[...] = prod
    flows[...] = flow


def mixed_out(mix, mixed, done, split):
    from_chunked(mix, split, mixed)
    done[...] = jnp.zeros_like(done)


def gate_grads(which, keep, carried, st, share, cand, du, dv, nmt, z, out, lows, small):
    length, units = carried.shape
    half = units // 2
    cols = pl.ds(pl.multiple_of(which * half, half), half)
    cf = carried[:, cols]
    q = share[:, cols]
    s = cf * (st[0:length, cols] * keep - cand[:, cols])
    ga = s * du[:, cols]
    gb = -(s * dv[:, cols])
    quarter = half // 2
    sum_a, sum_b = jnp.sum(ga, axis=0, keepdims=True), jnp.sum(gb, axis=0, keepdims=True)
    for i in range(2):
        at = pl.ds(4 * (2 * which + i), 1)
        small[at, 0:quarter] = sum_a[:, i * quarter : (i + 1) * quarter]
        small[at, quarter:] = sum_b[:, i * quarter : (i + 1) * quarter]
    part = nmt.shape[0] // 4
    for k, g in enumerate((ga, gb, cf * q)):
        lows[k] = g.astype(bf16)
        got = dot(nmt[...], lows[k])
        for zz in range(4):
            for p in range(4):
                top = zz * part + p * (part // 4)
                out[p, zz ^ z, k * (part // 4) : (k + 1) * (part // 4), :] = got[top : top + part // 4].astype(bf16)


def mixer_back(idx, own, r1, r2, r3, prods, flows, decay, share, cand, du, dv, st, grad_states, nmt, mask,
               carried, send, lows, small, others, carry8):
    length, units = decay.shape
    steps = length // chunks
    core, z = idx[0], idx[2]
    for j, ref in enumerate((own, r1, r2, r3)):
        others[j] = ref[...]
    flow = jnp.zeros((1, units), f32)
    for k in range(3, -1, -1):
        part = others[k ^ z]
        flow = jnp.where(k > z, flow * part[0:1] + part[1:2], flow)
    for k in range(chunks - 1, -1, -1):
        carry8[k : k + 1, :] = flow
        flow = flow * prods[k : k + 1, :] + flows[k : k + 1, :]

    def step(i, flow):
        rows = pl.ds(pl.multiple_of((steps - 1 - i) * chunks, chunks), chunks)
        got = grad_states[rows, :] + flow
        carried[rows, :] = got
        return got * decay[rows, :]

    lax.fori_loop(0, steps, step, carry8[...], unroll=8)
    small[...] = jnp.zeros_like(small)
    gate_grads(1 - core, mask[...], carried, st, share, cand, du, dv, nmt, z, send, lows, small)


def mixer_out(idx, carried, share, cand, du, dv, st, nmt, w, lows0, small0, small1, gain_row, x, mask,
              keep, gnm, small, lows):
    length, units = carried.shape
    core, z = idx[0], idx[2]
    small[...] = small0[...] + small1[...]
    gate_grads(core, mask[...], carried, st, share, cand, du, dv, nmt, z, keep, lows, small)
    half = units // 2
    total = jnp.zeros(gnm.shape, f32)
    for part, which in ((lows0, 1 - core), (lows, core)):
        cols = pl.ds(pl.multiple_of(which * half, half), half)
        for k in range(3):
            total = total + dot_nt(part[k], w[k, :, cols])
    gnm[...] = total
    v = x[...]
    r = lax.rsqrt(jnp.mean(v * v, axis=-1, keepdims=True) + norm_eps)
    gains = jnp.sum(gnm[...] * (v * r), axis=0, keepdims=True)
    n = gains.shape[1] // 4
    for k in range(4):
        small[4 * k + 1 : 4 * k + 2, 0:n] = gains[:, k * n : (k + 1) * n]
        small[4 * k + 1 : 4 * k + 2, n : 2 * n] = gain_row[:, k * n : (k + 1) * n]


def tokens_out(gnm, x, gain, grad_mid, grad_tok, done, total, split):
    v = x[...]
    r = lax.rsqrt(jnp.mean(v * v, axis=-1, keepdims=True) + norm_eps)
    scaled = v * r
    gg = gnm[...] * gain[...]
    total[...] = grad_mid[...] + r * (gg - scaled * jnp.mean(gg * scaled, axis=-1, keepdims=True))
    from_chunked(total, split, grad_tok)
    done[...] = jnp.zeros_like(done)


def pick_piece(idx, wu, wd, out, sems):
    rows = wu.shape[0] // 8
    at = pl.ds(pl.multiple_of((idx[0] * 4 + idx[1]) * rows, rows), rows)
    for copy in fetch([(wu.at[at, :], out.at[pl.ds(0, rows), :]), (wd.at[at, :], out.at[pl.ds(rows, rows), :])], sems):
        copy.wait()


def gate(value, after):
    any_space = pl.BlockSpec(memory_space=pl.ANY)
    return pl.pallas_call(
        lambda *refs: None,
        out_shape=jax.ShapeDtypeStruct(value.shape, value.dtype),
        in_specs=[any_space, any_space],
        out_specs=any_space,
        input_output_aliases={0: 0},
        compiler_params=pltpu.CompilerParams(vmem_limit_bytes=1 << 20),
        name="gate",
    )(value, after)


def join(*refs):
    out, rows = refs[-1], refs[0].shape[0]
    for k, ref in enumerate(refs[:-1]):
        if len(out.shape) == 3:
            out[k] = ref[...]
        else:
            out[k * rows : (k + 1) * rows, :] = ref[...]


def two_terms(v):
    high = v.astype(bf16)
    return high, (v - high.astype(f32)).astype(bf16)


def add_pair(keep, got, out):
    out[...] = (keep[...].astype(f32) + got[...].astype(f32)).astype(bf16)


def add_core(idx, keep_a, got_a, more_a, keep_b, got_b, keep_c, got_c, send_x, send_y, own_x, own_y):
    x, y = idx[1] % 2, idx[1] // 2
    half = send_x.shape[1]

    def put(ref, k, p, first):
        top = 0
        for arrays in ((keep_a, got_a, more_a), (keep_b, got_b), (keep_c, got_c)):
            n = arrays[0].shape[1]
            low, high = max(first, top), min(first + half, top + n)
            if low < high:
                rows = slice(low - top, high - top)
                total = arrays[0][p, rows, :].astype(f32)
                for more in arrays[1:]:
                    total = total + more[p, rows, :].astype(f32)
                ref[k, low - first : high - first, :] = total.astype(ref.dtype)
            top += n

    for k in range(2):
        put(send_x, k, 2 * k + 1 - x, 0)
        put(own_x, k, 2 * k + x, 0)
        put(send_y, k, 2 * (1 - y) + k, half)
        put(own_y, k, 2 * y + k, half)


def add_cross(idx, own_x, got_x, own_y, got_y, send_y, send_x, out_x, out_y):
    x, y = idx[1] % 2, idx[1] // 2
    send_y[...] = (own_x[1 - y] + got_x[1 - y].astype(f32)).astype(bf16)
    out_x[...] = own_x[y] + got_x[y].astype(f32)
    send_x[...] = (own_y[1 - x] + got_y[1 - x].astype(f32)).astype(bf16)
    out_y[...] = own_y[x] + got_y[x].astype(f32)


def add_depth(own_x, got_x, own_y, got_y, send, own, total):
    half = own_x.shape[0]
    part = send.shape[0] // 6
    block = 4 * part
    total[0:half, :] = own_x[...] + got_x[...].astype(f32)
    total[half:, :] = own_y[...] + got_y[...].astype(f32)
    out = 3 * block
    for ref, to, at, n in ((send, 0, 2 * block, block), (send, block, out + part, part), (send, block + part, out + 3 * part, part),
                           (own, 0, 0, block), (own, block, out, part), (own, block + part, block, block), (own, 2 * block + part, out + 2 * part, part)):
        ref[to : to + n, :] = total[at : at + n, :].astype(ref.dtype)


def add_far(own, got, send, out):
    rows = out.shape[0]
    part = rows // 5
    block = 4 * part
    out[0:block, :] = own[0:block, :]
    out[block:, :] = own[block:rows, :] + got[block:rows, :].astype(f32)
    send[0:block, :] = (own[rows : rows + block, :] + got[0:block, :].astype(f32)).astype(bf16)
    send[block:, :] = (own[rows + block :, :] + got[rows:, :].astype(f32)).astype(bf16)


def add_last(own, got, out):
    out[...] = (own[...] + got[...].astype(f32)).astype(out.dtype)


def add_core_small(idx, keep, got, small, send, own, tiny, slots):
    z = idx[2]
    rows = keep.shape[1] // 4
    n = small.shape[0] // 4
    slots[...] = jnp.zeros_like(slots)
    for k in range(4):
        slots[k, 0:n, :] = small[k * n : (k + 1) * n, :]
    for p in range(4):
        for j in range(4):
            at = slice(j * rows, (j + 1) * rows)
            total = keep[p, at, :].astype(f32) + got[p, at, :].astype(f32)
            base = j // 2 * rows
            if j % 2:
                send[p * 2 * rows + base : p * 2 * rows + base + rows, :] = total.astype(bf16)
            else:
                own[p, base : base + rows, :] = total
    for k in range(2):
        base = 8 * rows + 16 * k
        high, low = two_terms(slots[z ^ (2 * k + 1)])
        send[base : base + 16, :] = jnp.concatenate([high, low], axis=0)
        tiny[8 * k : 8 * k + 8, :] = slots[z ^ (2 * k)]


def add_near_small(idx, own, got, tiny, send_x, send_y, own_x, own_y, tiny_out):
    x, y = idx[1] % 2, idx[1] // 2
    rows = own.shape[1] // 2
    for k in range(2):
        base = 8 * rows + 16 * k
        other = got[base : base + 16, :].astype(f32)
        high, low = two_terms(tiny[8 * k : 8 * k + 8, :] + (other[0:8] + other[8:16]))
        for ref, top in ((tiny_out, 0), (send_x, 2 * rows)):
            ref[top + 8 * k : top + 8 * k + 8, :] = high
            ref[top + 16 + 8 * k : top + 24 + 8 * k, :] = low

    def total(p, slot):
        at = pl.ds(pl.multiple_of(p * 2 * rows + slot * rows, 16), rows)
        return own[p, slot * rows : (slot + 1) * rows, :] + got[at, :].astype(f32)

    for k in range(2):
        at = slice(k * rows, (k + 1) * rows)
        send_x[at, :] = total(2 * k + 1 - x, 0).astype(bf16)
        own_x[k] = total(2 * k + x, 0)
        send_y[at, :] = total(2 * (1 - y) + k, 1).astype(bf16)
        own_y[k] = total(2 * y + k, 1)


def add_tiny(tiny, got, at):
    n = tiny.shape[0] // 2
    return (tiny[0:n, :].astype(f32) + tiny[n:, :].astype(f32)) + (
        got[at : at + n, :].astype(f32) + got[at + n : at + 2 * n, :].astype(f32)
    )


def add_cross_small(idx, own_x, got_x, own_y, got_y, tiny, send_y, send_x, out_x, out_y, tiny_out):
    x, y = idx[1] % 2, idx[1] // 2
    half, n = out_x.shape[0], tiny.shape[0] // 2
    high, low = two_terms(add_tiny(tiny, got_x, 2 * half))
    tiny_out[0:n, :] = high
    tiny_out[n:, :] = low
    send_y[half : half + n, :] = high
    send_y[half + n :, :] = low
    side = pl.ds(pl.multiple_of((1 - y) * half, half), half)
    send_y[0:half, :] = (own_x[1 - y] + got_x[side, :].astype(f32)).astype(bf16)
    side = pl.ds(pl.multiple_of(y * half, half), half)
    out_x[...] = own_x[y] + got_x[side, :].astype(f32)
    side = pl.ds(pl.multiple_of((1 - x) * half, half), half)
    send_x[...] = (own_y[1 - x] + got_y[side, :].astype(f32)).astype(bf16)
    side = pl.ds(pl.multiple_of(x * half, half), half)
    out_y[...] = own_y[x] + got_y[side, :].astype(f32)


def add_far_small(own_x, got_x, own_y, got_y, tiny, send, out, tiny_out):
    rows = out.shape[0]
    total = add_tiny(tiny, got_x, rows)
    out[...] = own_x[...] + got_x[0:rows, :].astype(f32)
    tiny_out[...] = total[0:8]
    send[0:rows, :] = (own_y[...] + got_y[...].astype(f32)).astype(bf16)
    high, low = two_terms(total[8:16])
    send[rows:, :] = jnp.concatenate([high, low], axis=0)


def add_last_small(own, tiny, got, out, tiny_out):
    rows, n = own.shape[0], tiny.shape[0]
    out[...] = (own[...] + got[0:rows, :].astype(f32)).astype(out.dtype)
    other = got[rows:, :].astype(f32)
    tiny_out[...] = tiny[...] + (other[0:n] + other[n : 2 * n])


def spread_mlp(idx, near, far, up, down, w_out, done):
    rows = up.shape[0] // 8
    rows_out = w_out.shape[0] // 8
    for which, pieces in ((idx[0], near), (1 - idx[0], far)):
        for k in range(4):
            spot = which * 4 + (idx[1] ^ k)
            at = pl.ds(pl.multiple_of(spot * rows, rows), rows)
            up[at, :] = pieces[k, 0:rows, :].astype(f32)
            down[at, :] = pieces[k, rows : 2 * rows, :].astype(f32)
            w_out[pl.ds(pl.multiple_of(spot * rows_out, rows_out), rows_out), :] = pieces[k, 2 * rows :, :].astype(f32)
    done[...] = jnp.zeros_like(done)


def spread_mix(idx, tiny, tiny_far, near, far, out, bias_f, bias_i, gain_mix, gain_mlp, b_up):
    rows, half = out.shape[1] // 4, out.shape[2] // 2
    for which, pieces in ((idx[0], near), (1 - idx[0], far)):
        cols = pl.ds(pl.multiple_of(which * half, half), half)
        for k in range(4):
            at = pl.ds(pl.multiple_of((idx[1] ^ k) * rows, rows), rows)
            for i in range(3):
                out[i, at, cols] = pieces[k, i * rows : (i + 1) * rows, :].astype(f32)
    small = tiny[...] + tiny_far[...]
    n = bias_f.shape[1]
    bias_f[...] = small[0:1, 0:n]
    bias_i[...] = small[0:1, n:]
    n = gain_mix.shape[1]
    gain_mix[...] = small[1:2, 0:n]
    gain_mlp[...] = small[1:2, n : 2 * n]
    b_up[...] = small[2:3, :]


def swap(value, axis, bit):
    size = lax.axis_size(axis)
    return lax.ppermute(value, axis, [(i, i ^ bit) for i in range(size)])


def across(value, turn):
    size = lax.axis_size("dp")
    return lax.ppermute(value, "dp", [(i, i ^ (2 << ((i & 1) ^ turn))) for i in range(size)])


def on_device(tokens, gain_mix, w_mix, bias_forget, bias_input, w_out, gain_mlp, w_up, b_up, w_down, resets, cotangent):
    length, width = tokens.shape[1:]
    units = w_out.shape[0]
    ff = w_up.shape[1]
    dp, mp = lax.axis_size("dp"), lax.axis_size("mp")
    assert mp == 4 and dp % 8 == 0 and tokens.shape[0] == 1
    idx = None
    tok, cot = tokens[0], cotangent[0]
    w3 = w_mix.transpose(1, 0, 2)
    row = lambda v: v.reshape(1, -1)
    lanes = width // 128

    (piece,) = call(pick_piece, "pick_piece", (idx, w_up, w_down), [shape_of(bf16, width // 4, ff)],
                    [pltpu.SemaphoreType.DMA((2,))], hbm=2, limit=2)
    depth = [swap(piece, "mp", j) for j in (1, 2, 3)]

    wide = shape_of(f32, length, units)
    square = shape_of(f32, length, width)
    square16 = shape_of(bf16, length, width)
    edge = shape_of(f32, chunks, units)
    decay, share, cand, du, dv, nmt, x, prods, ends, payload, mask = call(
        mixer_in, "mixer_in",
        (idx, resets, tok, row(gain_mix), row(bias_forget), row(bias_input), row(b_up), w3),
        [wide] * 5 + [shape_of(bf16, width, length), square, edge, edge, shape_of(f32, 4, units), shape_of(f32, length, 1)],
        [pltpu.SMEM(resets.shape, jnp.int32), pltpu.VMEM((lanes, length, 128), f32), pltpu.VMEM((length, width), bf16), pltpu.VMEM((1, width), f32)]
        + [pltpu.VMEM((1, units), f32)] * 2 + [pltpu.VMEM((1, ff), f32), pltpu.VMEM((3, width, units), bf16),
                                              pltpu.SemaphoreType.DMA((6 + units // 256,))],
        hbm=7, after=(piece,),
    )
    ahead = [swap(payload, "mp", j) for j in (1, 2, 3)]
    around = lambda v: [v] + [swap(v, "dp", 2 * k) for k in (1, 2, 3)]
    mine = gate(depth[0], payload)
    (two,) = call(join, "join_depth", depth[1:], [shape_of(bf16, width // 2, ff)], after=(payload,))
    (one_a,) = call(join, "join_one", (mine, across(mine, 0)), [shape_of(bf16, 2, width // 4, ff)], after=(two, *ahead))
    far_two = across(two, 0)
    quarter = width // 8
    st, stT, middle, nm2, nm2t, cotp = call(
        mid_in, "mid_in",
        (idx, payload, *ahead, prods, ends, decay, share, cand, x, cot, w_out, row(gain_mlp)),
        [shape_of(f32, length + chunks, units), shape_of(bf16, units, length), square, square16, shape_of(bf16, width, length), square16],
        [pltpu.VMEM((lanes, length, 128), f32), pltpu.VMEM((4, 4, units), f32), pltpu.VMEM((chunks, units), f32), pltpu.VMEM((length, width), f32)],
    )
    (two_a,) = call(join, "join_two", (two, far_two), [shape_of(bf16, 2, width // 2, ff)], after=(nm2,))
    two_b = across(two_a, 1)
    block = 2 * quarter
    pair = lambda dtype, rows: shape_of(dtype, 2, rows, width)
    weights = [pltpu.VMEM((ff, length), bf16), pltpu.VMEM((width, ff), bf16), pltpu.VMEM((ff, width), bf16)]
    grads = lambda rows: [square] * 2 + [shape_of(bf16, 4, rows, width)] * 2 + [shape_of(f32, 16, width)]
    one_b = gate(across(one_a, 1), nm2)
    mix, gn, keep0, send0, small_mlp = call(
        mlp_own, "mlp_own", (idx, w_up, w_down, row(b_up), middle, nm2, nm2t, cotp), grads(block), weights[:1], after=(two_a,),
    )
    mix, gn, keep_a, send_a, small_mlp = call(
        mlp_one, "mlp_one",
        (idx, one_a, one_b, swap(one_a, "dp", 1), swap(one_b, "dp", 1), ahead[0], mix, gn, small_mlp, nm2, nm2t, cotp), grads(block), weights,
    )
    (pair_a,) = call(add_pair, "add_pair", (keep_a, swap(send_a, "dp", 1)), [shape_of(bf16, 4, block, width)])
    more_a = swap(pair_a, "mp", 1)
    mix, gn, keep, send, small_mlp = call(
        mlp_two, "mlp_two",
        (idx, two_a, two_b, swap(two_a, "dp", 1), swap(two_b, "dp", 1), ahead[1], ahead[2], mix, gn, small_mlp, nm2, nm2t, cotp),
        grads(2 * block), weights, after=(pair_a,),
    )
    got, got0 = swap(send, "dp", 1), swap(send0, "dp", 1)
    out_rows = units // 8
    keep_out, send_out, grad_mid, grad_states, payload, prods, flows, gain_row = call(
        mid_back, "mid_back",
        (idx, gn, cotp, middle, row(gain_mlp), stT, w_out, decay),
        [shape_of(bf16, 4, out_rows, width)] * 2 + [square, wide, shape_of(f32, 2, units), edge, edge, shape_of(f32, 1, width)],
    )
    payload = gate(payload, got)
    behind = [swap(payload, "mp", j) for j in (1, 2, 3)]

    half = (3 * block + out_rows) // 2
    send_x, send_y, own_x, own_y = call(add_core, "add_core", (idx, keep0, got0, more_a, keep, got, keep_out, swap(send_out, "dp", 1)),
                                        [pair(bf16, half)] * 2 + [pair(f32, half)] * 2)
    got_x, got_y = swap(send_x, "dp", 2), swap(send_y, "dp", 4)

    rows_m = 3 * width // 16
    carried, send, lows, small = call(
        mixer_back, "mixer_back",
        (idx, payload, *behind, prods, flows, decay, share, cand, du, dv, st, grad_states, nmt, mask),
        [wide, shape_of(bf16, 4, 4, rows_m, units // 2), shape_of(bf16, 3, length, units // 2), shape_of(f32, 16, width)],
        [pltpu.VMEM((4, 2, units), f32), pltpu.VMEM((chunks, units), f32)], after=(own_x,),
    )
    flat = lambda v: v.reshape(4, -1, width)
    got = swap(send, "dp", 1)
    keep, gnm, small = call(
        mixer_out, "mixer_out",
        (idx, carried, share, cand, du, dv, st, nmt, w3, lows, small, small_mlp, gain_row, x, mask),
        [shape_of(bf16, 4, 4, rows_m, units // 2), square, shape_of(f32, 16, width)],
        [pltpu.VMEM((3, length, units // 2), bf16)],
    )
    one = lambda dtype, rows: shape_of(dtype, rows, width)
    send_m, own_m, tiny = call(
        add_core_small, "add_core_small", (idx, flat(keep), flat(got), small),
        [one(bf16, 8 * rows_m + 32), shape_of(f32, 4, 2 * rows_m, width), one(f32, 16)], [pltpu.VMEM((4, 8, width), f32)],
    )
    got_m = swap(send_m, "mp", 1)
    mark = shape_of(f32, 8, 128)
    grad_tok, done_tok = call(tokens_out, "tokens_out", (gnm, x, row(gain_mix), grad_mid), [square16, mark],
                       [pltpu.VMEM((length, width), f32), pltpu.VMEM((lanes, length, 128), f32)], after=(own_m,))
    mixed, done_mix = call(mixed_out, "mixed_out", (mix,), [square16, mark], [pltpu.VMEM((lanes, length, 128), f32)], after=(own_m,))

    send_y, send_x, own_x, own_y = call(add_cross, "add_cross", (idx, own_x, got_x, own_y, got_y),
                                        [one(bf16, half)] * 2 + [one(f32, half)] * 2, after=(own_m,))
    got_x, got_y = swap(send_y, "dp", 4), swap(send_x, "dp", 2)
    rows_f = block + units // 32
    send, own = call(add_depth, "add_depth", (own_x, got_x, own_y, got_y), [one(bf16, block + units // 16), one(f32, 2 * rows_f)],
                     [pltpu.VMEM((2 * half, width), f32)])
    got = swap(send, "mp", 1)
    send_mx, send_my, own_mx, own_my, tiny = call(
        add_near_small, "add_near_small", (idx, own_m, got_m, tiny),
        [one(bf16, 2 * rows_m + 32), one(bf16, 2 * rows_m), pair(f32, rows_m), pair(f32, rows_m), one(bf16, 32)],
        after=(own, done_mix, done_tok),
    )
    got_mx, got_my = swap(send_mx, "dp", 2), swap(send_my, "dp", 4)
    send, own = call(add_far, "add_far", (own, got), [one(bf16, rows_f), one(f32, rows_f)], after=(tiny,))
    got = swap(send, "mp", 2)
    send_my, send_mx, own_mx, own_my, tiny = call(
        add_cross_small, "add_cross_small", (idx, own_mx, got_mx, own_my, got_my, tiny),
        [one(bf16, rows_m + 32), one(bf16, rows_m), one(f32, rows_m), one(f32, rows_m), one(bf16, 32)], after=(own,),
    )
    got_mx, got_my = swap(send_my, "dp", 4), swap(send_mx, "dp", 2)
    send_m, own_m, tiny = call(
        add_far_small, "add_far_small", (own_mx, got_mx, own_my, got_my, tiny), [one(bf16, rows_m + 16), one(f32, rows_m), one(f32, 8)],
    )
    got_m = swap(send_m, "mp", 2)
    groups = [[g * 8 + i for g in range(dp // 8)] for i in range(8)]

    def last(fn, name, operands, outs, after):
        if dp == 8:
            return call(fn, name, operands, outs, after=after)
        done = call(fn, name, operands, [shape_of(f32, *o.shape) for o in outs], after=after)
        return [lax.psum(v, "dp", axis_index_groups=groups).astype(o.dtype) for v, o in zip(done, outs)]

    (part,) = last(add_last, "add_last", (own, got), [one(bf16, rows_f)], (tiny,))
    near_f = around(part)
    part, tiny = last(add_last_small, "add_last_small", (own_m, tiny, got_m), [one(bf16, rows_m), one(f32, 8)], (part,))
    near_m = around(part)
    (near,) = call(join, "join_mlp", near_f, [shape_of(bf16, 4, rows_f, width)], after=(part,))
    grad_up, grad_down, grad_out, done = call(
        spread_mlp, "spread_mlp", (idx, near, swap(near, "dp", 1)),
        [shape_of(f32, width, ff), shape_of(f32, ff, width), shape_of(f32, units // 4, width), mark],
    )
    (near,) = call(join, "join_mix", near_m, [shape_of(bf16, 4, rows_m, width)])
    grad_mix, g_bf, g_bi, g_gain_mix, g_gain_mlp, g_bu = call(
        spread_mix, "spread_mix", (idx, tiny, swap(tiny, "dp", 1), near, swap(near, "dp", 1)),
        [shape_of(f32, 3, width // 4, units), shape_of(f32, 1, units // 4), shape_of(f32, 1, units // 4),
         shape_of(f32, 1, width // 4), shape_of(f32, 1, width // 4), shape_of(f32, 1, ff)],
        after=(done,),
    )
    return (
        mixed[None], grad_tok[None], g_gain_mix[0], grad_mix.transpose(1, 0, 2), g_bf[0], g_bi[0],
        grad_out, g_gain_mlp[0], grad_up, g_bu[0], grad_down,
    )


def solution(mesh):
    return jax.shard_map(
        on_device,
        mesh=mesh,
        in_specs=(P("dp", "mp", None), P(), P(), P(), P(), P(), P(), P(None, "mp"), P("mp"), P("mp", None), P("dp", None), P("dp", "mp", None)),
        out_specs=(P("dp", "mp", None), P("dp", "mp", None), P("mp"), P("mp", None, None), P("mp"), P("mp"), P("mp", None), P("mp"), P(None, "mp"), P("mp"), P("mp", None)),
        check_vma=False,
    )
```

```python
from functools import partial

import jax
import jax.numpy as jnp
from jax import lax
from jax.experimental import pallas as pl
from jax.experimental.pallas import tpu as pltpu
from jax.sharding import PartitionSpec as P

norm_eps = 1e-06
gelu_k = 0.7978845608028654
gelu_c = 0.044715
chunks = 8
f32 = jnp.float32
bf16 = jnp.bfloat16
VMEM = pl.BlockSpec(memory_space=pltpu.VMEM)
HBM = pl.BlockSpec(memory_space=pltpu.HBM)


weight = {
    "pick_piece": 16, "mixer_in": 0, "join_depth": 0, "join_one": 4, "mlp_one": 4, "join_two": 2, "mlp_two": 8, "mid_back": 8,
    "add_core": 0, "mixer_back": 0, "mixer_out": 0, "add_core_small": 0, "add_cross": 4, "mixed_out": 0, "tokens_out": 8,
    "add_cross_small": 8, "add_depth": 0, "add_near_small": 32, "add_far": 16, "add_far_small": 0, "add_last": 4,
    "add_last_small": 4, "join_mlp": 32, "join_mix": 16, "spread_mlp": 8, "spread_mix": 32, "add_pair": 32, "mid_in": 8,
    "mlp_own": 4,
}


def dot(a, b):
    return jnp.dot(a, b, preferred_element_type=f32)


def dot_nt(a, b):
    return lax.dot_general(a, b, (((1,), (1,)), ((), ())), preferred_element_type=f32)


def shape_of(dtype, *shape):
    return jax.ShapeDtypeStruct(shape, dtype)


def place():
    row = lax.axis_index("dp")
    return row & 1, (row >> 1) & 3, lax.axis_index("mp")


def call(body, name, operands, outs, scratch=(), limit=16, after=(), hbm=0):
    placed = operands[0] is None
    operands = operands[placed:]
    n, extra, cost = len(operands), len(after), weight[name]
    operands = [pltpu.with_memory_space_constraint(v, pltpu.HBM) if i < hbm else v for i, v in enumerate(operands)]

    def run(*refs):
        body(*((place(),) if placed else ()), *refs[:n], *refs[n + extra :])

    return pl.pallas_call(
        run,
        out_shape=outs,
        in_specs=[HBM] * hbm + [VMEM] * (n - hbm) + [pl.BlockSpec(memory_space=pl.ANY)] * extra,
        out_specs=[VMEM] * len(outs),
        scratch_shapes=list(scratch),
        compiler_params=pltpu.CompilerParams(vmem_limit_bytes=limit << 20),
        cost_estimate=pl.CostEstimate(flops=cost << 30, bytes_accessed=cost << 22, transcendentals=0),
        name=name,
    )(*operands, *after)


def to_chunked(src, split, put):
    length, width = src.shape
    steps = length // chunks
    for g in range(width // 128):
        cols = slice(g * 128, (g + 1) * 128)
        split[g] = src[:, cols].astype(f32)
        for s in range(steps):
            put(pl.ds(s * chunks, chunks), cols, split[g, pl.ds(s, chunks, stride=steps), :])


def from_chunked(values, split, out):
    length, width = out.shape
    steps = length // chunks
    for g in range(width // 128):
        cols = slice(g * 128, (g + 1) * 128)
        for s in range(steps):
            split[g, pl.ds(s, chunks, stride=steps), :] = values[s * chunks : (s + 1) * chunks, cols]
        out[:, cols] = split[g].astype(bf16)


def keep_mask(idx, resets, length):
    row = lax.broadcasted_iota(jnp.int32, (length, 1), 0)
    pos = idx[2] * length + (row % chunks) * (length // chunks) + row // chunks
    keep = jnp.ones((length, 1), f32)
    for i in range(3):
        keep = jnp.where(pos == resets[0, i], 0.0, keep)
    return keep


def fetch(pairs, sems):
    copies = [pltpu.make_async_copy(src, dst, sems.at[i]) for i, (src, dst) in enumerate(pairs)]
    for copy in copies:
        copy.start()
    return copies


def mixer_in(idx, res_hbm, tok_hbm, gain_hbm, bias_f_hbm, bias_i_hbm, b_up_hbm, w_hbm, decay, share, cand, du, dv, nmt, x, prods, ends, payload, mask,
             resets, split, tok, gain, bias_f, bias_i, b_up, w, sems):
    length, width = tok.shape
    units = bias_f.shape[1]
    steps = length // chunks
    block = 256
    pairs = [(tok_hbm, tok), (gain_hbm, gain), (bias_f_hbm, bias_f), (bias_i_hbm, bias_i), (b_up_hbm, b_up), (res_hbm, resets)]
    for h in range(0, units, block):
        sl = pl.ds(h, block)
        pairs.append((w_hbm.at[:, :, sl], w.at[:, :, sl]))
    copies = fetch(pairs, sems)
    for copy in copies[:6]:
        copy.wait()

    def put(rows, cols, values):
        x[rows, cols] = values

    to_chunked(tok, split, put)
    v = x[...]
    r = lax.rsqrt(jnp.mean(v * v, axis=-1, keepdims=True) + norm_eps)
    nm = (v * r * gain[...]).astype(bf16)
    nmt[...] = nm.T
    keep = keep_mask(idx, resets, length)
    mask[...] = keep
    for i, h in enumerate(range(0, units, block)):
        sl = pl.ds(h, block)
        copies[6 + i].wait()
        a = jnp.exp(jnp.minimum(-(dot(nm, w[0, :, sl]) + bias_f[:, sl]), 88.0))
        b = jnp.exp(jnp.minimum(-(dot(nm, w[1, :, sl]) + bias_i[:, sl]), 88.0))
        t = 1.0 / (2.0 + a + b)
        p = (1.0 + b) * t
        q = (1.0 + a) * t
        decay[:, sl] = p * keep
        share[:, sl] = q
        cand[:, sl] = dot(nm, w[2, :, sl])
        du[:, sl] = p * (a * t)
        dv[:, sl] = q * (b * t)

    def step(s, carry):
        prod, end = carry
        rows = pl.ds(pl.multiple_of(s * chunks, chunks), chunks)
        d = decay[rows, :]
        return prod * d, end * d + share[rows, :] * cand[rows, :]

    prod, end = lax.fori_loop(
        0, steps, step, (jnp.ones((chunks, units), f32), jnp.zeros((chunks, units), f32)), unroll=8
    )
    prods[...] = prod
    ends[...] = end
    total, state = prod[0:1], end[0:1]
    for k in range(1, chunks):
        total = total * prod[k : k + 1]
        state = state * prod[k : k + 1] + end[k : k + 1]
    payload[...] = jnp.zeros_like(payload)
    payload[0:1, :] = total
    payload[1:2, :] = state
    payload[2:3, 0 : b_up.shape[1]] = b_up[...]


def store_pieces(ref, base, rows, values):
    for p in range(4):
        ref[p, base : base + rows, :] = values[p * rows : (p + 1) * rows].astype(bf16)


def send_first(ref, core, values):
    n = values.shape[0] // 2
    ref[pl.ds(pl.multiple_of((1 - core) * n, n), n), :] = values[0:n]
    ref[pl.ds(pl.multiple_of(core * n, n), n), :] = values[n:]


def ffn_block(slot, core, nm, nmt, cot, wu, wd, bu, mix, gn, keep, send, hT):
    pre = dot(nm, wu[...]) + bu
    grad_act = dot_nt(cot, wd[...])
    sq = pre * pre
    t = jnp.tanh(pre * (gelu_k + gelu_k * gelu_c * sq))
    half = 0.5 + 0.5 * t
    h = pre * half
    slope = half + h * (1.0 - t) * (gelu_k + 3.0 * gelu_k * gelu_c * sq)
    grad_pre = grad_act * slope
    total = jnp.sum(grad_pre, axis=0, keepdims=True)
    h, g = h.astype(bf16), grad_pre.astype(bf16)
    send_first(hT, core, h.T)
    mix[...] += dot(h, wd[...])
    gn[...] += dot_nt(g, wu[...])
    n = nm.shape[1] // 2
    for base, got in ((0, dot(nmt[...], g)), (n // 4, dot(hT[...], cot))):
        store_pieces(send, slot * (n // 2) + base, n // 4, got[0:n])
        store_pieces(keep, slot * (n // 2) + base, n // 4, got[n:])
    return total


def mid_in(idx, own, r1, r2, r3, prods, ends, decay, share, cand, x, cot, w_out, gain,
           st, stT, middle, nm2, nm2t, cotp, split, others, carry8, square):
    length = x.shape[0]
    steps = length // chunks
    units = decay.shape[1]
    z = idx[2]
    for j, ref in enumerate((own, r1, r2, r3)):
        others[j] = ref[...]
    state = jnp.zeros((1, units), f32)
    for k in range(4):
        part = others[k ^ z]
        state = jnp.where(k < z, state * part[0:1] + part[1:2], state)
    for k in range(chunks):
        carry8[k : k + 1, :] = state
        state = state * prods[k : k + 1, :] + ends[k : k + 1, :]
    st[0:chunks, :] = carry8[...]

    def step(s, state):
        rows = pl.ds(pl.multiple_of(s * chunks, chunks), chunks)
        state = state * decay[rows, :] + share[rows, :] * cand[rows, :]
        st[pl.ds(pl.multiple_of(s * chunks + chunks, chunks), chunks), :] = state
        return state

    lax.fori_loop(0, steps, step, carry8[...], unroll=8)
    low = st[chunks:, :].astype(bf16)
    stT[...] = low.T
    mid = x[...] + dot(low, w_out[...])
    middle[...] = mid
    r = lax.rsqrt(jnp.mean(mid * mid, axis=-1, keepdims=True) + norm_eps)
    nm = (mid * r * gain[...]).astype(bf16)
    nm2[...] = nm
    send_first(nm2t, idx[0], nm.T)

    def put(rows, cols, values):
        square[rows, cols] = values

    to_chunked(cot, split, put)
    cotp[...] = square[...].astype(bf16)


def pieces_of(idx, near, near_far, far, far_far):
    for which, arrays in ((idx[0], (near, near_far)), (1 - idx[0], (far, far_far))):
        for k in range(2):
            for i in range(2):
                yield which, idx[1] ^ (i * (1 + which) + k * (2 - which)), arrays[k].at[i]


def lay_out(idx, arrays, at, wu, wd):
    rows = wu.shape[0] // 8
    for which, place, piece in pieces_of(idx, *arrays):
        spot = pl.ds(pl.multiple_of((which * 4 + place) * rows, rows), rows)
        wu[spot, :] = piece[at : at + rows, :]
        wd[spot, :] = piece[at + rows : at + 2 * rows, :]


def mlp_own(idx, wu, wd, bu, middle, nm2, nm2t, cotp, mix, gn, keep, send, small, hT):
    mix[...] = middle[...]
    gn[...] = jnp.zeros_like(gn)
    small[...] = jnp.zeros_like(small)
    small[pl.ds(4 * idx[2] + 2, 1), :] = ffn_block(
        0, idx[0], nm2[...], nm2t, cotp[...], wu, wd, bu[...], mix, gn, keep, send, hT
    )


def mlp_one(idx, n1, n2, f1, f2, bias, mix0, gn0, small0, nm2, nm2t, cotp, mix, gn, keep, send, small, hT, wu, wd):
    mix[...] = mix0[...]
    gn[...] = gn0[...]
    small[...] = small0[...]
    lay_out(idx, (n1, n2, f1, f2), 0, wu, wd)
    small[pl.ds(4 * (idx[2] ^ 1) + 2, 1), :] = ffn_block(
        0, idx[0], nm2[...], nm2t, cotp[...], wu, wd, bias[2:3, 0 : wu.shape[1]], mix, gn, keep, send, hT
    )


def mlp_two(idx, n1, n2, f1, f2, bias2, bias3, mix0, gn0, small0, nm2, nm2t, cotp, mix, gn, keep, send, small, hT, wu, wd):
    mix[...] = mix0[...]
    gn[...] = gn0[...]
    small[...] = small0[...]
    for slot, bias in enumerate((bias2, bias3)):
        lay_out(idx, (n1, n2, f1, f2), slot * wu.shape[0] // 4, wu, wd)
        small[pl.ds(4 * (idx[2] ^ (2 + slot)) + 2, 1), :] = ffn_block(
            slot, idx[0], nm2[...], nm2t, cotp[...], wu, wd, bias[2:3, 0 : wu.shape[1]], mix, gn, keep, send, hT
        )


def mid_back(idx, gn, cotp, middle, gain, stT, w_out, decay,
             keep, send, grad_mid, grad_states, payload, prods, flows, gain_row):
    core, z = idx[0], idx[2]
    length, units = decay.shape
    steps = length // chunks
    mid = middle[...]
    r = lax.rsqrt(jnp.mean(mid * mid, axis=-1, keepdims=True) + norm_eps)
    scaled = mid * r
    g = gn[...]
    gain_row[...] = jnp.sum(g * scaled, axis=0, keepdims=True)
    gg = g * gain[...]
    gm = cotp[...].astype(f32) + r * (gg - scaled * jnp.mean(gg * scaled, axis=-1, keepdims=True))
    grad_mid[...] = gm
    low = gm.astype(bf16)
    grad_states[...] = dot_nt(low, w_out[...])
    part = units // 8
    for k in range(4):
        for ref, which in ((send, 1 - core), (keep, core)):
            got = dot(stT[pl.ds(pl.multiple_of((2 * k + which) * part, part), part), :], low)
            at = pl.ds(pl.multiple_of((k ^ z) * (part // 4), part // 4), part // 4)
            for p in range(4):
                ref[p, at, :] = got[p * (part // 4) : (p + 1) * (part // 4)].astype(bf16)

    def step(i, carry):
        prod, flow = carry
        rows = pl.ds(pl.multiple_of((steps - 1 - i) * chunks, chunks), chunks)
        d = decay[rows, :]
        return prod * d, (flow + grad_states[rows, :]) * d

    prod, flow = lax.fori_loop(
        0, steps, step, (jnp.ones((chunks, units), f32), jnp.zeros((chunks, units), f32)), unroll=8
    )
    total, out = prod[chunks - 1 :], flow[chunks - 1 :]
    for k in range(chunks - 2, -1, -1):
        total = total * prod[k : k + 1]
        out = out * prod[k : k + 1] + flow[k : k + 1]
    payload[0:1, :] = total
    payload[1:2, :] = out
    prods[...] = prod
    flows[...] = flow


def mixed_out(mix, mixed, done, split):
    from_chunked(mix, split, mixed)
    done[...] = jnp.zeros_like(done)


def gate_grads(which, keep, carried, st, share, cand, du, dv, nmt, z, out, lows, small):
    length, units = carried.shape
    half = units // 2
    cols = pl.ds(pl.multiple_of(which * half, half), half)
    cf = carried[:, cols]
    q = share[:, cols]
    s = cf * (st[0:length, cols] * keep - cand[:, cols])
    ga = s * du[:, cols]
    gb = -(s * dv[:, cols])
    quarter = half // 2
    sum_a, sum_b = jnp.sum(ga, axis=0, keepdims=True), jnp.sum(gb, axis=0, keepdims=True)
    for i in range(2):
        at = pl.ds(4 * (2 * which + i), 1)
        small[at, 0:quarter] = sum_a[:, i * quarter : (i + 1) * quarter]
        small[at, quarter:] = sum_b[:, i * quarter : (i + 1) * quarter]
    part = nmt.shape[0] // 4
    for k, g in enumerate((ga, gb, cf * q)):
        lows[k] = g.astype(bf16)
        got = dot(nmt[...], lows[k])
        for zz in range(4):
            for p in range(4):
                top = zz * part + p * (part // 4)
                out[p, zz ^ z, k * (part // 4) : (k + 1) * (part // 4), :] = got[top : top + part // 4].astype(bf16)


def mixer_back(idx, own, r1, r2, r3, prods, flows, decay, share, cand, du, dv, st, grad_states, nmt, mask,
               carried, send, lows, small, others, carry8):
    length, units = decay.shape
    steps = length // chunks
    core, z = idx[0], idx[2]
    for j, ref in enumerate((own, r1, r2, r3)):
        others[j] = ref[...]
    flow = jnp.zeros((1, units), f32)
    for k in range(3, -1, -1):
        part = others[k ^ z]
        flow = jnp.where(k > z, flow * part[0:1] + part[1:2], flow)
    for k in range(chunks - 1, -1, -1):
        carry8[k : k + 1, :] = flow
        flow = flow * prods[k : k + 1, :] + flows[k : k + 1, :]

    def step(i, flow):
        rows = pl.ds(pl.multiple_of((steps - 1 - i) * chunks, chunks), chunks)
        got = grad_states[rows, :] + flow
        carried[rows, :] = got
        return got * decay[rows, :]

    lax.fori_loop(0, steps, step, carry8[...], unroll=8)
    small[...] = jnp.zeros_like(small)
    gate_grads(1 - core, mask[...], carried, st, share, cand, du, dv, nmt, z, send, lows, small)


def mixer_out(idx, carried, share, cand, du, dv, st, nmt, w, lows0, small0, small1, gain_row, x, mask,
              keep, gnm, small, lows):
    length, units = carried.shape
    core, z = idx[0], idx[2]
    small[...] = small0[...] + small1[...]
    gate_grads(core, mask[...], carried, st, share, cand, du, dv, nmt, z, keep, lows, small)
    half = units // 2
    total = jnp.zeros(gnm.shape, f32)
    for part, which in ((lows0, 1 - core), (lows, core)):
        cols = pl.ds(pl.multiple_of(which * half, half), half)
        for k in range(3):
            total = total + dot_nt(part[k], w[k, :, cols])
    gnm[...] = total
    v = x[...]
    r = lax.rsqrt(jnp.mean(v * v, axis=-1, keepdims=True) + norm_eps)
    gains = jnp.sum(gnm[...] * (v * r), axis=0, keepdims=True)
    n = gains.shape[1] // 4
    for k in range(4):
        small[4 * k + 1 : 4 * k + 2, 0:n] = gains[:, k * n : (k + 1) * n]
        small[4 * k + 1 : 4 * k + 2, n : 2 * n] = gain_row[:, k * n : (k + 1) * n]


def tokens_out(gnm, x, gain, grad_mid, grad_tok, done, total, split):
    v = x[...]
    r = lax.rsqrt(jnp.mean(v * v, axis=-1, keepdims=True) + norm_eps)
    scaled = v * r
    gg = gnm[...] * gain[...]
    total[...] = grad_mid[...] + r * (gg - scaled * jnp.mean(gg * scaled, axis=-1, keepdims=True))
    from_chunked(total, split, grad_tok)
    done[...] = jnp.zeros_like(done)


def pick_piece(idx, wu, wd, out, sems):
    rows = wu.shape[0] // 8
    at = pl.ds(pl.multiple_of((idx[0] * 4 + idx[1]) * rows, rows), rows)
    for copy in fetch([(wu.at[at, :], out.at[pl.ds(0, rows), :]), (wd.at[at, :], out.at[pl.ds(rows, rows), :])], sems):
        copy.wait()


def gate(value, after):
    any_space = pl.BlockSpec(memory_space=pl.ANY)
    return pl.pallas_call(
        lambda *refs: None,
        out_shape=jax.ShapeDtypeStruct(value.shape, value.dtype),
        in_specs=[any_space, any_space],
        out_specs=any_space,
        input_output_aliases={0: 0},
        compiler_params=pltpu.CompilerParams(vmem_limit_bytes=1 << 20),
        name="gate",
    )(value, after)


def join(*refs):
    out, rows = refs[-1], refs[0].shape[0]
    for k, ref in enumerate(refs[:-1]):
        if len(out.shape) == 3:
            out[k] = ref[...]
        else:
            out[k * rows : (k + 1) * rows, :] = ref[...]


def two_terms(v):
    high = v.astype(bf16)
    return high, (v - high.astype(f32)).astype(bf16)


def add_pair(keep, got, out):
    out[...] = (keep[...].astype(f32) + got[...].astype(f32)).astype(bf16)


def add_core(idx, keep_a, got_a, more_a, keep_b, got_b, keep_c, got_c, send_x, send_y, own_x, own_y):
    x, y = idx[1] % 2, idx[1] // 2
    half = send_x.shape[1]

    def put(ref, k, p, first):
        top = 0
        for arrays in ((keep_a, got_a, more_a), (keep_b, got_b), (keep_c, got_c)):
            n = arrays[0].shape[1]
            low, high = max(first, top), min(first + half, top + n)
            if low < high:
                rows = slice(low - top, high - top)
                total = arrays[0][p, rows, :].astype(f32)
                for more in arrays[1:]:
                    total = total + more[p, rows, :].astype(f32)
                ref[k, low - first : high - first, :] = total.astype(ref.dtype)
            top += n

    for k in range(2):
        put(send_x, k, 2 * k + 1 - x, 0)
        put(own_x, k, 2 * k + x, 0)
        put(send_y, k, 2 * (1 - y) + k, half)
        put(own_y, k, 2 * y + k, half)


def add_cross(idx, own_x, got_x, own_y, got_y, send_y, send_x, out_x, out_y):
    x, y = idx[1] % 2, idx[1] // 2
    send_y[...] = (own_x[1 - y] + got_x[1 - y].astype(f32)).astype(bf16)
    out_x[...] = own_x[y] + got_x[y].astype(f32)
    send_x[...] = (own_y[1 - x] + got_y[1 - x].astype(f32)).astype(bf16)
    out_y[...] = own_y[x] + got_y[x].astype(f32)


def add_depth(own_x, got_x, own_y, got_y, send, own, total):
    half = own_x.shape[0]
    part = send.shape[0] // 6
    block = 4 * part
    total[0:half, :] = own_x[...] + got_x[...].astype(f32)
    total[half:, :] = own_y[...] + got_y[...].astype(f32)
    out = 3 * block
    for ref, to, at, n in ((send, 0, 2 * block, block), (send, block, out + part, part), (send, block + part, out + 3 * part, part),
                           (own, 0, 0, block), (own, block, out, part), (own, block + part, block, block), (own, 2 * block + part, out + 2 * part, part)):
        ref[to : to + n, :] = total[at : at + n, :].astype(ref.dtype)


def add_far(own, got, send, out):
    rows = out.shape[0]
    part = rows // 5
    block = 4 * part
    out[0:block, :] = own[0:block, :]
    out[block:, :] = own[block:rows, :] + got[block:rows, :].astype(f32)
    send[0:block, :] = (own[rows : rows + block, :] + got[0:block, :].astype(f32)).astype(bf16)
    send[block:, :] = (own[rows + block :, :] + got[rows:, :].astype(f32)).astype(bf16)


def add_last(own, got, out):
    out[...] = (own[...] + got[...].astype(f32)).astype(out.dtype)


def add_core_small(idx, keep, got, small, send, own, tiny, slots):
    z = idx[2]
    rows = keep.shape[1] // 4
    n = small.shape[0] // 4
    slots[...] = jnp.zeros_like(slots)
    for k in range(4):
        slots[k, 0:n, :] = small[k * n : (k + 1) * n, :]
    for p in range(4):
        for j in range(4):
            at = slice(j * rows, (j + 1) * rows)
            total = keep[p, at, :].astype(f32) + got[p, at, :].astype(f32)
            base = j // 2 * rows
            if j % 2:
                send[p * 2 * rows + base : p * 2 * rows + base + rows, :] = total.astype(bf16)
            else:
                own[p, base : base + rows, :] = total
    for k in range(2):
        base = 8 * rows + 16 * k
        high, low = two_terms(slots[z ^ (2 * k + 1)])
        send[base : base + 16, :] = jnp.concatenate([high, low], axis=0)
        tiny[8 * k : 8 * k + 8, :] = slots[z ^ (2 * k)]


def add_near_small(idx, own, got, tiny, send_x, send_y, own_x, own_y, tiny_out):
    x, y = idx[1] % 2, idx[1] // 2
    rows = own.shape[1] // 2
    for k in range(2):
        base = 8 * rows + 16 * k
        other = got[base : base + 16, :].astype(f32)
        high, low = two_terms(tiny[8 * k : 8 * k + 8, :] + (other[0:8] + other[8:16]))
        for ref, top in ((tiny_out, 0), (send_x, 2 * rows)):
            ref[top + 8 * k : top + 8 * k + 8, :] = high
            ref[top + 16 + 8 * k : top + 24 + 8 * k, :] = low

    def total(p, slot):
        at = pl.ds(pl.multiple_of(p * 2 * rows + slot * rows, 16), rows)
        return own[p, slot * rows : (slot + 1) * rows, :] + got[at, :].astype(f32)

    for k in range(2):
        at = slice(k * rows, (k + 1) * rows)
        send_x[at, :] = total(2 * k + 1 - x, 0).astype(bf16)
        own_x[k] = total(2 * k + x, 0)
        send_y[at, :] = total(2 * (1 - y) + k, 1).astype(bf16)
        own_y[k] = total(2 * y + k, 1)


def add_tiny(tiny, got, at):
    n = tiny.shape[0] // 2
    return (tiny[0:n, :].astype(f32) + tiny[n:, :].astype(f32)) + (
        got[at : at + n, :].astype(f32) + got[at + n : at + 2 * n, :].astype(f32)
    )


def add_cross_small(idx, own_x, got_x, own_y, got_y, tiny, send_y, send_x, out_x, out_y, tiny_out):
    x, y = idx[1] % 2, idx[1] // 2
    half, n = out_x.shape[0], tiny.shape[0] // 2
    high, low = two_terms(add_tiny(tiny, got_x, 2 * half))
    tiny_out[0:n, :] = high
    tiny_out[n:, :] = low
    send_y[half : half + n, :] = high
    send_y[half + n :, :] = low
    side = pl.ds(pl.multiple_of((1 - y) * half, half), half)
    send_y[0:half, :] = (own_x[1 - y] + got_x[side, :].astype(f32)).astype(bf16)
    side = pl.ds(pl.multiple_of(y * half, half), half)
    out_x[...] = own_x[y] + got_x[side, :].astype(f32)
    side = pl.ds(pl.multiple_of((1 - x) * half, half), half)
    send_x[...] = (own_y[1 - x] + got_y[side, :].astype(f32)).astype(bf16)
    side = pl.ds(pl.multiple_of(x * half, half), half)
    out_y[...] = own_y[x] + got_y[side, :].astype(f32)


def add_far_small(own_x, got_x, own_y, got_y, tiny, send, out, tiny_out):
    rows = out.shape[0]
    total = add_tiny(tiny, got_x, rows)
    out[...] = own_x[...] + got_x[0:rows, :].astype(f32)
    tiny_out[...] = total[0:8]
    send[0:rows, :] = (own_y[...] + got_y[...].astype(f32)).astype(bf16)
    high, low = two_terms(total[8:16])
    send[rows:, :] = jnp.concatenate([high, low], axis=0)


def add_last_small(own, tiny, got, out, tiny_out):
    rows, n = own.shape[0], tiny.shape[0]
    out[...] = (own[...] + got[0:rows, :].astype(f32)).astype(out.dtype)
    other = got[rows:, :].astype(f32)
    tiny_out[...] = tiny[...] + (other[0:n] + other[n : 2 * n])


def spread_mlp(idx, near, far, up, down, w_out, done):
    rows = up.shape[0] // 8
    rows_out = w_out.shape[0] // 8
    for which, pieces in ((idx[0], near), (1 - idx[0], far)):
        for k in range(4):
            spot = which * 4 + (idx[1] ^ k)
            at = pl.ds(pl.multiple_of(spot * rows, rows), rows)
            up[at, :] = pieces[k, 0:rows, :].astype(f32)
            down[at, :] = pieces[k, rows : 2 * rows, :].astype(f32)
            w_out[pl.ds(pl.multiple_of(spot * rows_out, rows_out), rows_out), :] = pieces[k, 2 * rows :, :].astype(f32)
    done[...] = jnp.zeros_like(done)


def spread_mix(idx, tiny, tiny_far, near, far, out, bias_f, bias_i, gain_mix, gain_mlp, b_up):
    rows, half = out.shape[1] // 4, out.shape[2] // 2
    for which, pieces in ((idx[0], near), (1 - idx[0], far)):
        cols = pl.ds(pl.multiple_of(which * half, half), half)
        for k in range(4):
            at = pl.ds(pl.multiple_of((idx[1] ^ k) * rows, rows), rows)
            for i in range(3):
                out[i, at, cols] = pieces[k, i * rows : (i + 1) * rows, :].astype(f32)
    small = tiny[...] + tiny_far[...]
    n = bias_f.shape[1]
    bias_f[...] = small[0:1, 0:n]
    bias_i[...] = small[0:1, n:]
    n = gain_mix.shape[1]
    gain_mix[...] = small[1:2, 0:n]
    gain_mlp[...] = small[1:2, n : 2 * n]
    b_up[...] = small[2:3, :]


def swap(value, axis, bit):
    size = lax.axis_size(axis)
    return lax.ppermute(value, axis, [(i, i ^ bit) for i in range(size)])


def across(value, turn):
    size = lax.axis_size("dp")
    return lax.ppermute(value, "dp", [(i, i ^ (2 << ((i & 1) ^ turn))) for i in range(size)])


def on_device(tokens, gain_mix, w_mix, bias_forget, bias_input, w_out, gain_mlp, w_up, b_up, w_down, resets, cotangent):
    length, width = tokens.shape[1:]
    units = w_out.shape[0]
    ff = w_up.shape[1]
    dp, mp = lax.axis_size("dp"), lax.axis_size("mp")
    assert mp == 4 and dp % 8 == 0 and tokens.shape[0] == 1
    idx = None
    tok, cot = tokens[0], cotangent[0]
    w3 = w_mix.transpose(1, 0, 2)
    row = lambda v: v.reshape(1, -1)
    lanes = width // 128

    (piece,) = call(pick_piece, "pick_piece", (idx, w_up, w_down), [shape_of(bf16, width // 4, ff)],
                    [pltpu.SemaphoreType.DMA((2,))], hbm=2, limit=2)
    depth = [swap(piece, "mp", j) for j in (1, 2, 3)]

    wide = shape_of(f32, length, units)
    square = shape_of(f32, length, width)
    square16 = shape_of(bf16, length, width)
    edge = shape_of(f32, chunks, units)
    decay, share, cand, du, dv, nmt, x, prods, ends, payload, mask = call(
        mixer_in, "mixer_in",
        (idx, resets, tok, row(gain_mix), row(bias_forget), row(bias_input), row(b_up), w3),
        [wide] * 5 + [shape_of(bf16, width, length), square, edge, edge, shape_of(f32, 4, units), shape_of(f32, length, 1)],
        [pltpu.SMEM(resets.shape, jnp.int32), pltpu.VMEM((lanes, length, 128), f32), pltpu.VMEM((length, width), bf16), pltpu.VMEM((1, width), f32)]
        + [pltpu.VMEM((1, units), f32)] * 2 + [pltpu.VMEM((1, ff), f32), pltpu.VMEM((3, width, units), bf16),
                                              pltpu.SemaphoreType.DMA((6 + units // 256,))],
        hbm=7, after=(piece,),
    )
    ahead = [swap(payload, "mp", j) for j in (1, 2, 3)]
    around = lambda v: [v] + [swap(v, "dp", 2 * k) for k in (1, 2, 3)]
    mine = gate(depth[0], payload)
    (two,) = call(join, "join_depth", depth[1:], [shape_of(bf16, width // 2, ff)], after=(payload,))
    (one_a,) = call(join, "join_one", (mine, across(mine, 0)), [shape_of(bf16, 2, width // 4, ff)], after=(two, *ahead))
    far_two = across(two, 0)
    quarter = width // 8
    st, stT, middle, nm2, nm2t, cotp = call(
        mid_in, "mid_in",
        (idx, payload, *ahead, prods, ends, decay, share, cand, x, cot, w_out, row(gain_mlp)),
        [shape_of(f32, length + chunks, units), shape_of(bf16, units, length), square, square16, shape_of(bf16, width, length), square16],
        [pltpu.VMEM((lanes, length, 128), f32), pltpu.VMEM((4, 4, units), f32), pltpu.VMEM((chunks, units), f32), pltpu.VMEM((length, width), f32)],
    )
    (two_a,) = call(join, "join_two", (two, far_two), [shape_of(bf16, 2, width // 2, ff)], after=(nm2,))
    two_b = across(two_a, 1)
    block = 2 * quarter
    pair = lambda dtype, rows: shape_of(dtype, 2, rows, width)
    weights = [pltpu.VMEM((ff, length), bf16), pltpu.VMEM((width, ff), bf16), pltpu.VMEM((ff, width), bf16)]
    grads = lambda rows: [square] * 2 + [shape_of(bf16, 4, rows, width)] * 2 + [shape_of(f32, 16, width)]
    one_b = gate(across(one_a, 1), nm2)
    mix, gn, keep0, send0, small_mlp = call(
        mlp_own, "mlp_own", (idx, w_up, w_down, row(b_up), middle, nm2, nm2t, cotp), grads(block), weights[:1], after=(two_a,),
    )
    mix, gn, keep_a, send_a, small_mlp = call(
        mlp_one, "mlp_one",
        (idx, one_a, one_b, swap(one_a, "dp", 1), swap(one_b, "dp", 1), ahead[0], mix, gn, small_mlp, nm2, nm2t, cotp), grads(block), weights,
    )
    (pair_a,) = call(add_pair, "add_pair", (keep_a, swap(send_a, "dp", 1)), [shape_of(bf16, 4, block, width)])
    more_a = swap(pair_a, "mp", 1)
    mix, gn, keep, send, small_mlp = call(
        mlp_two, "mlp_two",
        (idx, two_a, two_b, swap(two_a, "dp", 1), swap(two_b, "dp", 1), ahead[1], ahead[2], mix, gn, small_mlp, nm2, nm2t, cotp),
        grads(2 * block), weights, after=(pair_a,),
    )
    got, got0 = swap(send, "dp", 1), swap(send0, "dp", 1)
    out_rows = units // 8
    keep_out, send_out, grad_mid, grad_states, payload, prods, flows, gain_row = call(
        mid_back, "mid_back",
        (idx, gn, cotp, middle, row(gain_mlp), stT, w_out, decay),
        [shape_of(bf16, 4, out_rows, width)] * 2 + [square, wide, shape_of(f32, 2, units), edge, edge, shape_of(f32, 1, width)],
    )
    payload = gate(payload, got)
    behind = [swap(payload, "mp", j) for j in (1, 2, 3)]

    half = (3 * block + out_rows) // 2
    send_x, send_y, own_x, own_y = call(add_core, "add_core", (idx, keep0, got0, more_a, keep, got, keep_out, swap(send_out, "dp", 1)),
                                        [pair(bf16, half)] * 2 + [pair(f32, half)] * 2)
    got_x, got_y = swap(send_x, "dp", 2), swap(send_y, "dp", 4)

    rows_m = 3 * width // 16
    carried, send, lows, small = call(
        mixer_back, "mixer_back",
        (idx, payload, *behind, prods, flows, decay, share, cand, du, dv, st, grad_states, nmt, mask),
        [wide, shape_of(bf16, 4, 4, rows_m, units // 2), shape_of(bf16, 3, length, units // 2), shape_of(f32, 16, width)],
        [pltpu.VMEM((4, 2, units), f32), pltpu.VMEM((chunks, units), f32)], after=(own_x,),
    )
    flat = lambda v: v.reshape(4, -1, width)
    got = swap(send, "dp", 1)
    keep, gnm, small = call(
        mixer_out, "mixer_out",
        (idx, carried, share, cand, du, dv, st, nmt, w3, lows, small, small_mlp, gain_row, x, mask),
        [shape_of(bf16, 4, 4, rows_m, units // 2), square, shape_of(f32, 16, width)],
        [pltpu.VMEM((3, length, units // 2), bf16)],
    )
    one = lambda dtype, rows: shape_of(dtype, rows, width)
    send_m, own_m, tiny = call(
        add_core_small, "add_core_small", (idx, flat(keep), flat(got), small),
        [one(bf16, 8 * rows_m + 32), shape_of(f32, 4, 2 * rows_m, width), one(f32, 16)], [pltpu.VMEM((4, 8, width), f32)],
    )
    got_m = swap(send_m, "mp", 1)
    mark = shape_of(f32, 8, 128)
    grad_tok, done_tok = call(tokens_out, "tokens_out", (gnm, x, row(gain_mix), grad_mid), [square16, mark],
                       [pltpu.VMEM((length, width), f32), pltpu.VMEM((lanes, length, 128), f32)], after=(own_m,))
    mixed, done_mix = call(mixed_out, "mixed_out", (mix,), [square16, mark], [pltpu.VMEM((lanes, length, 128), f32)], after=(own_m,))

    send_y, send_x, own_x, own_y = call(add_cross, "add_cross", (idx, own_x, got_x, own_y, got_y),
                                        [one(bf16, half)] * 2 + [one(f32, half)] * 2, after=(own_m,))
    got_x, got_y = swap(send_y, "dp", 4), swap(send_x, "dp", 2)
    rows_f = block + units // 32
    send, own = call(add_depth, "add_depth", (own_x, got_x, own_y, got_y), [one(bf16, block + units // 16), one(f32, 2 * rows_f)],
                     [pltpu.VMEM((2 * half, width), f32)])
    got = swap(send, "mp", 1)
    send_mx, send_my, own_mx, own_my, tiny = call(
        add_near_small, "add_near_small", (idx, own_m, got_m, tiny),
        [one(bf16, 2 * rows_m + 32), one(bf16, 2 * rows_m), pair(f32, rows_m), pair(f32, rows_m), one(bf16, 32)],
        after=(own, done_mix, done_tok),
    )
    got_mx, got_my = swap(send_mx, "dp", 2), swap(send_my, "dp", 4)
    send, own = call(add_far, "add_far", (own, got), [one(bf16, rows_f), one(f32, rows_f)], after=(tiny,))
    got = swap(send, "mp", 2)
    send_my, send_mx, own_mx, own_my, tiny = call(
        add_cross_small, "add_cross_small", (idx, own_mx, got_mx, own_my, got_my, tiny),
        [one(bf16, rows_m + 32), one(bf16, rows_m), one(f32, rows_m), one(f32, rows_m), one(bf16, 32)], after=(own,),
    )
    got_mx, got_my = swap(send_my, "dp", 4), swap(send_mx, "dp", 2)
    send_m, own_m, tiny = call(
        add_far_small, "add_far_small", (own_mx, got_mx, own_my, got_my, tiny), [one(bf16, rows_m + 16), one(f32, rows_m), one(f32, 8)],
    )
    got_m = swap(send_m, "mp", 2)
    groups = [[g * 8 + i for g in range(dp // 8)] for i in range(8)]

    def last(fn, name, operands, outs, after):
        if dp == 8:
            return call(fn, name, operands, outs, after=after)
        done = call(fn, name, operands, [shape_of(f32, *o.shape) for o in outs], after=after)
        return [lax.psum(v, "dp", axis_index_groups=groups).astype(o.dtype) for v, o in zip(done, outs)]

    (part,) = last(add_last, "add_last", (own, got), [one(bf16, rows_f)], (tiny,))
    near_f = around(part)
    part, tiny = last(add_last_small, "add_last_small", (own_m, tiny, got_m), [one(bf16, rows_m), one(f32, 8)], (part,))
    near_m = around(part)
    (near,) = call(join, "join_mlp", near_f, [shape_of(bf16, 4, rows_f, width)], after=(part,))
    grad_up, grad_down, grad_out, done = call(
        spread_mlp, "spread_mlp", (idx, near, swap(near, "dp", 1)),
        [shape_of(f32, width, ff), shape_of(f32, ff, width), shape_of(f32, units // 4, width), mark],
    )
    (near,) = call(join, "join_mix", near_m, [shape_of(bf16, 4, rows_m, width)])
    grad_mix, g_bf, g_bi, g_gain_mix, g_gain_mlp, g_bu = call(
        spread_mix, "spread_mix", (idx, tiny, swap(tiny, "dp", 1), near, swap(near, "dp", 1)),
        [shape_of(f32, 3, width // 4, units), shape_of(f32, 1, units // 4), shape_of(f32, 1, units // 4),
         shape_of(f32, 1, width // 4), shape_of(f32, 1, width // 4), shape_of(f32, 1, ff)],
        after=(done,),
    )
    return (
        mixed[None], grad_tok[None], g_gain_mix[0], grad_mix.transpose(1, 0, 2), g_bf[0], g_bi[0],
        grad_out, g_gain_mlp[0], grad_up, g_bu[0], grad_down,
    )


def solution(mesh):
    return jax.shard_map(
        on_device,
        mesh=mesh,
        in_specs=(P("dp", "mp", None), P(), P(), P(), P(), P(), P(), P(None, "mp"), P("mp"), P("mp", None), P("dp", None), P("dp", "mp", None)),
        out_specs=(P("dp", "mp", None), P("dp", "mp", None), P("mp"), P("mp", None, None), P("mp"), P("mp"), P("mp", None), P("mp"), P(None, "mp"), P("mp"), P("mp", None)),
        check_vma=False,
    )
```

```python
from functools import partial

import jax
import jax.numpy as jnp
from jax import lax
from jax.experimental import pallas as pl
from jax.experimental.pallas import tpu as pltpu
from jax.sharding import PartitionSpec as P

norm_eps = 1e-06
gelu_k = 0.7978845608028654
gelu_c = 0.044715
chunks = 8
f32 = jnp.float32
bf16 = jnp.bfloat16
VMEM = pl.BlockSpec(memory_space=pltpu.VMEM)
HBM = pl.BlockSpec(memory_space=pltpu.HBM)


weight = {
    "pick_piece": 16, "mixer_in": 0, "join_depth": 0, "join_one": 4, "mlp_one": 4, "join_two": 2, "mlp_two": 8, "mid_back": 8,
    "add_core": 0, "mixer_back": 0, "mixer_out": 0, "add_core_small": 0, "add_cross": 4, "mixed_out": 0, "tokens_out": 8,
    "add_cross_small": 8, "add_depth": 0, "add_near_small": 32, "add_far": 16, "add_far_small": 0, "add_last": 4,
    "add_last_small": 4, "join_mlp": 32, "join_mix": 16, "spread_mlp": 8, "spread_mix": 32, "add_pair": 32, "mid_in": 8,
    "mlp_own": 4,
}


def dot(a, b):
    return jnp.dot(a, b, preferred_element_type=f32)


def dot_nt(a, b):
    return lax.dot_general(a, b, (((1,), (1,)), ((), ())), preferred_element_type=f32)


def shape_of(dtype, *shape):
    return jax.ShapeDtypeStruct(shape, dtype)


def place():
    row = lax.axis_index("dp")
    return row & 1, (row >> 1) & 3, lax.axis_index("mp")


def call(body, name, operands, outs, scratch=(), limit=16, after=(), hbm=0):
    placed = operands[0] is None
    operands = operands[placed:]
    n, extra, cost = len(operands), len(after), weight[name]
    operands = [pltpu.with_memory_space_constraint(v, pltpu.HBM) if i < hbm else v for i, v in enumerate(operands)]

    def run(*refs):
        body(*((place(),) if placed else ()), *refs[:n], *refs[n + extra :])

    return pl.pallas_call(
        run,
        out_shape=outs,
        in_specs=[HBM] * hbm + [VMEM] * (n - hbm) + [pl.BlockSpec(memory_space=pl.ANY)] * extra,
        out_specs=[VMEM] * len(outs),
        scratch_shapes=list(scratch),
        compiler_params=pltpu.CompilerParams(vmem_limit_bytes=limit << 20),
        cost_estimate=pl.CostEstimate(flops=cost << 30, bytes_accessed=cost << 22, transcendentals=0),
        name=name,
    )(*operands, *after)


def to_chunked(src, split, put):
    length, width = src.shape
    steps = length // chunks
    for g in range(width // 128):
        cols = slice(g * 128, (g + 1) * 128)
        split[g] = src[:, cols].astype(f32)
        for s in range(steps):
            put(pl.ds(s * chunks, chunks), cols, split[g, pl.ds(s, chunks, stride=steps), :])


def from_chunked(values, split, out):
    length, width = out.shape
    steps = length // chunks
    for g in range(width // 128):
        cols = slice(g * 128, (g + 1) * 128)
        for s in range(steps):
            split[g, pl.ds(s, chunks, stride=steps), :] = values[s * chunks : (s + 1) * chunks, cols]
        out[:, cols] = split[g].astype(bf16)


def keep_mask(idx, resets, length):
    row = lax.broadcasted_iota(jnp.int32, (length, 1), 0)
    pos = idx[2] * length + (row % chunks) * (length // chunks) + row // chunks
    keep = jnp.ones((length, 1), f32)
    for i in range(3):
        keep = jnp.where(pos == resets[0, i], 0.0, keep)
    return keep


def fetch(pairs, sems):
    copies = [pltpu.make_async_copy(src, dst, sems.at[i]) for i, (src, dst) in enumerate(pairs)]
    for copy in copies:
        copy.start()
    return copies


def mixer_in(idx, res_hbm, tok_hbm, gain_hbm, bias_f_hbm, bias_i_hbm, b_up_hbm, w_hbm, decay, share, cand, du, dv, nmt, x, prods, ends, payload, mask,
             resets, split, tok, gain, bias_f, bias_i, b_up, w, sems):
    length, width = tok.shape
    units = bias_f.shape[1]
    steps = length // chunks
    block = 256
    pairs = [(tok_hbm, tok), (gain_hbm, gain), (bias_f_hbm, bias_f), (bias_i_hbm, bias_i), (b_up_hbm, b_up), (res_hbm, resets)]
    for h in range(0, units, block):
        sl = pl.ds(h, block)
        pairs.append((w_hbm.at[:, :, sl], w.at[:, :, sl]))
    copies = fetch(pairs, sems)
    for copy in copies[:6]:
        copy.wait()

    def put(rows, cols, values):
        x[rows, cols] = values

    to_chunked(tok, split, put)
    v = x[...]
    r = lax.rsqrt(jnp.mean(v * v, axis=-1, keepdims=True) + norm_eps)
    nm = (v * r * gain[...]).astype(bf16)
    nmt[...] = nm.T
    keep = keep_mask(idx, resets, length)
    mask[...] = keep
    for i, h in enumerate(range(0, units, block)):
        sl = pl.ds(h, block)
        copies[6 + i].wait()
        a = jnp.exp(jnp.minimum(-(dot(nm, w[0, :, sl]) + bias_f[:, sl]), 88.0))
        b = jnp.exp(jnp.minimum(-(dot(nm, w[1, :, sl]) + bias_i[:, sl]), 88.0))
        t = 1.0 / (2.0 + a + b)
        p = (1.0 + b) * t
        q = (1.0 + a) * t
        decay[:, sl] = p * keep
        share[:, sl] = q
        cand[:, sl] = dot(nm, w[2, :, sl])
        du[:, sl] = p * (a * t)
        dv[:, sl] = q * (b * t)

    def step(s, carry):
        prod, end = carry
        rows = pl.ds(pl.multiple_of(s * chunks, chunks), chunks)
        d = decay[rows, :]
        return prod * d, end * d + share[rows, :] * cand[rows, :]

    prod, end = lax.fori_loop(
        0, steps, step, (jnp.ones((chunks, units), f32), jnp.zeros((chunks, units), f32)), unroll=8
    )
    prods[...] = prod
    ends[...] = end
    total, state = prod[0:1], end[0:1]
    for k in range(1, chunks):
        total = total * prod[k : k + 1]
        state = state * prod[k : k + 1] + end[k : k + 1]
    payload[...] = jnp.zeros_like(payload)
    payload[0:1, :] = total
    payload[1:2, :] = state
    payload[2:3, 0 : b_up.shape[1]] = b_up[...]


def store_pieces(ref, base, rows, values):
    for p in range(4):
        ref[p, base : base + rows, :] = values[p * rows : (p + 1) * rows].astype(bf16)


def send_first(ref, core, values):
    n = values.shape[0] // 2
    ref[pl.ds(pl.multiple_of((1 - core) * n, n), n), :] = values[0:n]
    ref[pl.ds(pl.multiple_of(core * n, n), n), :] = values[n:]


def ffn_block(slot, core, nm, nmt, cot, wu, wd, bu, mix, gn, keep, send, hT):
    pre = dot(nm, wu[...]) + bu
    grad_act = dot_nt(cot, wd[...])
    sq = pre * pre
    t = jnp.tanh(pre * (gelu_k + gelu_k * gelu_c * sq))
    half = 0.5 + 0.5 * t
    h = pre * half
    slope = half + h * (1.0 - t) * (gelu_k + 3.0 * gelu_k * gelu_c * sq)
    grad_pre = grad_act * slope
    total = jnp.sum(grad_pre, axis=0, keepdims=True)
    h, g = h.astype(bf16), grad_pre.astype(bf16)
    send_first(hT, core, h.T)
    mix[...] += dot(h, wd[...])
    gn[...] += dot_nt(g, wu[...])
    n = nm.shape[1] // 2
    for base, got in ((0, dot(nmt[...], g)), (n // 4, dot(hT[...], cot))):
        store_pieces(send, slot * (n // 2) + base, n // 4, got[0:n])
        store_pieces(keep, slot * (n // 2) + base, n // 4, got[n:])
    return total


def mid_in(idx, own, r1, r2, r3, prods, ends, decay, share, cand, x, cot, w_out, gain,
           st, stT, middle, nm2, nm2t, cotp, split, others, carry8, square):
    length = x.shape[0]
    steps = length // chunks
    units = decay.shape[1]
    z = idx[2]
    for j, ref in enumerate((own, r1, r2, r3)):
        others[j] = ref[...]
    state = jnp.zeros((1, units), f32)
    for k in range(4):
        part = others[k ^ z]
        state = jnp.where(k < z, state * part[0:1] + part[1:2], state)
    for k in range(chunks):
        carry8[k : k + 1, :] = state
        state = state * prods[k : k + 1, :] + ends[k : k + 1, :]
    st[0:chunks, :] = carry8[...]

    def step(s, state):
        rows = pl.ds(pl.multiple_of(s * chunks, chunks), chunks)
        state = state * decay[rows, :] + share[rows, :] * cand[rows, :]
        st[pl.ds(pl.multiple_of(s * chunks + chunks, chunks), chunks), :] = state
        return state

    lax.fori_loop(0, steps, step, carry8[...], unroll=8)
    low = st[chunks:, :].astype(bf16)
    stT[...] = low.T
    mid = x[...] + dot(low, w_out[...])
    middle[...] = mid
    r = lax.rsqrt(jnp.mean(mid * mid, axis=-1, keepdims=True) + norm_eps)
    nm = (mid * r * gain[...]).astype(bf16)
    nm2[...] = nm
    send_first(nm2t, idx[0], nm.T)

    def put(rows, cols, values):
        square[rows, cols] = values

    to_chunked(cot, split, put)
    cotp[...] = square[...].astype(bf16)


def pieces_of(idx, near, near_far, far, far_far):
    for which, arrays in ((idx[0], (near, near_far)), (1 - idx[0], (far, far_far))):
        for k in range(2):
            for i in range(2):
                yield which, idx[1] ^ (i * (1 + which) + k * (2 - which)), arrays[k].at[i]


def lay_out(idx, arrays, at, wu, wd):
    rows = wu.shape[0] // 8
    for which, place, piece in pieces_of(idx, *arrays):
        spot = pl.ds(pl.multiple_of((which * 4 + place) * rows, rows), rows)
        wu[spot, :] = piece[at : at + rows, :]
        wd[spot, :] = piece[at + rows : at + 2 * rows, :]


def mlp_own(idx, wu, wd, bu, middle, nm2, nm2t, cotp, mix, gn, keep, send, small, hT):
    mix[...] = middle[...]
    gn[...] = jnp.zeros_like(gn)
    small[...] = jnp.zeros_like(small)
    small[pl.ds(4 * idx[2] + 2, 1), :] = ffn_block(
        0, idx[0], nm2[...], nm2t, cotp[...], wu, wd, bu[...], mix, gn, keep, send, hT
    )


def mlp_one(idx, n1, n2, f1, f2, bias, mix0, gn0, small0, nm2, nm2t, cotp, mix, gn, keep, send, small, hT, wu, wd):
    mix[...] = mix0[...]
    gn[...] = gn0[...]
    small[...] = small0[...]
    lay_out(idx, (n1, n2, f1, f2), 0, wu, wd)
    small[pl.ds(4 * (idx[2] ^ 1) + 2, 1), :] = ffn_block(
        0, idx[0], nm2[...], nm2t, cotp[...], wu, wd, bias[2:3, 0 : wu.shape[1]], mix, gn, keep, send, hT
    )


def mlp_two(idx, n1, n2, f1, f2, bias2, bias3, mix0, gn0, small0, nm2, nm2t, cotp, mix, gn, keep, send, small, hT, wu, wd):
    mix[...] = mix0[...]
    gn[...] = gn0[...]
    small[...] = small0[...]
    for slot, bias in enumerate((bias2, bias3)):
        lay_out(idx, (n1, n2, f1, f2), slot * wu.shape[0] // 4, wu, wd)
        small[pl.ds(4 * (idx[2] ^ (2 + slot)) + 2, 1), :] = ffn_block(
            slot, idx[0], nm2[...], nm2t, cotp[...], wu, wd, bias[2:3, 0 : wu.shape[1]], mix, gn, keep, send, hT
        )


def mid_back(idx, gn, cotp, middle, gain, stT, w_out, decay,
             keep, send, grad_mid, grad_states, payload, prods, flows, gain_row):
    core, z = idx[0], idx[2]
    length, units = decay.shape
    steps = length // chunks
    mid = middle[...]
    r = lax.rsqrt(jnp.mean(mid * mid, axis=-1, keepdims=True) + norm_eps)
    scaled = mid * r
    g = gn[...]
    gain_row[...] = jnp.sum(g * scaled, axis=0, keepdims=True)
    gg = g * gain[...]
    gm = cotp[...].astype(f32) + r * (gg - scaled * jnp.mean(gg * scaled, axis=-1, keepdims=True))
    grad_mid[...] = gm
    low = gm.astype(bf16)
    grad_states[...] = dot_nt(low, w_out[...])
    part = units // 8
    for k in range(4):
        for ref, which in ((send, 1 - core), (keep, core)):
            got = dot(stT[pl.ds(pl.multiple_of((2 * k + which) * part, part), part), :], low)
            at = pl.ds(pl.multiple_of((k ^ z) * (part // 4), part // 4), part // 4)
            for p in range(4):
                ref[p, at, :] = got[p * (part // 4) : (p + 1) * (part // 4)].astype(bf16)

    def step(i, carry):
        prod, flow = carry
        rows = pl.ds(pl.multiple_of((steps - 1 - i) * chunks, chunks), chunks)
        d = decay[rows, :]
        return prod * d, (flow + grad_states[rows, :]) * d

    prod, flow = lax.fori_loop(
        0, steps, step, (jnp.ones((chunks, units), f32), jnp.zeros((chunks, units), f32)), unroll=8
    )
    total, out = prod[chunks - 1 :], flow[chunks - 1 :]
    for k in range(chunks - 2, -1, -1):
        total = total * prod[k : k + 1]
        out = out * prod[k : k + 1] + flow[k : k + 1]
    payload[0:1, :] = total
    payload[1:2, :] = out
    prods[...] = prod
    flows[...] = flow


def mixed_out(mix, mixed, done, split):
    from_chunked(mix, split, mixed)
    done[...] = jnp.zeros_like(done)


def gate_grads(which, keep, carried, st, share, cand, du, dv, nmt, z, out, lows, small):
    length, units = carried.shape
    half = units // 2
    cols = pl.ds(pl.multiple_of(which * half, half), half)
    cf = carried[:, cols]
    q = share[:, cols]
    s = cf * (st[0:length, cols] * keep - cand[:, cols])
    ga = s * du[:, cols]
    gb = -(s * dv[:, cols])
    quarter = half // 2
    sum_a, sum_b = jnp.sum(ga, axis=0, keepdims=True), jnp.sum(gb, axis=0, keepdims=True)
    for i in range(2):
        at = pl.ds(4 * (2 * which + i), 1)
        small[at, 0:quarter] = sum_a[:, i * quarter : (i + 1) * quarter]
        small[at, quarter:] = sum_b[:, i * quarter : (i + 1) * quarter]
    part = nmt.shape[0] // 4
    for k, g in enumerate((ga, gb, cf * q)):
        lows[k] = g.astype(bf16)
        got = dot(nmt[...], lows[k])
        for zz in range(4):
            for p in range(4):
                top = zz * part + p * (part // 4)
                out[p, zz ^ z, k * (part // 4) : (k + 1) * (part // 4), :] = got[top : top + part // 4].astype(bf16)


def mixer_back(idx, own, r1, r2, r3, prods, flows, decay, share, cand, du, dv, st, grad_states, nmt, mask,
               carried, send, lows, small, others, carry8):
    length, units = decay.shape
    steps = length // chunks
    core, z = idx[0], idx[2]
    for j, ref in enumerate((own, r1, r2, r3)):
        others[j] = ref[...]
    flow = jnp.zeros((1, units), f32)
    for k in range(3, -1, -1):
        part = others[k ^ z]
        flow = jnp.where(k > z, flow * part[0:1] + part[1:2], flow)
    for k in range(chunks - 1, -1, -1):
        carry8[k : k + 1, :] = flow
        flow = flow * prods[k : k + 1, :] + flows[k : k + 1, :]

    def step(i, flow):
        rows = pl.ds(pl.multiple_of((steps - 1 - i) * chunks, chunks), chunks)
        got = grad_states[rows, :] + flow
        carried[rows, :] = got
        return got * decay[rows, :]

    lax.fori_loop(0, steps, step, carry8[...], unroll=8)
    small[...] = jnp.zeros_like(small)
    gate_grads(1 - core, mask[...], carried, st, share, cand, du, dv, nmt, z, send, lows, small)


def mixer_out(idx, carried, share, cand, du, dv, st, nmt, w, lows0, small0, small1, gain_row, x, mask,
              keep, gnm, small, lows):
    length, units = carried.shape
    core, z = idx[0], idx[2]
    small[...] = small0[...] + small1[...]
    gate_grads(core, mask[...], carried, st, share, cand, du, dv, nmt, z, keep, lows, small)
    half = units // 2
    total = jnp.zeros(gnm.shape, f32)
    for part, which in ((lows0, 1 - core), (lows, core)):
        cols = pl.ds(pl.multiple_of(which * half, half), half)
        for k in range(3):
            total = total + dot_nt(part[k], w[k, :, cols])
    gnm[...] = total
    v = x[...]
    r = lax.rsqrt(jnp.mean(v * v, axis=-1, keepdims=True) + norm_eps)
    gains = jnp.sum(gnm[...] * (v * r), axis=0, keepdims=True)
    n = gains.shape[1] // 4
    for k in range(4):
        small[4 * k + 1 : 4 * k + 2, 0:n] = gains[:, k * n : (k + 1) * n]
        small[4 * k + 1 : 4 * k + 2, n : 2 * n] = gain_row[:, k * n : (k + 1) * n]


def tokens_out(gnm, x, gain, grad_mid, grad_tok, done, total, split):
    v = x[...]
    r = lax.rsqrt(jnp.mean(v * v, axis=-1, keepdims=True) + norm_eps)
    scaled = v * r
    gg = gnm[...] * gain[...]
    total[...] = grad_mid[...] + r * (gg - scaled * jnp.mean(gg * scaled, axis=-1, keepdims=True))
    from_chunked(total, split, grad_tok)
    done[...] = jnp.zeros_like(done)


def pick_piece(idx, wu, wd, out, sems):
    rows = wu.shape[0] // 8
    at = pl.ds(pl.multiple_of((idx[0] * 4 + idx[1]) * rows, rows), rows)
    for copy in fetch([(wu.at[at, :], out.at[pl.ds(0, rows), :]), (wd.at[at, :], out.at[pl.ds(rows, rows), :])], sems):
        copy.wait()


def gate(value, after):
    any_space = pl.BlockSpec(memory_space=pl.ANY)
    return pl.pallas_call(
        lambda *refs: None,
        out_shape=jax.ShapeDtypeStruct(value.shape, value.dtype),
        in_specs=[any_space, any_space],
        out_specs=any_space,
        input_output_aliases={0: 0},
        compiler_params=pltpu.CompilerParams(vmem_limit_bytes=1 << 20),
        name="gate",
    )(value, after)


def join(*refs):
    out, rows = refs[-1], refs[0].shape[0]
    for k, ref in enumerate(refs[:-1]):
        if len(out.shape) == 3:
            out[k] = ref[...]
        else:
            out[k * rows : (k + 1) * rows, :] = ref[...]


def stacked(*parts):
    return jnp.concatenate([v.astype(f32) for v in parts], axis=0).astype(bf16)


def two_terms(v):
    high = v.astype(bf16)
    return high, (v - high.astype(f32)).astype(bf16)


def add_pair(keep, got, out):
    out[...] = (keep[...].astype(f32) + got[...].astype(f32)).astype(bf16)


def add_core(idx, keep_a, got_a, more_a, keep_b, got_b, keep_c, got_c, send_x, send_y, own_x, own_y):
    x, y = idx[1] % 2, idx[1] // 2
    half = send_x.shape[1]

    def put(ref, k, p, first):
        top = 0
        for arrays in ((keep_a, got_a, more_a), (keep_b, got_b), (keep_c, got_c)):
            n = arrays[0].shape[1]
            low, high = max(first, top), min(first + half, top + n)
            if low < high:
                rows = slice(low - top, high - top)
                total = arrays[0][p, rows, :].astype(f32)
                for more in arrays[1:]:
                    total = total + more[p, rows, :].astype(f32)
                ref[k, low - first : high - first, :] = total.astype(ref.dtype)
            top += n

    for k in range(2):
        put(send_x, k, 2 * k + 1 - x, 0)
        put(own_x, k, 2 * k + x, 0)
        put(send_y, k, 2 * (1 - y) + k, half)
        put(own_y, k, 2 * y + k, half)


def add_cross(idx, own_x, got_x, own_y, got_y, send_y, send_x, out_x, out_y):
    x, y = idx[1] % 2, idx[1] // 2
    send_y[...] = (own_x[1 - y] + got_x[1 - y].astype(f32)).astype(bf16)
    out_x[...] = own_x[y] + got_x[y].astype(f32)
    send_x[...] = (own_y[1 - x] + got_y[1 - x].astype(f32)).astype(bf16)
    out_y[...] = own_y[x] + got_y[x].astype(f32)


def add_depth(own_x, got_x, own_y, got_y, send, own, total):
    half = own_x.shape[0]
    part = send.shape[0] // 6
    block = 4 * part
    total[0:half, :] = own_x[...] + got_x[...].astype(f32)
    total[half:, :] = own_y[...] + got_y[...].astype(f32)
    out = 3 * block
    for ref, to, at, n in ((send, 0, 2 * block, block), (send, block, out + part, part), (send, block + part, out + 3 * part, part),
                           (own, 0, 0, block), (own, block, out, part), (own, block + part, block, block), (own, 2 * block + part, out + 2 * part, part)):
        ref[to : to + n, :] = total[at : at + n, :].astype(ref.dtype)


def add_far(own, got, send, out):
    rows = out.shape[0]
    part = rows // 5
    block = 4 * part
    out[0:block, :] = own[0:block, :]
    out[block:, :] = own[block:rows, :] + got[block:rows, :].astype(f32)
    send[0:block, :] = (own[rows : rows + block, :] + got[0:block, :].astype(f32)).astype(bf16)
    send[block:, :] = (own[rows + block :, :] + got[rows:, :].astype(f32)).astype(bf16)


def add_last(own, got, out):
    out[...] = (own[...] + got[...].astype(f32)).astype(out.dtype)


def add_core_small(idx, keep, got, small, send, own, tiny, slots):
    z = idx[2]
    rows = keep.shape[1] // 4
    n = small.shape[0] // 4
    slots[...] = jnp.zeros_like(slots)
    for k in range(4):
        slots[k, 0:n, :] = small[k * n : (k + 1) * n, :]
    for p in range(4):
        for j in range(4):
            at = slice(j * rows, (j + 1) * rows)
            total = keep[p, at, :].astype(f32) + got[p, at, :].astype(f32)
            base = j // 2 * rows
            if j % 2:
                send[p * 2 * rows + base : p * 2 * rows + base + rows, :] = total.astype(bf16)
            else:
                own[p, base : base + rows, :] = total
    for k in range(2):
        base = 8 * rows + 16 * k
        high, low = two_terms(slots[z ^ (2 * k + 1)])
        send[base : base + 16, :] = stacked(high, low)
        tiny[8 * k : 8 * k + 8, :] = slots[z ^ (2 * k)]


def add_near_small(idx, own, got, tiny, send_x, send_y, own_x, own_y, tiny_out):
    x, y = idx[1] % 2, idx[1] // 2
    rows = own.shape[1] // 2
    terms = []
    for k in range(2):
        base = 8 * rows + 16 * k
        other = got[base : base + 16, :].astype(f32)
        terms.append(two_terms(tiny[8 * k : 8 * k + 8, :] + (other[0:8] + other[8:16])))
    for i in range(2):
        both = stacked(terms[0][i], terms[1][i])
        tiny_out[16 * i : 16 * i + 16, :] = both
        send_x[2 * rows + 16 * i : 2 * rows + 16 * i + 16, :] = both

    def total(p, slot):
        at = pl.ds(pl.multiple_of(p * 2 * rows + slot * rows, 16), rows)
        return own[p, slot * rows : (slot + 1) * rows, :] + got[at, :].astype(f32)

    for k in range(2):
        at = slice(k * rows, (k + 1) * rows)
        send_x[at, :] = total(2 * k + 1 - x, 0).astype(bf16)
        own_x[k] = total(2 * k + x, 0)
        send_y[at, :] = total(2 * (1 - y) + k, 1).astype(bf16)
        own_y[k] = total(2 * y + k, 1)


def add_tiny(tiny, got, at):
    n = tiny.shape[0] // 2
    return (tiny[0:n, :].astype(f32) + tiny[n:, :].astype(f32)) + (
        got[at : at + n, :].astype(f32) + got[at + n : at + 2 * n, :].astype(f32)
    )


def add_cross_small(idx, own_x, got_x, own_y, got_y, tiny, send_y, send_x, out_x, out_y, tiny_out):
    x, y = idx[1] % 2, idx[1] // 2
    half, n = out_x.shape[0], tiny.shape[0] // 2
    high, low = two_terms(add_tiny(tiny, got_x, 2 * half))
    tiny_out[0:n, :] = high
    tiny_out[n:, :] = low
    send_y[half : half + n, :] = high
    send_y[half + n :, :] = low
    side = pl.ds(pl.multiple_of((1 - y) * half, half), half)
    send_y[0:half, :] = (own_x[1 - y] + got_x[side, :].astype(f32)).astype(bf16)
    side = pl.ds(pl.multiple_of(y * half, half), half)
    out_x[...] = own_x[y] + got_x[side, :].astype(f32)
    side = pl.ds(pl.multiple_of((1 - x) * half, half), half)
    send_x[...] = (own_y[1 - x] + got_y[side, :].astype(f32)).astype(bf16)
    side = pl.ds(pl.multiple_of(x * half, half), half)
    out_y[...] = own_y[x] + got_y[side, :].astype(f32)


def add_far_small(own_x, got_x, own_y, got_y, tiny, send, out, tiny_out):
    rows = out.shape[0]
    total = add_tiny(tiny, got_x, rows)
    out[...] = own_x[...] + got_x[0:rows, :].astype(f32)
    tiny_out[...] = total[0:8]
    send[0:rows, :] = (own_y[...] + got_y[...].astype(f32)).astype(bf16)
    high, low = two_terms(total[8:16])
    send[rows:, :] = stacked(high, low)


def add_last_small(own, tiny, got, out, tiny_out):
    rows, n = own.shape[0], tiny.shape[0]
    out[...] = (own[...] + got[0:rows, :].astype(f32)).astype(out.dtype)
    other = got[rows:, :].astype(f32)
    tiny_out[...] = tiny[...] + (other[0:n] + other[n : 2 * n])


def spread_mlp(idx, near, far, up, down, w_out, done):
    rows = up.shape[0] // 8
    rows_out = w_out.shape[0] // 8
    for which, pieces in ((idx[0], near), (1 - idx[0], far)):
        for k in range(4):
            spot = which * 4 + (idx[1] ^ k)
            at = pl.ds(pl.multiple_of(spot * rows, rows), rows)
            up[at, :] = pieces[k, 0:rows, :].astype(f32)
            down[at, :] = pieces[k, rows : 2 * rows, :].astype(f32)
            w_out[pl.ds(pl.multiple_of(spot * rows_out, rows_out), rows_out), :] = pieces[k, 2 * rows :, :].astype(f32)
    done[...] = jnp.zeros_like(done)


def spread_mix(idx, tiny, tiny_far, near, far, out, bias_f, bias_i, gain_mix, gain_mlp, b_up):
    rows, half = out.shape[1] // 4, out.shape[2] // 2
    for which, pieces in ((idx[0], near), (1 - idx[0], far)):
        cols = pl.ds(pl.multiple_of(which * half, half), half)
        for k in range(4):
            at = pl.ds(pl.multiple_of((idx[1] ^ k) * rows, rows), rows)
            for i in range(3):
                out[i, at, cols] = pieces[k, i * rows : (i + 1) * rows, :].astype(f32)
    small = tiny[...] + tiny_far[...]
    n = bias_f.shape[1]
    bias_f[...] = small[0:1, 0:n]
    bias_i[...] = small[0:1, n:]
    n = gain_mix.shape[1]
    gain_mix[...] = small[1:2, 0:n]
    gain_mlp[...] = small[1:2, n : 2 * n]
    b_up[...] = small[2:3, :]


def swap(value, axis, bit):
    size = lax.axis_size(axis)
    return lax.ppermute(value, axis, [(i, i ^ bit) for i in range(size)])


def across(value, turn):
    size = lax.axis_size("dp")
    return lax.ppermute(value, "dp", [(i, i ^ (2 << ((i & 1) ^ turn))) for i in range(size)])


def on_device(tokens, gain_mix, w_mix, bias_forget, bias_input, w_out, gain_mlp, w_up, b_up, w_down, resets, cotangent):
    length, width = tokens.shape[1:]
    units = w_out.shape[0]
    ff = w_up.shape[1]
    dp, mp = lax.axis_size("dp"), lax.axis_size("mp")
    assert mp == 4 and dp % 8 == 0 and tokens.shape[0] == 1
    idx = None
    tok, cot = tokens[0], cotangent[0]
    w3 = w_mix.transpose(1, 0, 2)
    row = lambda v: v.reshape(1, -1)
    lanes = width // 128

    (piece,) = call(pick_piece, "pick_piece", (idx, w_up, w_down), [shape_of(bf16, width // 4, ff)],
                    [pltpu.SemaphoreType.DMA((2,))], hbm=2, limit=2)
    depth = [swap(piece, "mp", j) for j in (1, 2, 3)]

    wide = shape_of(f32, length, units)
    square = shape_of(f32, length, width)
    square16 = shape_of(bf16, length, width)
    edge = shape_of(f32, chunks, units)
    decay, share, cand, du, dv, nmt, x, prods, ends, payload, mask = call(
        mixer_in, "mixer_in",
        (idx, resets, tok, row(gain_mix), row(bias_forget), row(bias_input), row(b_up), w3),
        [wide] * 5 + [shape_of(bf16, width, length), square, edge, edge, shape_of(f32, 4, units), shape_of(f32, length, 1)],
        [pltpu.SMEM(resets.shape, jnp.int32), pltpu.VMEM((lanes, length, 128), f32), pltpu.VMEM((length, width), bf16), pltpu.VMEM((1, width), f32)]
        + [pltpu.VMEM((1, units), f32)] * 2 + [pltpu.VMEM((1, ff), f32), pltpu.VMEM((3, width, units), bf16),
                                              pltpu.SemaphoreType.DMA((6 + units // 256,))],
        hbm=7, after=(piece,),
    )
    ahead = [swap(payload, "mp", j) for j in (1, 2, 3)]
    around = lambda v: [v] + [swap(v, "dp", 2 * k) for k in (1, 2, 3)]
    mine = gate(depth[0], payload)
    (two,) = call(join, "join_depth", depth[1:], [shape_of(bf16, width // 2, ff)], after=(payload,))
    (one_a,) = call(join, "join_one", (mine, across(mine, 0)), [shape_of(bf16, 2, width // 4, ff)], after=(two, *ahead))
    far_two = across(two, 0)
    quarter = width // 8
    st, stT, middle, nm2, nm2t, cotp = call(
        mid_in, "mid_in",
        (idx, payload, *ahead, prods, ends, decay, share, cand, x, cot, w_out, row(gain_mlp)),
        [shape_of(f32, length + chunks, units), shape_of(bf16, units, length), square, square16, shape_of(bf16, width, length), square16],
        [pltpu.VMEM((lanes, length, 128), f32), pltpu.VMEM((4, 4, units), f32), pltpu.VMEM((chunks, units), f32), pltpu.VMEM((length, width), f32)],
    )
    (two_a,) = call(join, "join_two", (two, far_two), [shape_of(bf16, 2, width // 2, ff)], after=(nm2,))
    two_b = across(two_a, 1)
    block = 2 * quarter
    pair = lambda dtype, rows: shape_of(dtype, 2, rows, width)
    weights = [pltpu.VMEM((ff, length), bf16), pltpu.VMEM((width, ff), bf16), pltpu.VMEM((ff, width), bf16)]
    grads = lambda rows: [square] * 2 + [shape_of(bf16, 4, rows, width)] * 2 + [shape_of(f32, 16, width)]
    one_b = gate(across(one_a, 1), nm2)
    mix, gn, keep0, send0, small_mlp = call(
        mlp_own, "mlp_own", (idx, w_up, w_down, row(b_up), middle, nm2, nm2t, cotp), grads(block), weights[:1], after=(two_a,),
    )
    mix, gn, keep_a, send_a, small_mlp = call(
        mlp_one, "mlp_one",
        (idx, one_a, one_b, swap(one_a, "dp", 1), swap(one_b, "dp", 1), ahead[0], mix, gn, small_mlp, nm2, nm2t, cotp), grads(block), weights,
    )
    (pair_a,) = call(add_pair, "add_pair", (keep_a, swap(send_a, "dp", 1)), [shape_of(bf16, 4, block, width)])
    more_a = swap(pair_a, "mp", 1)
    mix, gn, keep, send, small_mlp = call(
        mlp_two, "mlp_two",
        (idx, two_a, two_b, swap(two_a, "dp", 1), swap(two_b, "dp", 1), ahead[1], ahead[2], mix, gn, small_mlp, nm2, nm2t, cotp),
        grads(2 * block), weights, after=(pair_a,),
    )
    got, got0 = swap(send, "dp", 1), swap(send0, "dp", 1)
    out_rows = units // 8
    keep_out, send_out, grad_mid, grad_states, payload, prods, flows, gain_row = call(
        mid_back, "mid_back",
        (idx, gn, cotp, middle, row(gain_mlp), stT, w_out, decay),
        [shape_of(bf16, 4, out_rows, width)] * 2 + [square, wide, shape_of(f32, 2, units), edge, edge, shape_of(f32, 1, width)],
    )
    payload = gate(payload, got)
    behind = [swap(payload, "mp", j) for j in (1, 2, 3)]

    half = (3 * block + out_rows) // 2
    send_x, send_y, own_x, own_y = call(add_core, "add_core", (idx, keep0, got0, more_a, keep, got, keep_out, swap(send_out, "dp", 1)),
                                        [pair(bf16, half)] * 2 + [pair(f32, half)] * 2)
    got_x, got_y = swap(send_x, "dp", 2), swap(send_y, "dp", 4)

    rows_m = 3 * width // 16
    carried, send, lows, small = call(
        mixer_back, "mixer_back",
        (idx, payload, *behind, prods, flows, decay, share, cand, du, dv, st, grad_states, nmt, mask),
        [wide, shape_of(bf16, 4, 4, rows_m, units // 2), shape_of(bf16, 3, length, units // 2), shape_of(f32, 16, width)],
        [pltpu.VMEM((4, 2, units), f32), pltpu.VMEM((chunks, units), f32)], after=(own_x,),
    )
    flat = lambda v: v.reshape(4, -1, width)
    got = swap(send, "dp", 1)
    keep, gnm, small = call(
        mixer_out, "mixer_out",
        (idx, carried, share, cand, du, dv, st, nmt, w3, lows, small, small_mlp, gain_row, x, mask),
        [shape_of(bf16, 4, 4, rows_m, units // 2), square, shape_of(f32, 16, width)],
        [pltpu.VMEM((3, length, units // 2), bf16)],
    )
    one = lambda dtype, rows: shape_of(dtype, rows, width)
    send_m, own_m, tiny = call(
        add_core_small, "add_core_small", (idx, flat(keep), flat(got), small),
        [one(bf16, 8 * rows_m + 32), shape_of(f32, 4, 2 * rows_m, width), one(f32, 16)], [pltpu.VMEM((4, 8, width), f32)],
    )
    got_m = swap(send_m, "mp", 1)
    mark = shape_of(f32, 8, 128)
    grad_tok, done_tok = call(tokens_out, "tokens_out", (gnm, x, row(gain_mix), grad_mid), [square16, mark],
                       [pltpu.VMEM((length, width), f32), pltpu.VMEM((lanes, length, 128), f32)], after=(own_m,))
    mixed, done_mix = call(mixed_out, "mixed_out", (mix,), [square16, mark], [pltpu.VMEM((lanes, length, 128), f32)], after=(own_m,))

    send_y, send_x, own_x, own_y = call(add_cross, "add_cross", (idx, own_x, got_x, own_y, got_y),
                                        [one(bf16, half)] * 2 + [one(f32, half)] * 2, after=(own_m,))
    got_x, got_y = swap(send_y, "dp", 4), swap(send_x, "dp", 2)
    rows_f = block + units // 32
    send, own = call(add_depth, "add_depth", (own_x, got_x, own_y, got_y), [one(bf16, block + units // 16), one(f32, 2 * rows_f)],
                     [pltpu.VMEM((2 * half, width), f32)])
    got = swap(send, "mp", 1)
    send_mx, send_my, own_mx, own_my, tiny = call(
        add_near_small, "add_near_small", (idx, own_m, got_m, tiny),
        [one(bf16, 2 * rows_m + 32), one(bf16, 2 * rows_m), pair(f32, rows_m), pair(f32, rows_m), one(bf16, 32)],
        after=(own, done_mix, done_tok),
    )
    got_mx, got_my = swap(send_mx, "dp", 2), swap(send_my, "dp", 4)
    send, own = call(add_far, "add_far", (own, got), [one(bf16, rows_f), one(f32, rows_f)], after=(tiny,))
    got = swap(send, "mp", 2)
    send_my, send_mx, own_mx, own_my, tiny = call(
        add_cross_small, "add_cross_small", (idx, own_mx, got_mx, own_my, got_my, tiny),
        [one(bf16, rows_m + 32), one(bf16, rows_m), one(f32, rows_m), one(f32, rows_m), one(bf16, 32)], after=(own,),
    )
    got_mx, got_my = swap(send_my, "dp", 4), swap(send_mx, "dp", 2)
    send_m, own_m, tiny = call(
        add_far_small, "add_far_small", (own_mx, got_mx, own_my, got_my, tiny), [one(bf16, rows_m + 16), one(f32, rows_m), one(f32, 8)],
    )
    got_m = swap(send_m, "mp", 2)
    groups = [[g * 8 + i for g in range(dp // 8)] for i in range(8)]

    def last(fn, name, operands, outs, after):
        if dp == 8:
            return call(fn, name, operands, outs, after=after)
        done = call(fn, name, operands, [shape_of(f32, *o.shape) for o in outs], after=after)
        return [lax.psum(v, "dp", axis_index_groups=groups).astype(o.dtype) for v, o in zip(done, outs)]

    (part,) = last(add_last, "add_last", (own, got), [one(bf16, rows_f)], (tiny,))
    near_f = around(part)
    part, tiny = last(add_last_small, "add_last_small", (own_m, tiny, got_m), [one(bf16, rows_m), one(f32, 8)], (part,))
    near_m = around(part)
    (near,) = call(join, "join_mlp", near_f, [shape_of(bf16, 4, rows_f, width)], after=(part,))
    grad_up, grad_down, grad_out, done = call(
        spread_mlp, "spread_mlp", (idx, near, swap(near, "dp", 1)),
        [shape_of(f32, width, ff), shape_of(f32, ff, width), shape_of(f32, units // 4, width), mark],
    )
    (near,) = call(join, "join_mix", near_m, [shape_of(bf16, 4, rows_m, width)])
    grad_mix, g_bf, g_bi, g_gain_mix, g_gain_mlp, g_bu = call(
        spread_mix, "spread_mix", (idx, tiny, swap(tiny, "dp", 1), near, swap(near, "dp", 1)),
        [shape_of(f32, 3, width // 4, units), shape_of(f32, 1, units // 4), shape_of(f32, 1, units // 4),
         shape_of(f32, 1, width // 4), shape_of(f32, 1, width // 4), shape_of(f32, 1, ff)],
        after=(done,),
    )
    return (
        mixed[None], grad_tok[None], g_gain_mix[0], grad_mix.transpose(1, 0, 2), g_bf[0], g_bi[0],
        grad_out, g_gain_mlp[0], grad_up, g_bu[0], grad_down,
    )


def solution(mesh):
    return jax.shard_map(
        on_device,
        mesh=mesh,
        in_specs=(P("dp", "mp", None), P(), P(), P(), P(), P(), P(), P(None, "mp"), P("mp"), P("mp", None), P("dp", None), P("dp", "mp", None)),
        out_specs=(P("dp", "mp", None), P("dp", "mp", None), P("mp"), P("mp", None, None), P("mp"), P("mp"), P("mp", None), P("mp"), P(None, "mp"), P("mp"), P("mp", None)),
        check_vma=False,
    )
```

```python
from functools import partial

import jax
import jax.numpy as jnp
from jax import lax
from jax.experimental import pallas as pl
from jax.experimental.pallas import tpu as pltpu
from jax.sharding import PartitionSpec as P

norm_eps = 1e-06
gelu_k = 0.7978845608028654
gelu_c = 0.044715
chunks = 8
f32 = jnp.float32
bf16 = jnp.bfloat16
VMEM = pl.BlockSpec(memory_space=pltpu.VMEM)
HBM = pl.BlockSpec(memory_space=pltpu.HBM)


weight = {
    "pick_piece": 16, "mixer_in": 0, "join_depth": 0, "join_one": 4, "mlp_one": 4, "join_two": 2, "mlp_two": 8, "mid_back": 8,
    "add_core": 0, "mixer_back": 0, "mixer_out": 0, "add_core_small": 0, "add_cross": 4, "mixed_out": 0, "tokens_out": 8,
    "add_cross_small": 8, "add_depth": 0, "add_near_small": 32, "add_far": 16, "add_far_small": 0, "add_last": 4,
    "add_last_small": 4, "join_mlp": 32, "join_mix": 16, "spread_mlp": 8, "spread_mix": 32, "add_pair": 32, "mid_in": 8,
    "mlp_own": 4,
}


def dot(a, b):
    return jnp.dot(a, b, preferred_element_type=f32)


def dot_nt(a, b):
    return lax.dot_general(a, b, (((1,), (1,)), ((), ())), preferred_element_type=f32)


def shape_of(dtype, *shape):
    return jax.ShapeDtypeStruct(shape, dtype)


def place():
    row = lax.axis_index("dp")
    return row & 1, (row >> 1) & 3, lax.axis_index("mp")


def call(body, name, operands, outs, scratch=(), limit=16, after=(), hbm=0):
    placed = operands[0] is None
    operands = operands[placed:]
    n, extra, cost = len(operands), len(after), weight[name]
    operands = [pltpu.with_memory_space_constraint(v, pltpu.HBM) if i < hbm else v for i, v in enumerate(operands)]

    def run(*refs):
        body(*((place(),) if placed else ()), *refs[:n], *refs[n + extra :])

    return pl.pallas_call(
        run,
        out_shape=outs,
        in_specs=[HBM] * hbm + [VMEM] * (n - hbm) + [pl.BlockSpec(memory_space=pl.ANY)] * extra,
        out_specs=[VMEM] * len(outs),
        scratch_shapes=list(scratch),
        compiler_params=pltpu.CompilerParams(vmem_limit_bytes=limit << 20),
        cost_estimate=pl.CostEstimate(flops=cost << 30, bytes_accessed=cost << 22, transcendentals=0),
        name=name,
    )(*operands, *after)


def to_chunked(src, split, put):
    length, width = src.shape
    steps = length // chunks
    for g in range(width // 128):
        cols = slice(g * 128, (g + 1) * 128)
        split[g] = src[:, cols].astype(f32)
        for s in range(steps):
            put(pl.ds(s * chunks, chunks), cols, split[g, pl.ds(s, chunks, stride=steps), :])


def from_chunked(values, split, out):
    length, width = out.shape
    steps = length // chunks
    for g in range(width // 128):
        cols = slice(g * 128, (g + 1) * 128)
        for s in range(steps):
            split[g, pl.ds(s, chunks, stride=steps), :] = values[s * chunks : (s + 1) * chunks, cols]
        out[:, cols] = split[g].astype(bf16)


def keep_mask(idx, resets, length):
    row = lax.broadcasted_iota(jnp.int32, (length, 1), 0)
    pos = idx[2] * length + (row % chunks) * (length // chunks) + row // chunks
    keep = jnp.ones((length, 1), f32)
    for i in range(3):
        keep = jnp.where(pos == resets[0, i], 0.0, keep)
    return keep


def fetch(pairs, sems):
    copies = [pltpu.make_async_copy(src, dst, sems.at[i]) for i, (src, dst) in enumerate(pairs)]
    for copy in copies:
        copy.start()
    return copies


def mixer_in(idx, res_hbm, tok_hbm, gain_hbm, bias_f_hbm, bias_i_hbm, b_up_hbm, w_hbm, decay, share, cand, du, dv, nmt, x, prods, ends, payload, mask,
             resets, split, tok, gain, bias_f, bias_i, b_up, w, sems):
    length, width = tok.shape
    units = bias_f.shape[1]
    steps = length // chunks
    block = 256
    pairs = [(tok_hbm, tok), (gain_hbm, gain), (bias_f_hbm, bias_f), (bias_i_hbm, bias_i), (b_up_hbm, b_up), (res_hbm, resets)]
    for h in range(0, units, block):
        sl = pl.ds(h, block)
        pairs.append((w_hbm.at[:, :, sl], w.at[:, :, sl]))
    copies = fetch(pairs, sems)
    for copy in copies[:6]:
        copy.wait()

    def put(rows, cols, values):
        x[rows, cols] = values

    to_chunked(tok, split, put)
    v = x[...]
    r = lax.rsqrt(jnp.mean(v * v, axis=-1, keepdims=True) + norm_eps)
    nm = (v * r * gain[...]).astype(bf16)
    nmt[...] = nm.T
    keep = keep_mask(idx, resets, length)
    mask[...] = keep
    for i, h in enumerate(range(0, units, block)):
        sl = pl.ds(h, block)
        copies[6 + i].wait()
        a = jnp.exp(jnp.minimum(-(dot(nm, w[0, :, sl]) + bias_f[:, sl]), 88.0))
        b = jnp.exp(jnp.minimum(-(dot(nm, w[1, :, sl]) + bias_i[:, sl]), 88.0))
        t = 1.0 / (2.0 + a + b)
        p = (1.0 + b) * t
        q = (1.0 + a) * t
        decay[:, sl] = p * keep
        share[:, sl] = q
        cand[:, sl] = dot(nm, w[2, :, sl])
        du[:, sl] = p * (a * t)
        dv[:, sl] = q * (b * t)

    def step(s, carry):
        prod, end = carry
        rows = pl.ds(pl.multiple_of(s * chunks, chunks), chunks)
        d = decay[rows, :]
        return prod * d, end * d + share[rows, :] * cand[rows, :]

    prod, end = lax.fori_loop(
        0, steps, step, (jnp.ones((chunks, units), f32), jnp.zeros((chunks, units), f32)), unroll=8
    )
    prods[...] = prod
    ends[...] = end
    total, state = prod[0:1], end[0:1]
    for k in range(1, chunks):
        total = total * prod[k : k + 1]
        state = state * prod[k : k + 1] + end[k : k + 1]
    payload[...] = jnp.zeros_like(payload)
    payload[0:1, :] = total
    payload[1:2, :] = state
    payload[2:3, 0 : b_up.shape[1]] = b_up[...]


def store_pieces(ref, base, rows, values):
    for p in range(4):
        ref[p, base : base + rows, :] = values[p * rows : (p + 1) * rows].astype(bf16)


def send_first(ref, core, values):
    n = values.shape[0] // 2
    ref[pl.ds(pl.multiple_of((1 - core) * n, n), n), :] = values[0:n]
    ref[pl.ds(pl.multiple_of(core * n, n), n), :] = values[n:]


def ffn_block(slot, core, nm, nmt, cot, wu, wd, bu, mix, gn, keep, send, hT):
    pre = dot(nm, wu[...]) + bu
    grad_act = dot_nt(cot, wd[...])
    sq = pre * pre
    t = jnp.tanh(pre * (gelu_k + gelu_k * gelu_c * sq))
    half = 0.5 + 0.5 * t
    h = pre * half
    slope = half + h * (1.0 - t) * (gelu_k + 3.0 * gelu_k * gelu_c * sq)
    grad_pre = grad_act * slope
    total = jnp.sum(grad_pre, axis=0, keepdims=True)
    h, g = h.astype(bf16), grad_pre.astype(bf16)
    send_first(hT, core, h.T)
    mix[...] += dot(h, wd[...])
    gn[...] += dot_nt(g, wu[...])
    n = nm.shape[1] // 2
    for base, got in ((0, dot(nmt[...], g)), (n // 4, dot(hT[...], cot))):
        store_pieces(send, slot * (n // 2) + base, n // 4, got[0:n])
        store_pieces(keep, slot * (n // 2) + base, n // 4, got[n:])
    return total


def mid_in(idx, own, r1, r2, r3, prods, ends, decay, share, cand, x, cot, w_out, gain,
           st, stT, middle, nm2, nm2t, cotp, split, others, carry8, square):
    length = x.shape[0]
    steps = length // chunks
    units = decay.shape[1]
    z = idx[2]
    for j, ref in enumerate((own, r1, r2, r3)):
        others[j] = ref[...]
    state = jnp.zeros((1, units), f32)
    for k in range(4):
        part = others[k ^ z]
        state = jnp.where(k < z, state * part[0:1] + part[1:2], state)
    for k in range(chunks):
        carry8[k : k + 1, :] = state
        state = state * prods[k : k + 1, :] + ends[k : k + 1, :]
    st[0:chunks, :] = carry8[...]

    def step(s, state):
        rows = pl.ds(pl.multiple_of(s * chunks, chunks), chunks)
        state = state * decay[rows, :] + share[rows, :] * cand[rows, :]
        st[pl.ds(pl.multiple_of(s * chunks + chunks, chunks), chunks), :] = state
        return state

    lax.fori_loop(0, steps, step, carry8[...], unroll=8)
    low = st[chunks:, :].astype(bf16)
    stT[...] = low.T
    mid = x[...] + dot(low, w_out[...])
    middle[...] = mid
    r = lax.rsqrt(jnp.mean(mid * mid, axis=-1, keepdims=True) + norm_eps)
    nm = (mid * r * gain[...]).astype(bf16)
    nm2[...] = nm
    send_first(nm2t, idx[0], nm.T)

    def put(rows, cols, values):
        square[rows, cols] = values

    to_chunked(cot, split, put)
    cotp[...] = square[...].astype(bf16)


def pieces_of(idx, near, near_far, far, far_far):
    for which, arrays in ((idx[0], (near, near_far)), (1 - idx[0], (far, far_far))):
        for k in range(2):
            for i in range(2):
                yield which, idx[1] ^ (i * (1 + which) + k * (2 - which)), arrays[k].at[i]


def lay_out(idx, arrays, at, wu, wd):
    rows = wu.shape[0] // 8
    for which, place, piece in pieces_of(idx, *arrays):
        spot = pl.ds(pl.multiple_of((which * 4 + place) * rows, rows), rows)
        wu[spot, :] = piece[at : at + rows, :]
        wd[spot, :] = piece[at + rows : at + 2 * rows, :]


def mlp_own(idx, wu, wd, bu, middle, nm2, nm2t, cotp, mix, gn, keep, send, small, hT):
    mix[...] = middle[...]
    gn[...] = jnp.zeros_like(gn)
    small[...] = jnp.zeros_like(small)
    small[pl.ds(4 * idx[2] + 2, 1), :] = ffn_block(
        0, idx[0], nm2[...], nm2t, cotp[...], wu, wd, bu[...], mix, gn, keep, send, hT
    )


def mlp_one(idx, n1, n2, f1, f2, bias, mix0, gn0, small0, nm2, nm2t, cotp, mix, gn, keep, send, small, hT, wu, wd):
    mix[...] = mix0[...]
    gn[...] = gn0[...]
    small[...] = small0[...]
    lay_out(idx, (n1, n2, f1, f2), 0, wu, wd)
    small[pl.ds(4 * (idx[2] ^ 1) + 2, 1), :] = ffn_block(
        0, idx[0], nm2[...], nm2t, cotp[...], wu, wd, bias[2:3, 0 : wu.shape[1]], mix, gn, keep, send, hT
    )


def mlp_two(idx, n1, n2, f1, f2, bias2, bias3, mix0, gn0, small0, nm2, nm2t, cotp, mix, gn, keep, send, small, hT, wu, wd):
    mix[...] = mix0[...]
    gn[...] = gn0[...]
    small[...] = small0[...]
    for slot, bias in enumerate((bias2, bias3)):
        lay_out(idx, (n1, n2, f1, f2), slot * wu.shape[0] // 4, wu, wd)
        small[pl.ds(4 * (idx[2] ^ (2 + slot)) + 2, 1), :] = ffn_block(
            slot, idx[0], nm2[...], nm2t, cotp[...], wu, wd, bias[2:3, 0 : wu.shape[1]], mix, gn, keep, send, hT
        )


def mid_back(idx, gn, cotp, middle, gain, stT, w_out, decay,
             keep, send, grad_mid, grad_states, payload, prods, flows, gain_row):
    core, z = idx[0], idx[2]
    length, units = decay.shape
    steps = length // chunks
    mid = middle[...]
    r = lax.rsqrt(jnp.mean(mid * mid, axis=-1, keepdims=True) + norm_eps)
    scaled = mid * r
    g = gn[...]
    gain_row[...] = jnp.sum(g * scaled, axis=0, keepdims=True)
    gg = g * gain[...]
    gm = cotp[...].astype(f32) + r * (gg - scaled * jnp.mean(gg * scaled, axis=-1, keepdims=True))
    grad_mid[...] = gm
    low = gm.astype(bf16)
    grad_states[...] = dot_nt(low, w_out[...])
    part = units // 8
    for k in range(4):
        for ref, which in ((send, 1 - core), (keep, core)):
            got = dot(stT[pl.ds(pl.multiple_of((2 * k + which) * part, part), part), :], low)
            at = pl.ds(pl.multiple_of((k ^ z) * (part // 4), part // 4), part // 4)
            for p in range(4):
                ref[p, at, :] = got[p * (part // 4) : (p + 1) * (part // 4)].astype(bf16)

    def step(i, carry):
        prod, flow = carry
        rows = pl.ds(pl.multiple_of((steps - 1 - i) * chunks, chunks), chunks)
        d = decay[rows, :]
        return prod * d, (flow + grad_states[rows, :]) * d

    prod, flow = lax.fori_loop(
        0, steps, step, (jnp.ones((chunks, units), f32), jnp.zeros((chunks, units), f32)), unroll=8
    )
    total, out = prod[chunks - 1 :], flow[chunks - 1 :]
    for k in range(chunks - 2, -1, -1):
        total = total * prod[k : k + 1]
        out = out * prod[k : k + 1] + flow[k : k + 1]
    payload[0:1, :] = total
    payload[1:2, :] = out
    prods[...] = prod
    flows[...] = flow


def mixed_out(mix, mixed, done, split):
    from_chunked(mix, split, mixed)
    done[...] = jnp.zeros_like(done)


def gate_grads(which, keep, carried, st, share, cand, du, dv, nmt, z, out, lows, small):
    length, units = carried.shape
    half = units // 2
    cols = pl.ds(pl.multiple_of(which * half, half), half)
    cf = carried[:, cols]
    q = share[:, cols]
    s = cf * (st[0:length, cols] * keep - cand[:, cols])
    ga = s * du[:, cols]
    gb = -(s * dv[:, cols])
    quarter = half // 2
    sum_a, sum_b = jnp.sum(ga, axis=0, keepdims=True), jnp.sum(gb, axis=0, keepdims=True)
    for i in range(2):
        at = pl.ds(4 * (2 * which + i), 1)
        small[at, 0:quarter] = sum_a[:, i * quarter : (i + 1) * quarter]
        small[at, quarter:] = sum_b[:, i * quarter : (i + 1) * quarter]
    part = nmt.shape[0] // 4
    for k, g in enumerate((ga, gb, cf * q)):
        lows[k] = g.astype(bf16)
        got = dot(nmt[...], lows[k])
        for zz in range(4):
            for p in range(4):
                top = zz * part + p * (part // 4)
                out[p, zz ^ z, k * (part // 4) : (k + 1) * (part // 4), :] = got[top : top + part // 4].astype(bf16)


def mixer_back(idx, own, r1, r2, r3, prods, flows, decay, share, cand, du, dv, st, grad_states, nmt, mask,
               carried, send, lows, small, others, carry8):
    length, units = decay.shape
    steps = length // chunks
    core, z = idx[0], idx[2]
    for j, ref in enumerate((own, r1, r2, r3)):
        others[j] = ref[...]
    flow = jnp.zeros((1, units), f32)
    for k in range(3, -1, -1):
        part = others[k ^ z]
        flow = jnp.where(k > z, flow * part[0:1] + part[1:2], flow)
    for k in range(chunks - 1, -1, -1):
        carry8[k : k + 1, :] = flow
        flow = flow * prods[k : k + 1, :] + flows[k : k + 1, :]

    def step(i, flow):
        rows = pl.ds(pl.multiple_of((steps - 1 - i) * chunks, chunks), chunks)
        got = grad_states[rows, :] + flow
        carried[rows, :] = got
        return got * decay[rows, :]

    lax.fori_loop(0, steps, step, carry8[...], unroll=8)
    small[...] = jnp.zeros_like(small)
    gate_grads(1 - core, mask[...], carried, st, share, cand, du, dv, nmt, z, send, lows, small)


def mixer_out(idx, carried, share, cand, du, dv, st, nmt, w, lows0, small0, small1, gain_row, x, mask,
              keep, gnm, small, lows):
    length, units = carried.shape
    core, z = idx[0], idx[2]
    small[...] = small0[...] + small1[...]
    gate_grads(core, mask[...], carried, st, share, cand, du, dv, nmt, z, keep, lows, small)
    half = units // 2
    total = jnp.zeros(gnm.shape, f32)
    for part, which in ((lows0, 1 - core), (lows, core)):
        cols = pl.ds(pl.multiple_of(which * half, half), half)
        for k in range(3):
            total = total + dot_nt(part[k], w[k, :, cols])
    gnm[...] = total
    v = x[...]
    r = lax.rsqrt(jnp.mean(v * v, axis=-1, keepdims=True) + norm_eps)
    gains = jnp.sum(gnm[...] * (v * r), axis=0, keepdims=True)
    n = gains.shape[1] // 4
    for k in range(4):
        small[4 * k + 1 : 4 * k + 2, 0:n] = gains[:, k * n : (k + 1) * n]
        small[4 * k + 1 : 4 * k + 2, n : 2 * n] = gain_row[:, k * n : (k + 1) * n]


def tokens_out(gnm, x, gain, grad_mid, grad_tok, done, total, split):
    v = x[...]
    r = lax.rsqrt(jnp.mean(v * v, axis=-1, keepdims=True) + norm_eps)
    scaled = v * r
    gg = gnm[...] * gain[...]
    total[...] = grad_mid[...] + r * (gg - scaled * jnp.mean(gg * scaled, axis=-1, keepdims=True))
    from_chunked(total, split, grad_tok)
    done[...] = jnp.zeros_like(done)


def pick_piece(idx, wu, wd, out, sems):
    rows = wu.shape[0] // 8
    at = pl.ds(pl.multiple_of((idx[0] * 4 + idx[1]) * rows, rows), rows)
    for copy in fetch([(wu.at[at, :], out.at[pl.ds(0, rows), :]), (wd.at[at, :], out.at[pl.ds(rows, rows), :])], sems):
        copy.wait()


def gate(value, after):
    any_space = pl.BlockSpec(memory_space=pl.ANY)
    return pl.pallas_call(
        lambda *refs: None,
        out_shape=jax.ShapeDtypeStruct(value.shape, value.dtype),
        in_specs=[any_space, any_space],
        out_specs=any_space,
        input_output_aliases={0: 0},
        compiler_params=pltpu.CompilerParams(vmem_limit_bytes=1 << 20),
        name="gate",
    )(value, after)


def join(*refs):
    out, rows = refs[-1], refs[0].shape[0]
    for k, ref in enumerate(refs[:-1]):
        if len(out.shape) == 3:
            out[k] = ref[...]
        else:
            out[k * rows : (k + 1) * rows, :] = ref[...]


def stacked(*parts):
    return jnp.concatenate([v.astype(f32) for v in parts], axis=0).astype(bf16)


def two_terms(v):
    high = v.astype(bf16)
    return high, (v - high.astype(f32)).astype(bf16)


def add_pair(keep, got, out):
    out[...] = (keep[...].astype(f32) + got[...].astype(f32)).astype(bf16)


def add_core(idx, keep_a, got_a, more_a, keep_b, got_b, keep_c, got_c, send_x, send_y, own_x, own_y):
    x, y = idx[1] % 2, idx[1] // 2
    half = send_x.shape[1]

    def put(ref, k, p, first):
        top = 0
        for arrays in ((keep_a, got_a, more_a), (keep_b, got_b), (keep_c, got_c)):
            n = arrays[0].shape[1]
            low, high = max(first, top), min(first + half, top + n)
            if low < high:
                rows = slice(low - top, high - top)
                total = arrays[0][p, rows, :].astype(f32)
                for more in arrays[1:]:
                    total = total + more[p, rows, :].astype(f32)
                ref[k, low - first : high - first, :] = total.astype(ref.dtype)
            top += n

    for k in range(2):
        put(send_x, k, 2 * k + 1 - x, 0)
        put(own_x, k, 2 * k + x, 0)
        put(send_y, k, 2 * (1 - y) + k, half)
        put(own_y, k, 2 * y + k, half)


def add_cross(idx, own_x, got_x, own_y, got_y, send_y, send_x, out_x, out_y):
    x, y = idx[1] % 2, idx[1] // 2
    send_y[...] = (own_x[1 - y] + got_x[1 - y].astype(f32)).astype(bf16)
    out_x[...] = own_x[y] + got_x[y].astype(f32)
    send_x[...] = (own_y[1 - x] + got_y[1 - x].astype(f32)).astype(bf16)
    out_y[...] = own_y[x] + got_y[x].astype(f32)


def add_depth(own_x, got_x, own_y, got_y, send, own, total):
    half = own_x.shape[0]
    part = send.shape[0] // 6
    block = 4 * part
    total[0:half, :] = own_x[...] + got_x[...].astype(f32)
    total[half:, :] = own_y[...] + got_y[...].astype(f32)
    out = 3 * block
    for ref, to, at, n in ((send, 0, 2 * block, block), (send, block, out + part, part), (send, block + part, out + 3 * part, part),
                           (own, 0, 0, block), (own, block, out, part), (own, block + part, block, block), (own, 2 * block + part, out + 2 * part, part)):
        ref[to : to + n, :] = total[at : at + n, :].astype(ref.dtype)


def add_far(own, got, send, out):
    rows = out.shape[0]
    part = rows // 5
    block = 4 * part
    out[0:block, :] = own[0:block, :]
    out[block:, :] = own[block:rows, :] + got[block:rows, :].astype(f32)
    send[0:block, :] = (own[rows : rows + block, :] + got[0:block, :].astype(f32)).astype(bf16)
    send[block:, :] = (own[rows + block :, :] + got[rows:, :].astype(f32)).astype(bf16)


def add_last(own, got, out):
    out[...] = (own[...] + got[...].astype(f32)).astype(out.dtype)


def add_core_small(idx, keep, got, small, send, own, tiny, slots):
    z = idx[2]
    rows = keep.shape[1] // 4
    n = small.shape[0] // 4
    slots[...] = jnp.zeros_like(slots)
    for k in range(4):
        slots[k, 0:n, :] = small[k * n : (k + 1) * n, :]
    for p in range(4):
        for j in range(4):
            at = slice(j * rows, (j + 1) * rows)
            total = keep[p, at, :].astype(f32) + got[p, at, :].astype(f32)
            base = j // 2 * rows
            if j % 2:
                send[p * 2 * rows + base : p * 2 * rows + base + rows, :] = total.astype(bf16)
            else:
                own[p, base : base + rows, :] = total
    for k in range(2):
        base = 8 * rows + 16 * k
        high, low = two_terms(slots[z ^ (2 * k + 1)])
        send[base : base + 16, :] = stacked(high, low)
        tiny[8 * k : 8 * k + 8, :] = slots[z ^ (2 * k)]


def add_near_small(idx, own, got, tiny, send_x, send_y, own_x, own_y, tiny_out):
    x, y = idx[1] % 2, idx[1] // 2
    rows = own.shape[1] // 2
    terms = []
    for k in range(2):
        base = 8 * rows + 16 * k
        other = got[base : base + 16, :].astype(f32)
        terms.append(two_terms(tiny[8 * k : 8 * k + 8, :] + (other[0:8] + other[8:16])))
    for i in range(2):
        both = stacked(terms[0][i], terms[1][i])
        tiny_out[16 * i : 16 * i + 16, :] = both
        send_x[2 * rows + 16 * i : 2 * rows + 16 * i + 16, :] = both

    def total(p, slot):
        at = pl.ds(pl.multiple_of(p * 2 * rows + slot * rows, 16), rows)
        return own[p, slot * rows : (slot + 1) * rows, :] + got[at, :].astype(f32)

    for k in range(2):
        at = slice(k * rows, (k + 1) * rows)
        send_x[at, :] = total(2 * k + 1 - x, 0).astype(bf16)
        own_x[k] = total(2 * k + x, 0)
        send_y[at, :] = total(2 * (1 - y) + k, 1).astype(bf16)
        own_y[k] = total(2 * y + k, 1)


def add_tiny(tiny, got, at):
    n = tiny.shape[0] // 2
    return (tiny[0:n, :].astype(f32) + tiny[n:, :].astype(f32)) + (
        got[at : at + n, :].astype(f32) + got[at + n : at + 2 * n, :].astype(f32)
    )


def add_cross_small(idx, own_x, got_x, own_y, got_y, tiny, send_y, send_x, out_x, out_y, tiny_out):
    x, y = idx[1] % 2, idx[1] // 2
    half, n = out_x.shape[0], tiny.shape[0] // 2
    high, low = two_terms(add_tiny(tiny, got_x, 2 * half))
    tiny_out[0:n, :] = high
    tiny_out[n:, :] = low
    send_y[half : half + n, :] = high
    send_y[half + n :, :] = low
    side = pl.ds(pl.multiple_of((1 - y) * half, half), half)
    send_y[0:half, :] = (own_x[1 - y] + got_x[side, :].astype(f32)).astype(bf16)
    side = pl.ds(pl.multiple_of(y * half, half), half)
    out_x[...] = own_x[y] + got_x[side, :].astype(f32)
    side = pl.ds(pl.multiple_of((1 - x) * half, half), half)
    send_x[...] = (own_y[1 - x] + got_y[side, :].astype(f32)).astype(bf16)
    side = pl.ds(pl.multiple_of(x * half, half), half)
    out_y[...] = own_y[x] + got_y[side, :].astype(f32)


def add_far_small(own_x, got_x, own_y, got_y, tiny, send, out, tiny_out):
    rows = out.shape[0]
    total = add_tiny(tiny, got_x, rows)
    out[...] = own_x[...] + got_x[0:rows, :].astype(f32)
    tiny_out[...] = total[0:8]
    send[0:rows, :] = (own_y[...] + got_y[...].astype(f32)).astype(bf16)
    high, low = two_terms(total[8:16])
    send[rows:, :] = stacked(high, low)


def add_last_small(own, tiny, got, out, tiny_out):
    rows, n = own.shape[0], tiny.shape[0]
    out[...] = (own[...] + got[0:rows, :].astype(f32)).astype(out.dtype)
    other = got[rows:, :].astype(f32)
    tiny_out[...] = tiny[...] + (other[0:n] + other[n : 2 * n])


def spread_mlp(idx, near, far, up, down, w_out, done):
    rows = up.shape[0] // 8
    rows_out = w_out.shape[0] // 8
    for which, pieces in ((idx[0], near), (1 - idx[0], far)):
        for k in range(4):
            spot = which * 4 + (idx[1] ^ k)
            at = pl.ds(pl.multiple_of(spot * rows, rows), rows)
            up[at, :] = pieces[k, 0:rows, :].astype(f32)
            down[at, :] = pieces[k, rows : 2 * rows, :].astype(f32)
            w_out[pl.ds(pl.multiple_of(spot * rows_out, rows_out), rows_out), :] = pieces[k, 2 * rows :, :].astype(f32)
    done[...] = jnp.zeros_like(done)


def spread_mix(idx, tiny, tiny_far, near, far, out, bias_f, bias_i, gain_mix, gain_mlp, b_up):
    rows, half = out.shape[1] // 4, out.shape[2] // 2
    for which, pieces in ((idx[0], near), (1 - idx[0], far)):
        cols = pl.ds(pl.multiple_of(which * half, half), half)
        for k in range(4):
            at = pl.ds(pl.multiple_of((idx[1] ^ k) * rows, rows), rows)
            for i in range(3):
                out[i, at, cols] = pieces[k, i * rows : (i + 1) * rows, :].astype(f32)
    small = tiny[...] + tiny_far[...]
    n = bias_f.shape[1]
    bias_f[...] = small[0:1, 0:n]
    bias_i[...] = small[0:1, n:]
    n = gain_mix.shape[1]
    gain_mix[...] = small[1:2, 0:n]
    gain_mlp[...] = small[1:2, n : 2 * n]
    b_up[...] = small[2:3, :]


def swap(value, axis, bit):
    size = lax.axis_size(axis)
    return lax.ppermute(value, axis, [(i, i ^ bit) for i in range(size)])


def across(value, turn):
    size = lax.axis_size("dp")
    return lax.ppermute(value, "dp", [(i, i ^ (2 << ((i & 1) ^ turn))) for i in range(size)])


def on_device(tokens, gain_mix, w_mix, bias_forget, bias_input, w_out, gain_mlp, w_up, b_up, w_down, resets, cotangent):
    length, width = tokens.shape[1:]
    units = w_out.shape[0]
    ff = w_up.shape[1]
    dp, mp = lax.axis_size("dp"), lax.axis_size("mp")
    assert mp == 4 and dp % 8 == 0 and tokens.shape[0] == 1
    idx = None
    tok, cot = tokens[0], cotangent[0]
    w3 = w_mix.transpose(1, 0, 2)
    row = lambda v: v.reshape(1, -1)
    lanes = width // 128

    (piece,) = call(pick_piece, "pick_piece", (idx, w_up, w_down), [shape_of(bf16, width // 4, ff)],
                    [pltpu.SemaphoreType.DMA((2,))], hbm=2, limit=2)
    depth = [swap(piece, "mp", j) for j in (1, 2, 3)]

    wide = shape_of(f32, length, units)
    square = shape_of(f32, length, width)
    square16 = shape_of(bf16, length, width)
    edge = shape_of(f32, chunks, units)
    decay, share, cand, du, dv, nmt, x, prods, ends, payload, mask = call(
        mixer_in, "mixer_in",
        (idx, resets, tok, row(gain_mix), row(bias_forget), row(bias_input), row(b_up), w3),
        [wide] * 5 + [shape_of(bf16, width, length), square, edge, edge, shape_of(f32, 4, units), shape_of(f32, length, 1)],
        [pltpu.SMEM(resets.shape, jnp.int32), pltpu.VMEM((lanes, length, 128), f32), pltpu.VMEM((length, width), bf16), pltpu.VMEM((1, width), f32)]
        + [pltpu.VMEM((1, units), f32)] * 2 + [pltpu.VMEM((1, ff), f32), pltpu.VMEM((3, width, units), bf16),
                                              pltpu.SemaphoreType.DMA((6 + units // 256,))],
        hbm=7, after=(piece,),
    )
    ahead = [swap(payload, "mp", j) for j in (1, 2, 3)]
    around = lambda v: [v] + [swap(v, "dp", 2 * k) for k in (1, 2, 3)]
    mine = gate(depth[0], payload)
    (two,) = call(join, "join_depth", depth[1:], [shape_of(bf16, width // 2, ff)], after=(payload,))
    (one_a,) = call(join, "join_one", (mine, across(mine, 0)), [shape_of(bf16, 2, width // 4, ff)], after=(two, *ahead))
    far_two = across(two, 0)
    quarter = width // 8
    st, stT, middle, nm2, nm2t, cotp = call(
        mid_in, "mid_in",
        (idx, payload, *ahead, prods, ends, decay, share, cand, x, cot, w_out, row(gain_mlp)),
        [shape_of(f32, length + chunks, units), shape_of(bf16, units, length), square, square16, shape_of(bf16, width, length), square16],
        [pltpu.VMEM((lanes, length, 128), f32), pltpu.VMEM((4, 4, units), f32), pltpu.VMEM((chunks, units), f32), pltpu.VMEM((length, width), f32)],
    )
    (two_a,) = call(join, "join_two", (two, far_two), [shape_of(bf16, 2, width // 2, ff)], after=(nm2,))
    two_b = across(two_a, 1)
    block = 2 * quarter
    pair = lambda dtype, rows: shape_of(dtype, 2, rows, width)
    weights = [pltpu.VMEM((ff, length), bf16), pltpu.VMEM((width, ff), bf16), pltpu.VMEM((ff, width), bf16)]
    grads = lambda rows: [square] * 2 + [shape_of(bf16, 4, rows, width)] * 2 + [shape_of(f32, 16, width)]
    one_b = gate(across(one_a, 1), nm2)
    mix, gn, keep0, send0, small_mlp = call(
        mlp_own, "mlp_own", (idx, w_up, w_down, row(b_up), middle, nm2, nm2t, cotp), grads(block), weights[:1], after=(two_a,),
    )
    mix, gn, keep_a, send_a, small_mlp = call(
        mlp_one, "mlp_one",
        (idx, one_a, one_b, swap(one_a, "dp", 1), swap(one_b, "dp", 1), ahead[0], mix, gn, small_mlp, nm2, nm2t, cotp), grads(block), weights,
    )
    (pair_a,) = call(add_pair, "add_pair", (keep_a, swap(send_a, "dp", 1)), [shape_of(bf16, 4, block, width)])
    more_a = swap(pair_a, "mp", 1)
    mix, gn, keep, send, small_mlp = call(
        mlp_two, "mlp_two",
        (idx, two_a, two_b, swap(two_a, "dp", 1), swap(two_b, "dp", 1), ahead[1], ahead[2], mix, gn, small_mlp, nm2, nm2t, cotp),
        grads(2 * block), weights, after=(pair_a,),
    )
    got, got0 = swap(send, "dp", 1), swap(send0, "dp", 1)
    out_rows = units // 8
    keep_out, send_out, grad_mid, grad_states, payload, prods, flows, gain_row = call(
        mid_back, "mid_back",
        (idx, gn, cotp, middle, row(gain_mlp), stT, w_out, decay),
        [shape_of(bf16, 4, out_rows, width)] * 2 + [square, wide, shape_of(f32, 2, units), edge, edge, shape_of(f32, 1, width)],
    )
    behind = [swap(payload, "mp", j) for j in (1, 2, 3)]

    half = (3 * block + out_rows) // 2
    send_x, send_y, own_x, own_y = call(add_core, "add_core", (idx, keep0, got0, more_a, keep, got, keep_out, swap(send_out, "dp", 1)),
                                        [pair(bf16, half)] * 2 + [pair(f32, half)] * 2)
    got_x, got_y = swap(send_x, "dp", 2), swap(send_y, "dp", 4)

    rows_m = 3 * width // 16
    carried, send, lows, small = call(
        mixer_back, "mixer_back",
        (idx, payload, *behind, prods, flows, decay, share, cand, du, dv, st, grad_states, nmt, mask),
        [wide, shape_of(bf16, 4, 4, rows_m, units // 2), shape_of(bf16, 3, length, units // 2), shape_of(f32, 16, width)],
        [pltpu.VMEM((4, 2, units), f32), pltpu.VMEM((chunks, units), f32)], after=(own_x,),
    )
    flat = lambda v: v.reshape(4, -1, width)
    got = swap(send, "dp", 1)
    keep, gnm, small = call(
        mixer_out, "mixer_out",
        (idx, carried, share, cand, du, dv, st, nmt, w3, lows, small, small_mlp, gain_row, x, mask),
        [shape_of(bf16, 4, 4, rows_m, units // 2), square, shape_of(f32, 16, width)],
        [pltpu.VMEM((3, length, units // 2), bf16)],
    )
    one = lambda dtype, rows: shape_of(dtype, rows, width)
    send_m, own_m, tiny = call(
        add_core_small, "add_core_small", (idx, flat(keep), flat(got), small),
        [one(bf16, 8 * rows_m + 32), shape_of(f32, 4, 2 * rows_m, width), one(f32, 16)], [pltpu.VMEM((4, 8, width), f32)],
    )
    got_m = swap(send_m, "mp", 1)
    mark = shape_of(f32, 8, 128)
    grad_tok, done_tok = call(tokens_out, "tokens_out", (gnm, x, row(gain_mix), grad_mid), [square16, mark],
                       [pltpu.VMEM((length, width), f32), pltpu.VMEM((lanes, length, 128), f32)], after=(own_m,))
    mixed, done_mix = call(mixed_out, "mixed_out", (mix,), [square16, mark], [pltpu.VMEM((lanes, length, 128), f32)], after=(own_m,))

    send_y, send_x, own_x, own_y = call(add_cross, "add_cross", (idx, own_x, got_x, own_y, got_y),
                                        [one(bf16, half)] * 2 + [one(f32, half)] * 2, after=(own_m,))
    got_x, got_y = swap(send_y, "dp", 4), swap(send_x, "dp", 2)
    rows_f = block + units // 32
    send, own = call(add_depth, "add_depth", (own_x, got_x, own_y, got_y), [one(bf16, block + units // 16), one(f32, 2 * rows_f)],
                     [pltpu.VMEM((2 * half, width), f32)])
    got = swap(send, "mp", 1)
    send_mx, send_my, own_mx, own_my, tiny = call(
        add_near_small, "add_near_small", (idx, own_m, got_m, tiny),
        [one(bf16, 2 * rows_m + 32), one(bf16, 2 * rows_m), pair(f32, rows_m), pair(f32, rows_m), one(bf16, 32)],
        after=(own, done_mix, done_tok),
    )
    got_mx, got_my = swap(send_mx, "dp", 2), swap(send_my, "dp", 4)
    send, own = call(add_far, "add_far", (own, got), [one(bf16, rows_f), one(f32, rows_f)], after=(tiny,))
    got = swap(send, "mp", 2)
    send_my, send_mx, own_mx, own_my, tiny = call(
        add_cross_small, "add_cross_small", (idx, own_mx, got_mx, own_my, got_my, tiny),
        [one(bf16, rows_m + 32), one(bf16, rows_m), one(f32, rows_m), one(f32, rows_m), one(bf16, 32)], after=(own,),
    )
    got_mx, got_my = swap(send_my, "dp", 4), swap(send_mx, "dp", 2)
    send_m, own_m, tiny = call(
        add_far_small, "add_far_small", (own_mx, got_mx, own_my, got_my, tiny), [one(bf16, rows_m + 16), one(f32, rows_m), one(f32, 8)],
    )
    got_m = swap(send_m, "mp", 2)
    groups = [[g * 8 + i for g in range(dp // 8)] for i in range(8)]

    def last(fn, name, operands, outs, after):
        if dp == 8:
            return call(fn, name, operands, outs, after=after)
        done = call(fn, name, operands, [shape_of(f32, *o.shape) for o in outs], after=after)
        return [lax.psum(v, "dp", axis_index_groups=groups).astype(o.dtype) for v, o in zip(done, outs)]

    (part,) = last(add_last, "add_last", (own, got), [one(bf16, rows_f)], (tiny,))
    near_f = around(part)
    part, tiny = last(add_last_small, "add_last_small", (own_m, tiny, got_m), [one(bf16, rows_m), one(f32, 8)], (part,))
    near_m = around(part)
    (near,) = call(join, "join_mlp", near_f, [shape_of(bf16, 4, rows_f, width)], after=(part,))
    grad_up, grad_down, grad_out, done = call(
        spread_mlp, "spread_mlp", (idx, near, swap(near, "dp", 1)),
        [shape_of(f32, width, ff), shape_of(f32, ff, width), shape_of(f32, units // 4, width), mark],
    )
    (near,) = call(join, "join_mix", near_m, [shape_of(bf16, 4, rows_m, width)])
    grad_mix, g_bf, g_bi, g_gain_mix, g_gain_mlp, g_bu = call(
        spread_mix, "spread_mix", (idx, tiny, swap(tiny, "dp", 1), near, swap(near, "dp", 1)),
        [shape_of(f32, 3, width // 4, units), shape_of(f32, 1, units // 4), shape_of(f32, 1, units // 4),
         shape_of(f32, 1, width // 4), shape_of(f32, 1, width // 4), shape_of(f32, 1, ff)],
        after=(done,),
    )
    return (
        mixed[None], grad_tok[None], g_gain_mix[0], grad_mix.transpose(1, 0, 2), g_bf[0], g_bi[0],
        grad_out, g_gain_mlp[0], grad_up, g_bu[0], grad_down,
    )


def solution(mesh):
    return jax.shard_map(
        on_device,
        mesh=mesh,
        in_specs=(P("dp", "mp", None), P(), P(), P(), P(), P(), P(), P(None, "mp"), P("mp"), P("mp", None), P("dp", None), P("dp", "mp", None)),
        out_specs=(P("dp", "mp", None), P("dp", "mp", None), P("mp"), P("mp", None, None), P("mp"), P("mp"), P("mp", None), P("mp"), P(None, "mp"), P("mp"), P("mp", None)),
        check_vma=False,
    )
```
